32 devices in a mesh: proj: 2 (over x), space: 16 (over z, y, core).
Axes of the slice: x: 2, y: 2, z: 4, core: 2. Of those that a mesh axis runs over, the one named last changes fastest.
Arguments:
- design: float32 [32, 64, 256], P('space', None, 'proj'), may hold values from 0.02 to 0.98
- solid_mask: int32 [32, 64, 256], P('space', None, 'proj'), may hold values 0 or 1
- void_mask: int32 [32, 64, 256], P('space', None, 'proj'), may hold values 0 or 1
- load_mask: int32 [32, 64, 256], P('space'), may hold values 0 or 1
- support_mask: int32 [32, 64, 256], P('space'), may hold values 0 or 1
- thresholds: int32 [2], P('proj'), may hold values from 300 to 700
- group_weight: float32 [2], P('proj'), may hold values from 0.5 to 2
Outputs:
- sensitivity: float32 [32, 64, 256], P('space', None, 'proj')
The draws below stay inside these ranges and needn't reach their ends.
All inputs are finite; a program needn't handle non-finite values. No bound on the sum of `solid_mask` or of `void_mask` or of `load_mask` or of `support_mask` on one device may be relied on, other than what follows from the above.
Results may differ from the reference program's by a relative error of at most 0.0001.
Values sent between devices are 32-bit elements; how exact they have to be, the bound alone decides.
No kernel may reach another device: no remote copies, remote signals or barrier semaphores. Data moves between devices by JAX's collectives and lax.ppermute only.
A program may use at most 64 MiB of HBM per device.

```python
import math
import jax
import jax.numpy as jnp

NY = 64
NPROJ = 2
NX = 32
NZ = 256


def place_ends(values, rng, least, top_value):
    dims = values.shape
    index_at = [jax.random.randint(jax.random.fold_in(rng, axis), (), 0, dims[axis]) for axis in range(len(dims))]
    values = values.at[tuple(index_at)].set(least)
    longest = dims.index(max(dims))
    index_at[longest] = (index_at[longest] + 1) % dims[longest]
    return values.at[tuple(index_at)].set(top_value)


def shard_levels(own_key, shape, cuts, low, high):
    loudness = 1.0
    for dim, shards_of in cuts:
        heights = jax.random.uniform(jax.random.fold_in(jax.random.fold_in(own_key, 6), dim), (shards_of,), jnp.float32, low / len(cuts), high / len(cuts))
        loudness = loudness * jnp.repeat(jnp.exp(heights), shape[dim] // shards_of).reshape((-1,) + (1,) * (len(shape) - 1 - dim))
    return loudness


def setup_inputs(seed: int = 0) -> dict:
    seeds = jax.random.split(jax.random.key(seed), 8)
    design = jnp.clip(0.02 + 0.96000002 * jax.random.uniform(seeds[0], (NX, NY, NZ), jnp.float32) ** shard_levels(seeds[0], (NX, NY, NZ), ((0, 16), (2, 2)), -0.2, 0.2), 0.02, 0.98)
    solid_mask = place_ends((jax.random.randint(seeds[1], (NX, NY, NZ), 0, 16) < 1).astype(jnp.int32), jax.random.fold_in(seeds[1], 1), 0, 1)
    void_mask = place_ends((jax.random.randint(seeds[2], (NX, NY, NZ), 0, 16) < 1).astype(jnp.int32), jax.random.fold_in(seeds[2], 1), 0, 1)
    load_mask = place_ends((jax.random.randint(seeds[3], (NX, NY, NZ), 0, 8) < 1).astype(jnp.int32), jax.random.fold_in(seeds[3], 1), 0, 1)
    support_mask = place_ends((jax.random.randint(seeds[4], (NX, NY, NZ), 0, 16) < 1).astype(jnp.int32), jax.random.fold_in(seeds[4], 1), 0, 1)
    thresholds = jax.random.randint(seeds[5], (NPROJ,), 300, 701).astype(jnp.int32)
    group_weight = jnp.clip(jnp.exp(math.log(2.0) - 1.3862944 * jax.random.uniform(seeds[6], (NPROJ,), jnp.float32) ** shard_levels(seeds[6], (NPROJ,), ((0, 2),), -0.2, 0.2)), 0.5, 2.0)
    return {"design": design, "solid_mask": solid_mask, "void_mask": void_mask, "load_mask": load_mask, "support_mask": support_mask, "thresholds": thresholds, "group_weight": group_weight}


RMIN = 2.0
BETA = 8.0
EMIN = 0.05
PENALTY = 4.0

def conic(padded):
    rows_x, rows_y, rows_z = padded.shape
    total = jnp.zeros((rows_x - 2, rows_y - 2, rows_z - 2), padded.dtype)
    for step_x in range(3):
        for step_y in range(3):
            for step_z in range(3):
                spread = (step_x - 1) * (step_x - 1) + (step_y - 1) * (step_y - 1) + (step_z - 1) * (step_z - 1)
                weight = RMIN - math.sqrt(spread)
                total = total + weight * padded[step_x:step_x + rows_x - 2, step_y:step_y + rows_y - 2, step_z:step_z + rows_z - 2]
    return total

def project(filtered, eta):
    bottom = jnp.tanh(BETA * eta) + jnp.tanh(BETA * (1.0 - eta))
    inner = jnp.tanh(BETA * (filtered - eta))
    return ((jnp.tanh(BETA * eta) + inner) / bottom, BETA * (1.0 - inner * inner) / bottom)

def neighbours(field_x):
    centre = field_x[1:-1]
    padded = jnp.pad(centre, ((0, 0), (1, 1), (1, 1)))
    others = [field_x[2:], field_x[:-2], padded[:, 2:, 1:-1], padded[:, :-2, 1:-1], padded[:, 1:-1, 2:], padded[:, 1:-1, :-2]]
    return (centre, others)

def conductance(stiff_x):
    centre, others = neighbours(stiff_x)
    return [0.5 * (centre + other) for other in others]

def operate(links, field_x):
    centre, others = neighbours(field_x)
    total = jnp.zeros_like(centre)
    for link, other in zip(links, others):
        total = total + link * (centre - other)
    return total

def energy(field_x):
    centre, others = neighbours(field_x)
    total = jnp.zeros_like(centre)
    for other in others:
        total = total + (centre - other) * (centre - other)
    return -0.5 * total

def extend(field):
    return jnp.pad(field, ((1, 1), (0, 0), (0, 0)))

def reference(design, solid_mask, void_mask, load_mask, support_mask, thresholds, group_weight):
    fixed = jnp.where(solid_mask == 1, jnp.ones_like(design), jnp.where(void_mask == 1, jnp.zeros_like(design), design))
    filtered = conic(jnp.pad(fixed, 1)) / conic(jnp.pad(jnp.ones_like(design), 1))
    load = load_mask.astype(design.dtype)
    support = support_mask.astype(design.dtype)
    sensitivity = jnp.zeros_like(design)
    for group in range(NPROJ):
        eta = thresholds[group].astype(design.dtype) / 1000.0
        value, slope = project(filtered, eta)
        stiff = EMIN + (1.0 - EMIN) * value * value * value
        links = conductance(extend(stiff))
        diag = sum(links) + PENALTY * support
        resid = load
        precond = resid / diag
        rz_now = jnp.sum(resid * precond)
        first = extend(precond)
        image = operate(links, first)
        step_one = rz_now / jnp.sum(precond * image)
        solution = step_one * first
        resid = resid - step_one * image
        precond = resid / diag
        rz_next = jnp.sum(resid * precond)
        second = extend(precond) + rz_next / rz_now * first
        image = operate(links, second)
        step_two = rz_next / jnp.sum(second[1:-1] * image)
        solution = solution + step_two * second
        sensitivity = sensitivity + group_weight[group] * energy(solution) * (3.0 * (1.0 - EMIN)) * value * value * slope
    return sensitivity
```

```python
import functools
import math

import jax
import jax.numpy as jnp
from jax import lax
from jax.experimental import pallas as pl
from jax.experimental.pallas import tpu as pltpu
from jax.sharding import PartitionSpec as P

RMIN = 2.0
BETA = 8.0
EMIN = 0.05
PENALTY = 4.0

PLACES = 10
GROUP = 8
HALF = GROUP // 2


def pair_swap(size):
    return [(i, i ^ 1) for i in range(size)]


def near_swap(size):
    ups = [(i, i + 1) for i in range(1, size - 1, 2)]
    return ups + [(j, i) for i, j in ups]


def both_axes(pairs, size, groups, step):
    return [
        (g * size + i, (g + step) % groups * size + j)
        for g in range(groups)
        for i, j in pairs
        if 0 <= g + step < groups or groups == 2
    ]


def lanes_of(shape):
    return lax.broadcasted_iota(jnp.int32, shape, len(shape) - 1)


def turn(array, shift, axis):
    return pltpu.roll(array, shift % array.shape[axis], axis)


def prepare(groups, design, solid, void, load, support, fixed_out, mask_out):
    core = lax.rem(lax.axis_index("space"), 2)
    layer = lax.axis_index("proj")
    depth, width, thick = design.shape
    lane = lanes_of((width, thick))
    lower = lax.rem(lane, GROUP) < HALF
    has_left = layer > 0
    has_right = layer < groups - 1
    centre = pl.ds(pl.multiple_of(layer * thick, thick), thick)
    left = pl.ds(pl.multiple_of(jnp.maximum(layer - 1, 0) * thick, thick), thick)
    right = pl.ds(pl.multiple_of(jnp.minimum(layer + 1, groups - 1) * thick, thick), thick)
    strips = jnp.zeros((width, thick), jnp.float32)
    for place in range(depth):
        plane = lax.rem(place + core, 2)
        fixed_out[place] = jnp.where(
            solid[plane] == 1, 1.0, jnp.where(void[plane] == 1, 0.0, design[plane])
        )
        for which, mask in enumerate((load, support)):
            mask_out[which * depth + place] = mask[plane, :, centre].astype(jnp.float32)
            before = jnp.where(has_left, mask[plane, :, left].astype(jnp.float32), 0.0)
            after = jnp.where(has_right, mask[plane, :, right].astype(jnp.float32), 0.0)
            start = (4 + place + 8 * which) * GROUP
            outside = jnp.where(lower, turn(before, start + HALF, 1), turn(after, start + HALF, 1))
            strips = jnp.where(lane // GROUP == 4 + place + 8 * which, outside, strips)
    mask_out[2 * depth] = strips


def pack(own, partner, thresholds, weights, out):
    width, thick = own.shape[1:]
    where = lanes_of((width, thick)) // GROUP
    packed = jnp.zeros((width, thick), jnp.float32)
    for place, plane in ((4, own[0]), (5, own[1]), (6, partner[1]), (7, partner[0])):
        for target in (place, 7 - place):
            packed = jnp.where(where == target, turn(plane, target * GROUP + HALF, 1), packed)
    out[0:width] = packed
    eta = thresholds[0].astype(jnp.float32) / 1000.0
    row = lax.broadcasted_iota(jnp.int32, (8, thick), 0)
    out[width : width + 8] = jnp.where(row == 0, eta, jnp.where(row == 1, weights[0], 0.0))


def around_y(plane, first, last):
    return jnp.where(first, 0.0, turn(plane, 1, 0)) + jnp.where(last, 0.0, turn(plane, -1, 0))


def joined(left, right, lower):
    return jnp.where(lower, turn(right, -1, 1), turn(left, 1, 1))


def edge_of(joint, place):
    return turn(joint, -(place * GROUP + HALF), 1)


def main_kernel(groups, size, *refs):
    n_side = 1 if groups == 2 else 2
    own, partner, near, far, inner, masks, partner_masks, near_masks = refs[:8]
    beside = refs[8 : 8 + n_side]
    beyond = refs[8 + n_side : 8 + 2 * n_side]
    inner_beyond = refs[8 + 2 * n_side : 8 + 3 * n_side]
    scalars = refs[8 + 3 * n_side]
    tails = refs[9 + 3 * n_side : len(refs) - 5]
    table, z_out, w_out, edge_out, factor_out = refs[len(refs) - 5 :]

    spot = lax.axis_index("space")
    layer = lax.axis_index("proj")
    core = lax.rem(spot, 2)
    width, thick = own.shape[1:]
    shape = (width, thick)
    lane = lanes_of(shape)
    row = lax.broadcasted_iota(jnp.int32, shape, 0)
    first, last = row == 0, row == width - 1
    at_left, at_right = lane == 0, lane == thick - 1
    where = lane // GROUP
    slot = lax.rem(lane, GROUP)
    lower = slot < HALF
    near_real = jnp.where(jnp.where(core == 0, spot > 0, spot < size - 1), 1.0, 0.0)
    inner_real = jnp.where(jnp.where(core == 0, spot < size - 2, spot > 1), 1.0, 0.0)
    real = [near_real] * 4 + [1.0] * 4 + [inner_real] * 2
    has_left = jnp.where(layer > 0, 1.0, 0.0)
    has_right = jnp.where(layer < groups - 1, 1.0, 0.0)

    def real_at(places):
        return jnp.where(places < 4, near_real, jnp.where(places < 8, 1.0, inner_real))

    planes = [far[0], far[1], near[1], near[0], own[0], own[1], partner[1], partner[0], inner[0], inner[1]]

    def outside(k):
        strip = jnp.where(where < 4, beyond[k][0:width], beside[k][0:width])
        back = inner_beyond[k][0:width]
        strip = jnp.where(where == 8, turn(back, 5 * GROUP, 1), strip)
        strip = jnp.where(where == 9, turn(back, 7 * GROUP, 1), strip)
        return jnp.where(where < PLACES, strip, 0.0)

    inside = jnp.zeros(shape, jnp.float32)
    for place in range(PLACES):
        inside = jnp.where(where == place, turn(planes[place], place * GROUP + HALF, 1), inside)
    before = outside(0) * has_left
    after = outside(n_side - 1) * has_right
    fixed_left = jnp.where(lower, before, inside)
    fixed_right = jnp.where(lower, inside, after)

    two, three = RMIN - math.sqrt(2.0), RMIN - math.sqrt(3.0)
    heads, sides = [], []
    rows_left, rows_right = (around_y(v, first, last) for v in (fixed_left, fixed_right))
    joint = joined(fixed_left, fixed_right, lower)
    joint_rows = joined(rows_left, rows_right, lower)

    def around_z(plane, edge):
        return jnp.where(at_left, edge, turn(plane, 1, 1)) + jnp.where(at_right, edge, turn(plane, -1, 1))

    for place in range(PLACES):
        plane = planes[place]
        by_y = around_y(plane, first, last)
        by_z = around_z(plane, edge_of(joint, place))
        by_yz = around_z(by_y, edge_of(joint_rows, place))
        heads.append(2.0 * plane + (by_y + by_z) + two * by_yz)
        sides.append(plane + two * (by_y + by_z) + three * by_yz)

    def strip_z(v):
        return turn(v, 1, 1) + turn(v, -1, 1)

    def strip_x(v):
        return turn(v, GROUP, 1) + turn(v, -GROUP, 1)

    def strip_sum(v):
        return strip_x(v) + strip_z(v) + around_y(v, first, last)

    span_z = thick * groups
    count_y = jnp.where(first, 0.0, 1.0) + jnp.where(last, 0.0, 1.0)

    def counts(places_z):
        count_z = jnp.where(places_z >= 1, 1.0, 0.0) + jnp.where(places_z < span_z - 1, 1.0, 0.0)
        head = 2.0 + (count_y + count_z) + two * (count_y * count_z)
        side = 1.0 + two * (count_y + count_z) + three * (count_y * count_z)
        return head, side

    head, side = counts(layer * thick + lane)
    over_two, over_one = 1.0 / (head + 2.0 * side), 1.0 / (head + side)
    filtered = {}
    for place in range(1, PLACES - 1):
        total = heads[place] + sides[place - 1] + sides[place + 1]
        count_x = real[place - 1] + real[place + 1]
        filtered[place] = total * jnp.where(count_x > 1.5, over_two, over_one)

    def filter_strip(fixed, rows, places_z):
        by_z = strip_z(fixed)
        by_yz = strip_z(rows)
        total = 2.0 * fixed + (rows + by_z) + two * by_yz
        total = total + strip_x(fixed + two * (rows + by_z) + three * by_yz)
        head, side = counts(places_z)
        count_x = real_at(where - 1) + real_at(where + 1)
        return total / (head + count_x * side)

    filtered_left = filter_strip(fixed_left, rows_left, layer * thick - HALF + slot)
    filtered_right = filter_strip(fixed_right, rows_right, layer * thick + thick - HALF + slot)
    real_strip = jnp.where(where < PLACES, real_at(where), 0.0)
    real_left = jnp.where(lower, has_left, 1.0) * real_strip
    real_right = jnp.where(lower, 1.0, has_right) * real_strip

    def mask_planes(which):
        base = 2 * which
        return {
            2: near_masks[base + 1], 3: near_masks[base], 4: masks[base], 5: masks[base + 1],
            6: partner_masks[base + 1], 7: partner_masks[base],
        }

    def mask_strips(which, planes_of):
        back = 8 * GROUP * which
        mine, theirs, nears = masks[4], partner_masks[4], near_masks[4]
        out = jnp.zeros(shape, jnp.float32)
        ins = jnp.zeros(shape, jnp.float32)
        for place, source, held in ((2, nears, 5), (3, nears, 4), (4, mine, 4), (5, mine, 5), (6, theirs, 5), (7, theirs, 4)):
            shift = (place - held) * GROUP - back
            out = jnp.where(where == place, turn(source, shift, 1) if shift else source, out)
            ins = jnp.where(where == place, turn(planes_of[place], place * GROUP + HALF, 1), ins)
        return jnp.where(lower, out, ins), jnp.where(lower, ins, out)

    load, support = mask_planes(0), mask_planes(1)
    load_left, load_right = mask_strips(0, load)
    support_left, support_right = mask_strips(1, support)

    tables = []
    for g in range(groups):
        eta, weight = scalars[width : width + 1], scalars[width + 1 : width + 2]
        for k, tail in enumerate(tails):
            mine = lax.rem(layer + k + 1, groups) == g
            eta = jnp.where(mine, tail[width : width + 1], eta)
            weight = jnp.where(mine, tail[width + 1 : width + 2], weight)
        if groups == 2:
            mine = layer != g
            eta = jnp.where(mine, beside[0][width : width + 1], eta)
            weight = jnp.where(mine, beside[0][width + 1 : width + 2], weight)
        low = jnp.tanh(BETA * eta)
        over_bottom = 1.0 / (low + jnp.tanh(BETA * (1.0 - eta)))

        def stiffness(density, present):
            inner_part = jnp.tanh(BETA * (density - eta))
            value = (low + inner_part) * over_bottom
            return inner_part, value, (EMIN + (1.0 - EMIN) * (value * value * value)) * present

        stiff = {}
        for place in range(1, PLACES - 1):
            inner_part, value, stiff[place] = stiffness(filtered[place], real[place])
            if place in (4, 5):
                slope = (BETA * over_bottom) * (1.0 - inner_part * inner_part)
                scale = -0.5 * 3.0 * (1.0 - EMIN) * weight
                factor_out[g, place - 4] = scale * (value * value) * slope
        stiff_left = stiffness(filtered_left, real_left)[2]
        stiff_right = stiffness(filtered_right, real_right)[2]

        def sum_of(field, joint, place):
            plane = field[place]
            return (
                (field[place - 1] + field[place + 1])
                + around_y(plane, first, last)
                + around_z(plane, edge_of(joint, place))
            )

        joint = joined(stiff_left, stiff_right, lower)
        links, over, z, sz = {}, {}, {}, {}
        for place in range(2, 8):
            links[place] = 3.0 * stiff[place] + 0.5 * sum_of(stiff, joint, place)
            over[place] = real[place] / jnp.maximum(links[place] + PENALTY * support[place], 0.1)
            z[place] = load[place] * over[place]
            sz[place] = stiff[place] * z[place]

        def strip_start(stiff_of, load_of, support_of, present):
            link = 3.0 * stiff_of + 0.5 * strip_sum(stiff_of)
            inverse = present / jnp.maximum(link + PENALTY * support_of, 0.1)
            z_of = load_of * inverse
            q_of = link * z_of - 0.5 * (stiff_of * strip_sum(z_of) + strip_sum(stiff_of * z_of))
            return z_of, q_of * inverse

        z_left, w_left = strip_start(stiff_left, load_left, support_left, real_left)
        z_right, w_right = strip_start(stiff_right, load_right, support_right, real_right)
        joint_z = joined(z_left, z_right, lower)
        joint_sz = joined(stiff_left * z_left, stiff_right * z_right, lower)
        joint_w = joined(w_left, w_right, lower)
        joint_sw = joined(stiff_left * w_left, stiff_right * w_right, lower)

        q, w, sw = {}, {}, {}
        for place in range(3, 7):
            q[place] = links[place] * z[place] - 0.5 * (
                stiff[place] * sum_of(z, joint_z, place) + sum_of(sz, joint_sz, place)
            )
            w[place] = q[place] * over[place]
            sw[place] = stiff[place] * w[place]
            z_out[g, place - 3] = z[place]
            w_out[g, place - 3] = w[place]
        edge_out[g, 0] = joint_z
        edge_out[g, 1] = joint_w
        sums = [0.0, 0.0, 0.0, 0.0]
        for place in (4, 5):
            aw = links[place] * w[place] - 0.5 * (
                stiff[place] * sum_of(w, joint_w, place) + sum_of(sw, joint_sw, place)
            )
            terms = (z[place], z[place] * q[place], q[place] * w[place], w[place] * aw)
            sums = [a + b for a, b in zip(sums, terms)]
        tables += [jnp.sum(s, axis=0, keepdims=True) for s in sums]

    lane_row = lanes_of((1, thick))
    line = jnp.zeros((1, thick), jnp.float32)
    for k, part in enumerate(tables):
        line = jnp.where(lane_row == k, jnp.sum(part, axis=1, keepdims=True), line)
    table[...] = jnp.broadcast_to(line, table.shape)


def finish(groups, table, z_in, w_in, edges, factors, out):
    core = lax.rem(lax.axis_index("space"), 2)
    width, thick = out.shape[1:]
    shape = (width, thick)
    lane = lanes_of(shape)
    row = lax.broadcasted_iota(jnp.int32, shape, 0)
    first, last = row == 0, row == width - 1
    at_left, at_right = lane == 0, lane == thick - 1
    line = jnp.sum(table[...], axis=0, keepdims=True)
    lane_row = lanes_of((1, thick))
    total = [jnp.zeros(shape, jnp.float32), jnp.zeros(shape, jnp.float32)]
    for g in range(groups):
        m0, m1, m2, m3 = (
            jnp.sum(jnp.where(lane_row == 4 * g + k, line, 0.0), axis=1, keepdims=True) for k in range(4)
        )
        step_one = m0 / m1
        rz_next = step_one * step_one * m2 - m0
        factor = rz_next / m0
        curve = (m1 - 2.0 * step_one * m2 + step_one * step_one * m3) - factor * factor * m1
        step_two = rz_next / curve
        of_z = step_one + step_two * (1.0 + factor)
        of_w = -step_one * step_two
        u = [of_z * z_in[g, k] + of_w * w_in[g, k] for k in range(4)]
        joint = of_z * edges[g, 0] + of_w * edges[g, 1]
        for k in (1, 2):
            edge = edge_of(joint, k + 3)
            plane = u[k]
            others = (
                u[k - 1],
                u[k + 1],
                jnp.where(first, 0.0, turn(plane, 1, 0)),
                jnp.where(last, 0.0, turn(plane, -1, 0)),
                jnp.where(at_left, edge, turn(plane, 1, 1)),
                jnp.where(at_right, edge, turn(plane, -1, 1)),
            )
            squares = [(plane - other) * (plane - other) for other in others]
            total[k - 1] = total[k - 1] + factors[g, k - 1] * sum(squares[1:], squares[0])
    for k in range(2):
        out[lax.rem(k + core, 2)] = total[k]


def call(body, outs, *args, scalars=()):
    smem = pl.BlockSpec(memory_space=pltpu.SMEM)
    vmem = pl.BlockSpec(memory_space=pltpu.VMEM)
    return pl.pallas_call(
        body,
        out_shape=[jax.ShapeDtypeStruct(shape, jnp.float32) for shape in outs],
        in_specs=[vmem] * len(args) + [smem] * len(scalars),
        out_specs=[vmem] * len(outs),
        compiler_params=pltpu.CompilerParams(vmem_limit_bytes=32 * 1024 * 1024),
    )(*args, *scalars)


def local(design, solid_mask, void_mask, load_mask, support_mask, thresholds, group_weight):
    depth, width, thick = design.shape
    size, groups = lax.axis_size("space"), lax.axis_size("proj")
    pair, near_pairs = pair_swap(size), near_swap(size)
    fixed, masks = call(
        functools.partial(prepare, groups),
        [(depth, width, thick), (2 * depth + 1, width, thick)],
        design, solid_mask, void_mask, load_mask, support_mask,
    )
    partner = lax.ppermute(fixed, "space", pair)
    near = lax.ppermute(fixed, "space", near_pairs)
    partner_masks = lax.ppermute(masks, "space", pair)
    near_masks = lax.ppermute(masks, "space", near_pairs)
    (packed,) = call(pack, [(width + 8, thick)], fixed, partner, scalars=(thresholds, group_weight))
    far = lax.ppermute(partner, "space", near_pairs)
    inner = lax.ppermute(near, "space", pair)
    steps = (1,) if groups == 2 else (1, -1)
    straight = [(i, i) for i in range(size)]
    both = ("proj", "space")
    beside = [lax.ppermute(packed, both, both_axes(straight, size, groups, s)) for s in steps]
    beyond = [lax.ppermute(packed, both, both_axes(near_pairs, size, groups, s)) for s in steps]
    inner_beyond = [lax.ppermute(b, "space", pair) for b in beyond]
    tails = []
    if groups > 2:
        for k in range(1, groups):
            tails.append(lax.ppermute(packed, "proj", [((g + k) % groups, g) for g in range(groups)]))
    rows = size * groups
    table, z, w, edges, factors = call(
        functools.partial(main_kernel, groups, size),
        [(rows, thick), (groups, 4, width, thick), (groups, 4, width, thick), (groups, 2, width, thick), (groups, depth, width, thick)],
        fixed, partner, near, far, inner, masks, partner_masks, near_masks, *beside, *beyond, *inner_beyond, packed, *tails,
    )
    table = lax.all_to_all(table, both, 0, 0, tiled=True)
    (out,) = call(functools.partial(finish, groups), [(depth, width, thick)], table, z, w, edges, factors)
    return out


def solution(mesh):
    placed = (
        P("space", None, "proj"),
        P("space", None, "proj"),
        P("space", None, "proj"),
        P("space", None, None),
        P("space", None, None),
        P("proj"),
        P("proj"),
    )
    return jax.shard_map(
        local, mesh=mesh, in_specs=placed, out_specs=P("space", None, "proj"), check_vma=False
    )
```

```python
import functools
import math

import jax
import jax.numpy as jnp
from jax import lax
from jax.experimental import pallas as pl
from jax.experimental.pallas import tpu as pltpu
from jax.sharding import PartitionSpec as P

RMIN = 2.0
BETA = 8.0
EMIN = 0.05
PENALTY = 4.0

PLACES = 10
GROUP = 8
HALF = GROUP // 2


def pair_swap(size):
    return [(i, i ^ 1) for i in range(size)]


def near_swap(size):
    ups = [(i, i + 1) for i in range(1, size - 1, 2)]
    return ups + [(j, i) for i, j in ups]


def lanes_of(shape):
    return lax.broadcasted_iota(jnp.int32, shape, len(shape) - 1)


def turn(array, shift, axis):
    return pltpu.roll(array, shift % array.shape[axis], axis)


def squeeze(strips):
    rows, lanes = strips.shape[0] // 4, strips.shape[1]
    parts = [turn(strips[k * rows : (k + 1) * rows], k * lanes // 4, 1) for k in range(4)]
    block = lanes_of((rows, lanes)) // (lanes // 4)
    return functools.reduce(lambda out, k: jnp.where(block == k, parts[k], out), range(1, 4), parts[0])


def spread(squeezed):
    lanes = squeezed.shape[1]
    return jnp.concatenate([turn(squeezed, -k * lanes // 4, 1) for k in range(4)], axis=0)


def prepare(groups, fixed, load, support, out):
    core = lax.rem(lax.axis_index("space"), 2)
    layer = lax.axis_index("proj")
    width, thick = load.shape[1], load.shape[2] // groups
    lane = lanes_of((width, thick))
    lower = lax.rem(lane, GROUP) < HALF
    has_left = layer > 0
    has_right = layer < groups - 1
    centre = pl.ds(pl.multiple_of(layer * thick, thick), thick)
    left = pl.ds(pl.multiple_of(jnp.maximum(layer - 1, 0) * thick, thick), thick)
    right = pl.ds(pl.multiple_of(jnp.minimum(layer + 1, groups - 1) * thick, thick), thick)
    strips = jnp.zeros((width, thick), jnp.float32)
    for place in range(2):
        plane = lax.rem(place + core, 2)
        out[place * width : (place + 1) * width] = fixed[plane]
        for which, mask in enumerate((load, support)):
            held = 2 * which + place
            out[(2 + held) * width : (3 + held) * width] = mask[plane, :, centre].astype(jnp.float32)
            before = jnp.where(has_left, mask[plane, :, left].astype(jnp.float32), 0.0)
            after = jnp.where(has_right, mask[plane, :, right].astype(jnp.float32), 0.0)
            start = held * GROUP + HALF
            outside = jnp.where(lower, turn(before, start, 1), turn(after, start, 1))
            strips = jnp.where(lane // GROUP == held, outside, strips)
    out[6 * width :] = squeeze(strips)


def join(own, partner, near_out, mask_out):
    half = near_out.shape[0] // 2
    near_out[0:half] = own[0:half]
    near_out[half:] = partner[0:half]
    mask_out[...] = own[half:]


def pick(near, out):
    out[...] = near[0 : out.shape[0]]


def plane_of(ref, k, width):
    return ref[k * width : (k + 1) * width]


def frame_of(own, partner, near, inner):
    order = ((near, 2), (near, 3), (near, 1), (near, 0), (own, 0), (own, 1), (partner, 1), (partner, 0), (inner, 0), (inner, 1))
    return [plane_of(ref, k, near.shape[0] // 4) for ref, k in order]


def pack(own, partner, near, inner, thresholds, weights, out):
    width, thick = near.shape[0] // 4, near.shape[1]
    where = lanes_of((width, thick)) // GROUP
    packed = jnp.zeros((width, thick), jnp.float32)
    for place, plane in enumerate(frame_of(own, partner, near, inner)):
        packed = jnp.where(where == place, turn(plane, place * GROUP + HALF, 1), packed)
    out[0:width] = packed
    eta = thresholds[0].astype(jnp.float32) / 1000.0
    row = lax.broadcasted_iota(jnp.int32, (8, thick), 0)
    out[width:] = jnp.where(row == 0, eta, jnp.where(row == 1, weights[0], 0.0))


def around_y(plane, first, last):
    return jnp.where(first, 0.0, turn(plane, 1, 0)) + jnp.where(last, 0.0, turn(plane, -1, 0))


def joined(left, right, lower):
    return jnp.where(lower, turn(right, -1, 1), turn(left, 1, 1))


def edge_of(joint, place):
    return turn(joint, -(place * GROUP + HALF), 1)


def main_kernel(groups, size, *refs):
    n_side = 1 if groups == 2 else 2
    own, partner, near, inner, near_masks, packed = refs[:6]
    beside = refs[6 : 6 + n_side]
    tails = refs[6 + n_side : len(refs) - 5]
    table, z_out, w_out, edge_out, factor_out = refs[len(refs) - 5 :]

    spot = lax.axis_index("space")
    layer = lax.axis_index("proj")
    core = lax.rem(spot, 2)
    width, thick = near.shape[0] // 4, near.shape[1]
    shape = (width, thick)
    lane = lanes_of(shape)
    row = lax.broadcasted_iota(jnp.int32, shape, 0)
    first, last = row == 0, row == width - 1
    at_left, at_right = lane == 0, lane == thick - 1
    where = lane // GROUP
    slot = lax.rem(lane, GROUP)
    lower = slot < HALF
    near_real = jnp.where(jnp.where(core == 0, spot > 0, spot < size - 1), 1.0, 0.0)
    inner_real = jnp.where(jnp.where(core == 0, spot < size - 2, spot > 1), 1.0, 0.0)
    real = [near_real] * 4 + [1.0] * 4 + [inner_real] * 2
    has_left = jnp.where(layer > 0, 1.0, 0.0)
    has_right = jnp.where(layer < groups - 1, 1.0, 0.0)

    def real_at(places):
        return jnp.where(places < 4, near_real, jnp.where(places < 8, 1.0, inner_real))

    planes = frame_of(own, partner, near, inner)
    inside = packed[0:width]
    before = beside[0][0:width] * has_left
    after = beside[-1][0:width] * has_right
    fixed_left = jnp.where(lower, before, inside)
    fixed_right = jnp.where(lower, inside, after)

    two, three = RMIN - math.sqrt(2.0), RMIN - math.sqrt(3.0)
    heads, sides = [], []
    rows_left, rows_right = (around_y(v, first, last) for v in (fixed_left, fixed_right))
    joint = joined(fixed_left, fixed_right, lower)
    joint_rows = joined(rows_left, rows_right, lower)

    def around_z(plane, edge):
        return jnp.where(at_left, edge, turn(plane, 1, 1)) + jnp.where(at_right, edge, turn(plane, -1, 1))

    for place in range(PLACES):
        plane = planes[place]
        by_y = around_y(plane, first, last)
        by_z = around_z(plane, edge_of(joint, place))
        by_yz = around_z(by_y, edge_of(joint_rows, place))
        heads.append(2.0 * plane + (by_y + by_z) + two * by_yz)
        sides.append(plane + two * (by_y + by_z) + three * by_yz)

    def strip_z(v):
        return turn(v, 1, 1) + turn(v, -1, 1)

    def strip_x(v):
        return turn(v, GROUP, 1) + turn(v, -GROUP, 1)

    def strip_sum(v):
        return strip_x(v) + strip_z(v) + around_y(v, first, last)

    span_z = thick * groups
    count_y = jnp.where(first, 0.0, 1.0) + jnp.where(last, 0.0, 1.0)

    def counts(places_z):
        count_z = jnp.where(places_z >= 1, 1.0, 0.0) + jnp.where(places_z < span_z - 1, 1.0, 0.0)
        head = 2.0 + (count_y + count_z) + two * (count_y * count_z)
        side = 1.0 + two * (count_y + count_z) + three * (count_y * count_z)
        return head, side

    head, side = counts(layer * thick + lane)
    over_two, over_one = 1.0 / (head + 2.0 * side), 1.0 / (head + side)
    filtered = {}
    for place in range(1, PLACES - 1):
        total = heads[place] + sides[place - 1] + sides[place + 1]
        count_x = real[place - 1] + real[place + 1]
        filtered[place] = total * jnp.where(count_x > 1.5, over_two, over_one)

    def filter_strip(fixed, rows, places_z):
        by_z = strip_z(fixed)
        by_yz = strip_z(rows)
        total = 2.0 * fixed + (rows + by_z) + two * by_yz
        total = total + strip_x(fixed + two * (rows + by_z) + three * by_yz)
        head, side = counts(places_z)
        count_x = real_at(where - 1) + real_at(where + 1)
        return total / (head + count_x * side)

    filtered_left = filter_strip(fixed_left, rows_left, layer * thick - HALF + slot)
    filtered_right = filter_strip(fixed_right, rows_right, layer * thick + thick - HALF + slot)
    real_strip = jnp.where(where < PLACES, real_at(where), 0.0)
    real_left = jnp.where(lower, has_left, 1.0) * real_strip
    real_right = jnp.where(lower, 1.0, has_right) * real_strip

    def mask_planes(which):
        order = ((near_masks, 1), (near_masks, 0), (own, 2), (own, 3), (partner, 3), (partner, 2))
        return {place + 2: plane_of(ref, 2 * which + k, width) for place, (ref, k) in enumerate(order)}

    mine, theirs, nears = spread(own[6 * width :]), spread(partner[6 * width :]), spread(near_masks[4 * width :])

    def mask_strips(which, planes_of):
        out = jnp.zeros(shape, jnp.float32)
        ins = jnp.zeros(shape, jnp.float32)
        for place, source, held in ((2, nears, 1), (3, nears, 0), (4, mine, 0), (5, mine, 1), (6, theirs, 1), (7, theirs, 0)):
            out = jnp.where(where == place, turn(source, (place - held - 2 * which) * GROUP, 1), out)
            ins = jnp.where(where == place, turn(planes_of[place], place * GROUP + HALF, 1), ins)
        return jnp.where(lower, out, ins), jnp.where(lower, ins, out)

    load, support = mask_planes(0), mask_planes(1)
    load_left, load_right = mask_strips(0, load)
    support_left, support_right = mask_strips(1, support)

    tables = []
    for g in range(groups):
        eta, weight = packed[width : width + 1], packed[width + 1 : width + 2]
        for k, tail in enumerate(tails):
            mine = lax.rem(layer + k + 1, groups) == g
            eta = jnp.where(mine, tail[width : width + 1], eta)
            weight = jnp.where(mine, tail[width + 1 : width + 2], weight)
        if groups == 2:
            mine = layer != g
            eta = jnp.where(mine, beside[0][width : width + 1], eta)
            weight = jnp.where(mine, beside[0][width + 1 : width + 2], weight)
        low = jnp.tanh(BETA * eta)
        over_bottom = 1.0 / (low + jnp.tanh(BETA * (1.0 - eta)))

        def stiffness(density, present):
            inner_part = jnp.tanh(BETA * (density - eta))
            value = (low + inner_part) * over_bottom
            return inner_part, value, (EMIN + (1.0 - EMIN) * (value * value * value)) * present

        stiff = {}
        for place in range(1, PLACES - 1):
            inner_part, value, stiff[place] = stiffness(filtered[place], real[place])
            if place in (4, 5):
                slope = (BETA * over_bottom) * (1.0 - inner_part * inner_part)
                scale = -0.5 * 3.0 * (1.0 - EMIN) * weight
                factor_out[g, place - 4] = scale * (value * value) * slope
        stiff_left = stiffness(filtered_left, real_left)[2]
        stiff_right = stiffness(filtered_right, real_right)[2]

        def sum_of(field, joint, place):
            plane = field[place]
            return (
                (field[place - 1] + field[place + 1])
                + around_y(plane, first, last)
                + around_z(plane, edge_of(joint, place))
            )

        joint = joined(stiff_left, stiff_right, lower)
        links, over, z, sz = {}, {}, {}, {}
        for place in range(2, 8):
            links[place] = 3.0 * stiff[place] + 0.5 * sum_of(stiff, joint, place)
            over[place] = real[place] / jnp.maximum(links[place] + PENALTY * support[place], 0.1)
            z[place] = load[place] * over[place]
            sz[place] = stiff[place] * z[place]

        def strip_start(stiff_of, load_of, support_of, present):
            link = 3.0 * stiff_of + 0.5 * strip_sum(stiff_of)
            inverse = present / jnp.maximum(link + PENALTY * support_of, 0.1)
            z_of = load_of * inverse
            q_of = link * z_of - 0.5 * (stiff_of * strip_sum(z_of) + strip_sum(stiff_of * z_of))
            return z_of, q_of * inverse

        z_left, w_left = strip_start(stiff_left, load_left, support_left, real_left)
        z_right, w_right = strip_start(stiff_right, load_right, support_right, real_right)
        joint_z = joined(z_left, z_right, lower)
        joint_sz = joined(stiff_left * z_left, stiff_right * z_right, lower)
        joint_w = joined(w_left, w_right, lower)
        joint_sw = joined(stiff_left * w_left, stiff_right * w_right, lower)

        q, w, sw = {}, {}, {}
        for place in range(3, 7):
            q[place] = links[place] * z[place] - 0.5 * (
                stiff[place] * sum_of(z, joint_z, place) + sum_of(sz, joint_sz, place)
            )
            w[place] = q[place] * over[place]
            sw[place] = stiff[place] * w[place]
            z_out[g, place - 3] = z[place]
            w_out[g, place - 3] = w[place]
        edge_out[g, 0] = joint_z
        edge_out[g, 1] = joint_w
        sums = [0.0, 0.0, 0.0, 0.0]
        for place in (4, 5):
            aw = links[place] * w[place] - 0.5 * (
                stiff[place] * sum_of(w, joint_w, place) + sum_of(sw, joint_sw, place)
            )
            terms = (z[place], z[place] * q[place], q[place] * w[place], w[place] * aw)
            sums = [a + b for a, b in zip(sums, terms)]
        tables += [jnp.sum(s, axis=0, keepdims=True) for s in sums]

    lane_row = lanes_of((1, thick))
    line = jnp.zeros((1, thick), jnp.float32)
    for k, part in enumerate(tables):
        line = jnp.where(lane_row == k, jnp.sum(part, axis=1, keepdims=True), line)
    table[...] = jnp.broadcast_to(line, table.shape)


def finish(groups, table, z_in, w_in, edges, factors, out):
    core = lax.rem(lax.axis_index("space"), 2)
    width, thick = out.shape[1:]
    shape = (width, thick)
    lane = lanes_of(shape)
    row = lax.broadcasted_iota(jnp.int32, shape, 0)
    first, last = row == 0, row == width - 1
    at_left, at_right = lane == 0, lane == thick - 1
    line = jnp.sum(table[...], axis=0, keepdims=True)
    lane_row = lanes_of((1, thick))
    total = [jnp.zeros(shape, jnp.float32), jnp.zeros(shape, jnp.float32)]
    for g in range(groups):
        m0, m1, m2, m3 = (
            jnp.sum(jnp.where(lane_row == 4 * g + k, line, 0.0), axis=1, keepdims=True) for k in range(4)
        )
        step_one = m0 / m1
        rz_next = step_one * step_one * m2 - m0
        factor = rz_next / m0
        curve = (m1 - 2.0 * step_one * m2 + step_one * step_one * m3) - factor * factor * m1
        step_two = rz_next / curve
        of_z = step_one + step_two * (1.0 + factor)
        of_w = -step_one * step_two
        u = [of_z * z_in[g, k] + of_w * w_in[g, k] for k in range(4)]
        joint = of_z * edges[g, 0] + of_w * edges[g, 1]
        for k in (1, 2):
            edge = edge_of(joint, k + 3)
            plane = u[k]
            others = (
                u[k - 1],
                u[k + 1],
                jnp.where(first, 0.0, turn(plane, 1, 0)),
                jnp.where(last, 0.0, turn(plane, -1, 0)),
                jnp.where(at_left, edge, turn(plane, 1, 1)),
                jnp.where(at_right, edge, turn(plane, -1, 1)),
            )
            squares = [(plane - other) * (plane - other) for other in others]
            total[k - 1] = total[k - 1] + factors[g, k - 1] * sum(squares[1:], squares[0])
    for k in range(2):
        out[lax.rem(k + core, 2)] = total[k]


def call(body, outs, *args, scalars=()):
    smem = pl.BlockSpec(memory_space=pltpu.SMEM)
    return pl.pallas_call(
        body,
        out_shape=[jax.ShapeDtypeStruct(shape, jnp.float32) for shape in outs],
        in_specs=[pl.BlockSpec(memory_space=pltpu.VMEM)] * len(args) + [smem] * len(scalars),
        out_specs=[pl.BlockSpec(memory_space=pltpu.VMEM)] * len(outs),
        compiler_params=pltpu.CompilerParams(vmem_limit_bytes=32 * 1024 * 1024),
    )(*args, *scalars)


def local(design, solid_mask, void_mask, load_mask, support_mask, thresholds, group_weight):
    depth, width, thick = design.shape
    size, groups = lax.axis_size("space"), lax.axis_size("proj")
    quarter = width // 4
    pair, near_pairs = pair_swap(size), near_swap(size)
    fixed = jnp.where(solid_mask == 1, 1.0, jnp.where(void_mask == 1, 0.0, design))
    (own,) = call(
        functools.partial(prepare, groups), [(6 * width + quarter, thick)], fixed, load_mask, support_mask
    )
    partner = lax.ppermute(own, "space", pair)
    both, masks = call(join, [(4 * width, thick), (4 * width + quarter, thick)], own, partner)
    near = lax.ppermute(both, "space", near_pairs)
    near_masks = lax.ppermute(masks, "space", near_pairs)
    (beyond,) = call(pick, [(2 * width, thick)], near)
    inner = lax.ppermute(beyond, "space", pair)
    frame = (own, partner, near, inner)
    (packed,) = call(pack, [(width + 8, thick)], *frame, scalars=(thresholds, group_weight))
    steps = (1,) if groups == 2 else (1, -1)
    beside = [
        lax.ppermute(
            packed, "proj", [(g, (g + s) % groups) for g in range(groups) if groups == 2 or 0 <= g + s < groups]
        )
        for s in steps
    ]
    tails = []
    if groups > 2:
        for k in range(1, groups):
            tails.append(lax.ppermute(packed, "proj", [((g + k) % groups, g) for g in range(groups)]))
    rows = size * groups
    table, z, w, edges, factors = call(
        functools.partial(main_kernel, groups, size),
        [(rows, thick), (groups, 4, width, thick), (groups, 4, width, thick), (groups, 2, width, thick), (groups, 2, width, thick)],
        *frame, near_masks, packed, *beside, *tails,
    )
    table = lax.all_to_all(table, ("proj", "space"), 0, 0, tiled=True)
    (out,) = call(functools.partial(finish, groups), [(depth, width, thick)], table, z, w, edges, factors)
    return out


def solution(mesh):
    placed = (
        P("space", None, "proj"),
        P("space", None, "proj"),
        P("space", None, "proj"),
        P("space", None, None),
        P("space", None, None),
        P("proj"),
        P("proj"),
    )
    return jax.shard_map(
        local, mesh=mesh, in_specs=placed, out_specs=P("space", None, "proj"), check_vma=False
    )
```

```python
import functools
import math

import jax
import jax.numpy as jnp
from jax import lax
from jax.experimental import pallas as pl
from jax.experimental.pallas import tpu as pltpu
from jax.sharding import PartitionSpec as P

RMIN = 2.0
BETA = 8.0
EMIN = 0.05
PENALTY = 4.0

PLACES = 10
GROUP = 8
HALF = GROUP // 2


def pair_swap(size):
    return [(i, i ^ 1) for i in range(size)]


def near_swap(size):
    ups = [(i, i + 1) for i in range(1, size - 1, 2)]
    return ups + [(j, i) for i, j in ups]


def lanes_of(shape):
    return lax.broadcasted_iota(jnp.int32, shape, len(shape) - 1)


def turn(array, shift, axis):
    return pltpu.roll(array, shift % array.shape[axis], axis)


def squeeze(strips):
    rows, lanes = strips.shape[0] // 4, strips.shape[1]
    parts = [turn(strips[k * rows : (k + 1) * rows], k * lanes // 4, 1) for k in range(4)]
    block = lanes_of((rows, lanes)) // (lanes // 4)
    return functools.reduce(lambda out, k: jnp.where(block == k, parts[k], out), range(1, 4), parts[0])


def spread(squeezed):
    lanes = squeezed.shape[1]
    return jnp.concatenate([turn(squeezed, -k * lanes // 4, 1) for k in range(4)], axis=0)


def prepare(groups, fixed, load, support, out):
    core = lax.rem(lax.axis_index("space"), 2)
    layer = lax.axis_index("proj")
    width, thick = load.shape[1], load.shape[2] // groups
    lane = lanes_of((width, thick))
    lower = lax.rem(lane, GROUP) < HALF
    has_left = layer > 0
    has_right = layer < groups - 1
    centre = pl.ds(pl.multiple_of(layer * thick, thick), thick)
    left = pl.ds(pl.multiple_of(jnp.maximum(layer - 1, 0) * thick, thick), thick)
    right = pl.ds(pl.multiple_of(jnp.minimum(layer + 1, groups - 1) * thick, thick), thick)
    strips = jnp.zeros((width, thick), jnp.float32)
    for place in range(2):
        plane = lax.rem(place + core, 2)
        out[place * width : (place + 1) * width] = fixed[plane]
        for which, mask in enumerate((load, support)):
            held = 2 * which + place
            out[(2 + held) * width : (3 + held) * width] = mask[plane, :, centre].astype(jnp.float32)
            before = jnp.where(has_left, mask[plane, :, left].astype(jnp.float32), 0.0)
            after = jnp.where(has_right, mask[plane, :, right].astype(jnp.float32), 0.0)
            start = held * GROUP + HALF
            outside = jnp.where(lower, turn(before, start, 1), turn(after, start, 1))
            strips = jnp.where(lane // GROUP == held, outside, strips)
    out[6 * width :] = squeeze(strips)


def join(own, partner, near_out, mask_out):
    half = near_out.shape[0] // 2
    near_out[0:half] = own[0:half]
    near_out[half:] = partner[0:half]
    mask_out[...] = own[half:]


def pick(near, out):
    out[...] = near[0 : out.shape[0]]


def plane_of(ref, k, width):
    return ref[k * width : (k + 1) * width]


def frame_of(own, partner, near, inner):
    order = ((near, 2), (near, 3), (near, 1), (near, 0), (own, 0), (own, 1), (partner, 1), (partner, 0), (inner, 0), (inner, 1))
    return [plane_of(ref, k, near.shape[0] // 4) for ref, k in order]


def pack(own, partner, near, inner, thresholds, weights, out):
    width, thick = near.shape[0] // 4, near.shape[1]
    where = lanes_of((width, thick)) // GROUP
    packed = jnp.zeros((width, thick), jnp.float32)
    for place, plane in enumerate(frame_of(own, partner, near, inner)):
        packed = jnp.where(where == place, turn(plane, place * GROUP + HALF, 1), packed)
    out[0:width] = packed
    eta = thresholds[0].astype(jnp.float32) / 1000.0
    row = lax.broadcasted_iota(jnp.int32, (8, thick), 0)
    out[width:] = jnp.where(row == 0, eta, jnp.where(row == 1, weights[0], 0.0))


def around_y(plane, first, last):
    return jnp.where(first, 0.0, turn(plane, 1, 0)) + jnp.where(last, 0.0, turn(plane, -1, 0))


class Spot:
    def __init__(self, groups, size, width, thick):
        self.groups, self.width, self.thick = groups, width, thick
        self.spot, self.layer = lax.axis_index("space"), lax.axis_index("proj")
        core = lax.rem(self.spot, 2)
        self.shape = (width, thick)
        self.lane = lanes_of(self.shape)
        row = lax.broadcasted_iota(jnp.int32, self.shape, 0)
        self.first, self.last = row == 0, row == width - 1
        self.at_left, self.at_right = self.lane == 0, self.lane == thick - 1
        self.where = self.lane // GROUP
        self.slot = lax.rem(self.lane, GROUP)
        self.lower = self.slot < HALF
        self.near_real = jnp.where(jnp.where(core == 0, self.spot > 0, self.spot < size - 1), 1.0, 0.0)
        self.inner_real = jnp.where(jnp.where(core == 0, self.spot < size - 2, self.spot > 1), 1.0, 0.0)
        self.real = [self.near_real] * 4 + [1.0] * 4 + [self.inner_real] * 2
        self.has_left = jnp.where(self.layer > 0, 1.0, 0.0)
        self.has_right = jnp.where(self.layer < groups - 1, 1.0, 0.0)
        self.n_strips = 1 if groups == 2 else 2
        self.is_right = self.layer == 0
        self.base = jnp.where(self.is_right, HALF + 1, HALF - 1) if groups == 2 else HALF

    def real_at(self, places):
        return jnp.where(places < 4, self.near_real, jnp.where(places < 8, 1.0, self.inner_real))

    def strips(self, inside, outside):
        right = jnp.where(self.lower, inside, outside[-1])
        left = jnp.where(self.lower, outside[0], inside)
        return [jnp.where(self.is_right, right, left)] if self.n_strips == 1 else [left, right]

    def strip_z(self):
        left, right = (self.layer * self.thick + self.slot + shift for shift in (-HALF, self.thick - HALF))
        return [jnp.where(self.is_right, right, left)] if self.n_strips == 1 else [left, right]

    def joint(self, lefts, rights):
        if self.n_strips == 1:
            return jnp.where(self.is_right, rights[0], lefts[0])
        return jnp.where(self.lower, turn(rights[1], -1, 1), turn(lefts[0], 1, 1))

    def edge(self, joint, place):
        return pltpu.roll(joint, self.thick - (place * GROUP + self.base), 1)


def count_terms(count_y, count_z):
    two, three = RMIN - math.sqrt(2.0), RMIN - math.sqrt(3.0)
    head = 2.0 + (count_y + count_z) + two * (count_y * count_z)
    side = 1.0 + two * (count_y + count_z) + three * (count_y * count_z)
    return head, side


def filter_kernel(groups, size, own, partner, near, inner, near_masks, filtered, masks, rows):
    width, thick = near.shape[0] // 4, near.shape[1]
    at = Spot(groups, size, width, thick)
    two, three = RMIN - math.sqrt(2.0), RMIN - math.sqrt(3.0)
    planes = frame_of(own, partner, near, inner)
    rows[:, 0:8] = jnp.zeros((PLACES, 8, thick), jnp.float32)
    rows[:, 8 + width :] = jnp.zeros((PLACES, 8, thick), jnp.float32)
    for place in range(PLACES):
        rows[place, 8 : 8 + width] = planes[place]

    count_y = jnp.where(at.first, 0.0, 1.0) + jnp.where(at.last, 0.0, 1.0)
    places_z = at.layer * thick + at.lane
    count_z = jnp.where(places_z >= 1, 1.0, 0.0) + jnp.where(places_z < groups * thick - 1, 1.0, 0.0)
    head, side = count_terms(count_y, count_z)
    over_two, over_one = 1.0 / (head + 2.0 * side), 1.0 / (head + side)
    straight, once, twice = [], [], []
    for place in range(PLACES):
        plane = planes[place]
        by_y = rows[place, 7 : 7 + width] + rows[place, 9 : 9 + width]
        straight.append(2.0 * plane + by_y)
        once.append(plane + two * by_y)
        twice.append(two * plane + three * by_y)
    for place in range(1, PLACES - 1):
        beside = once[place] + (twice[place - 1] + twice[place + 1])
        by_z = jnp.where(at.at_left, 0.0, turn(beside, 1, 1)) + jnp.where(at.at_right, 0.0, turn(beside, -1, 1))
        total = straight[place] + (once[place - 1] + once[place + 1]) + by_z
        count_x = at.real[place - 1] + at.real[place + 1]
        filtered[place - 1] = total * jnp.where(count_x > 1.5, over_two, over_one)

    mine, theirs, nears = spread(own[6 * width :]), spread(partner[6 * width :]), spread(near_masks[4 * width :])
    for which in (0, 1):
        order = ((near_masks, 1), (near_masks, 0), (own, 2), (own, 3), (partner, 3), (partner, 2))
        outer = jnp.zeros(at.shape, jnp.float32)
        inner_part = jnp.zeros(at.shape, jnp.float32)
        sources = ((nears, 1), (nears, 0), (mine, 0), (mine, 1), (theirs, 1), (theirs, 0))
        for place, (ref, k), (source, held) in zip(range(2, 8), order, sources):
            outer = jnp.where(at.where == place, turn(source, (place - held - 2 * which) * GROUP, 1), outer)
            plane = plane_of(ref, 2 * which + k, width)
            inner_part = jnp.where(at.where == place, turn(plane, place * GROUP + HALF, 1), inner_part)
        for k, value in enumerate(at.strips(inner_part, [outer, outer])):
            masks[which, k] = value


def main_kernel(groups, size, *refs):
    n_side = 1 if groups == 2 else 2
    own, partner, near_masks, packed, filtered_in, masks = refs[:6]
    beside, tails = refs[6 : 6 + n_side], refs[6 + n_side : len(refs) - 8]
    table, z_out, w_out, edge_out, factor_out, s_rows, z_rows, w_rows = refs[len(refs) - 8 :]
    width, thick = packed.shape[0] - 8, packed.shape[1]
    at = Spot(groups, size, width, thick)
    first, last, at_left, at_right = at.first, at.last, at.at_left, at.at_right
    two, three = RMIN - math.sqrt(2.0), RMIN - math.sqrt(3.0)
    for ref in (s_rows, z_rows, w_rows):
        ref[:, 0:8] = jnp.zeros((ref.shape[0], 8, thick), jnp.float32)
        ref[:, 8 + width :] = jnp.zeros((ref.shape[0], 8, thick), jnp.float32)

    def strip_z(v):
        return turn(v, 1, 1) + turn(v, -1, 1)

    def strip_x(v):
        return turn(v, GROUP, 1) + turn(v, -GROUP, 1)

    outside = [beside[0][0:width] * at.has_left, beside[-1][0:width] * at.has_right]
    fixed = at.strips(packed[0:width], outside)

    count_y = jnp.where(first, 0.0, 1.0) + jnp.where(last, 0.0, 1.0)
    count_x = at.real_at(at.where - 1) + at.real_at(at.where + 1)
    span_z = thick * groups
    filtered_strips, presents, sums = [], [], []
    for strip, z_at in zip(fixed, at.strip_z()):
        by_y = around_y(strip, first, last)
        once = strip + two * by_y
        total = 2.0 * strip + by_y + strip_x(once)
        sums.append(once + strip_x(two * strip + three * by_y))
        total = total + strip_z(sums[-1])
        count_z = jnp.where(z_at >= 1, 1.0, 0.0) + jnp.where(z_at < span_z - 1, 1.0, 0.0)
        head, side = count_terms(count_y, count_z)
        filtered_strips.append(total / (head + count_x * side))
        real = jnp.where((at.where < PLACES) & (z_at >= 0) & (z_at < span_z), at.real_at(at.where), 0.0)
        presents.append(real)
    head, side = count_terms(count_y, 2.0)
    joint = at.joint(sums, sums) / (head + count_x * side)
    ends = jnp.where(at_left, at.has_left, jnp.where(at_right, at.has_right, 0.0))
    filtered = {
        place: filtered_in[place - 1] + at.edge(joint, place) * ends for place in range(1, PLACES - 1)
    }

    def mask_planes(which):
        order = ((near_masks, 1), (near_masks, 0), (own, 2), (own, 3), (partner, 3), (partner, 2))
        return {place + 2: plane_of(ref, 2 * which + k, width) for place, (ref, k) in enumerate(order)}

    load, support = mask_planes(0), mask_planes(1)
    tables = []
    for g in range(groups):
        eta, weight = packed[width : width + 1], packed[width + 1 : width + 2]
        for k, tail in enumerate(tails):
            mine = lax.rem(at.layer + k + 1, groups) == g
            eta = jnp.where(mine, tail[width : width + 1], eta)
            weight = jnp.where(mine, tail[width + 1 : width + 2], weight)
        if groups == 2:
            mine = at.layer != g
            eta = jnp.where(mine, beside[0][width : width + 1], eta)
            weight = jnp.where(mine, beside[0][width + 1 : width + 2], weight)
        low = jnp.tanh(BETA * eta)
        over_bottom = 1.0 / (low + jnp.tanh(BETA * (1.0 - eta)))

        def stiffness(density, present):
            inner_part = jnp.tanh(BETA * (density - eta))
            value = (low + inner_part) * over_bottom
            return inner_part, value, (EMIN + (1.0 - EMIN) * (value * value * value)) * present

        stiff = {}
        for place in range(1, PLACES - 1):
            inner_part, value, stiff[place] = stiffness(filtered[place], at.real[place])
            if place in (4, 5):
                slope = (BETA * over_bottom) * (1.0 - inner_part * inner_part)
                scale = -0.5 * 3.0 * (1.0 - EMIN) * weight
                factor_out[g, place - 4] = scale * (value * value) * slope
            if 2 <= place < 8:
                s_rows[place - 2, 8 : 8 + width] = stiff[place]

        z_strips, w_strips, flow_strips, flow_w_strips, step_z, step_w, s_strips = [], [], [], [], [], [], []
        for k in range(at.n_strips):
            s = stiffness(filtered_strips[k], presents[k])[2]
            s_next, s_right = turn(s, -GROUP, 1), turn(s, -1, 1)
            s_up, s_down = jnp.where(first, 0.0, turn(s, 1, 0)), jnp.where(last, 0.0, turn(s, -1, 0))
            links = 6.0 * s + (s_next + turn(s, GROUP, 1)) + (s_right + turn(s, 1, 1)) + (s_up + s_down)
            inverse = presents[k] / jnp.maximum(0.5 * links + PENALTY * masks[1, k], 0.1)
            z = masks[0, k] * inverse
            flow_x = (s + s_next) * (z - turn(z, -GROUP, 1))
            z_step = z - turn(z, -1, 1)
            k_right = s + s_right
            flow_z = k_right * z_step
            z_up, z_down = jnp.where(first, 0.0, turn(z, 1, 0)), jnp.where(last, 0.0, turn(z, -1, 0))
            q = (flow_x - turn(flow_x, GROUP, 1)) + (flow_z - turn(flow_z, 1, 1))
            q = q + ((s + s_up) * (z - z_up) + (s + s_down) * (z - z_down))
            w = (0.5 * q) * inverse
            w_step = w - turn(w, -1, 1)
            s_strips.append(s)
            z_strips.append(z)
            w_strips.append(w)
            flow_strips.append(flow_z)
            flow_w_strips.append(k_right * w_step)
            step_z.append(z_step)
            step_w.append(w_step)

        def right_of(plane, edge):
            return jnp.where(at_right, edge * at.has_right, turn(plane, -1, 1))

        joint = at.joint(s_strips, s_strips)
        over, z, k_right = {}, {}, {}
        for place in range(2, 8):
            s = stiff[place]
            edge = at.edge(joint, place)
            s_right = right_of(s, edge)
            s_left = jnp.where(at_left, edge * at.has_left, turn(s, 1, 1))
            s_up, s_down = s_rows[place - 2, 7 : 7 + width], s_rows[place - 2, 9 : 9 + width]
            links = 6.0 * s + (stiff[place - 1] + stiff[place + 1]) + (s_left + s_right) + (s_up + s_down)
            over[place] = at.real[place] / jnp.maximum(0.5 * links + PENALTY * support[place], 0.1)
            z[place] = load[place] * over[place]
            k_right[place] = s + s_right

        def image(field, rows, start, joint, place, flow_before, flow_after):
            v, s = field[place], stiff[place]
            edge = at.edge(joint, place)
            flow_z = k_right[place] * (v - right_of(v, edge))
            outer = jnp.where(at.layer > 0, edge, -(s * v))
            total = (flow_after - flow_before) + (flow_z - jnp.where(at_left, outer, turn(flow_z, 1, 1)))
            s_up, s_down = s_rows[place - 2, 7 : 7 + width], s_rows[place - 2, 9 : 9 + width]
            v_up, v_down = rows[place - start, 7 : 7 + width], rows[place - start, 9 : 9 + width]
            return total + ((s + s_up) * (v - v_up) + (s + s_down) * (v - v_down))

        def flow_x(field, place):
            return (stiff[place] + stiff[place + 1]) * (field[place] - field[place + 1])

        for place in range(3, 7):
            z_rows[place - 3, 8 : 8 + width] = z[place]
            z_out[g, place - 3] = z[place]
        joint_z = at.joint(flow_strips, z_strips)
        flows = {place: flow_x(z, place) for place in range(2, 7)}
        q, w = {}, {}
        for place in range(3, 7):
            q[place] = 0.5 * image(z, z_rows, 3, joint_z, place, flows[place - 1], flows[place])
            w[place] = q[place] * over[place]
            w_out[g, place - 3] = w[place]
        for place in (4, 5):
            w_rows[place - 4, 8 : 8 + width] = w[place]
        joint_w = at.joint(flow_w_strips, w_strips)
        edge_out[g, 0] = at.joint(step_z, z_strips)
        edge_out[g, 1] = at.joint(step_w, w_strips)
        flows = {place: flow_x(w, place) for place in range(3, 6)}
        totals = [0.0, 0.0, 0.0, 0.0]
        for place in (4, 5):
            aw = 0.5 * image(w, w_rows, 4, joint_w, place, flows[place - 1], flows[place])
            terms = (z[place], z[place] * q[place], q[place] * w[place], w[place] * aw)
            totals = [a + b for a, b in zip(totals, terms)]
        tables += [jnp.sum(s, axis=0, keepdims=True) for s in totals]

    lane_row = lanes_of((1, thick))
    line = jnp.zeros((1, thick), jnp.float32)
    for k, part in enumerate(tables):
        line = jnp.where(lane_row == k, jnp.sum(part, axis=1, keepdims=True), line)
    table[...] = jnp.broadcast_to(line, table.shape)


def finish(groups, size, table, z_in, w_in, edges, factors, out):
    width, thick = out.shape[1:]
    at = Spot(groups, size, width, thick)
    core = lax.rem(at.spot, 2)
    line = jnp.sum(table[...], axis=0, keepdims=True)
    lane_row = lanes_of((1, thick))
    total = [jnp.zeros(at.shape, jnp.float32), jnp.zeros(at.shape, jnp.float32)]
    for g in range(groups):
        m0, m1, m2, m3 = (
            jnp.sum(jnp.where(lane_row == 4 * g + k, line, 0.0), axis=1, keepdims=True) for k in range(4)
        )
        step_one = m0 / m1
        rz_next = step_one * step_one * m2 - m0
        factor = rz_next / m0
        curve = (m1 - 2.0 * step_one * m2 + step_one * step_one * m3) - factor * factor * m1
        step_two = rz_next / curve
        of_z = step_one + step_two * (1.0 + factor)
        of_w = -step_one * step_two
        u = [of_z * z_in[g, k] + of_w * w_in[g, k] for k in range(4)]
        joint = of_z * edges[g, 0] + of_w * edges[g, 1]
        between = [u[k] - u[k + 1] for k in range(3)]
        for k in (1, 2):
            edge = at.edge(joint, k + 3)
            plane = u[k]
            step = plane - jnp.where(at.at_right, edge * at.has_right, turn(plane, -1, 1))
            back = jnp.where(at.at_left, jnp.where(at.layer > 0, edge, -plane), turn(step, 1, 1))
            up = plane - jnp.where(at.first, 0.0, turn(plane, 1, 0))
            down = plane - jnp.where(at.last, 0.0, turn(plane, -1, 0))
            squares = [v * v for v in (between[k - 1], between[k], step, back, up, down)]
            total[k - 1] = total[k - 1] + factors[g, k - 1] * sum(squares[1:], squares[0])
    for k in range(2):
        out[lax.rem(k + core, 2)] = total[k]


def call(body, outs, *args, scalars=(), scratch=()):
    smem = pl.BlockSpec(memory_space=pltpu.SMEM)
    return pl.pallas_call(
        body,
        out_shape=[jax.ShapeDtypeStruct(shape, jnp.float32) for shape in outs],
        in_specs=[pl.BlockSpec(memory_space=pltpu.VMEM)] * len(args) + [smem] * len(scalars),
        out_specs=[pl.BlockSpec(memory_space=pltpu.VMEM)] * len(outs),
        scratch_shapes=[pltpu.VMEM(shape, jnp.float32) for shape in scratch],
        compiler_params=pltpu.CompilerParams(vmem_limit_bytes=32 * 1024 * 1024),
    )(*args, *scalars)


def local(design, solid_mask, void_mask, load_mask, support_mask, thresholds, group_weight):
    depth, width, thick = design.shape
    size, groups = lax.axis_size("space"), lax.axis_size("proj")
    quarter = width // 4
    pair, near_pairs = pair_swap(size), near_swap(size)
    fixed = jnp.where(solid_mask == 1, 1.0, jnp.where(void_mask == 1, 0.0, design))
    (own,) = call(
        functools.partial(prepare, groups), [(6 * width + quarter, thick)], fixed, load_mask, support_mask
    )
    partner = lax.ppermute(own, "space", pair)
    both, masks = call(join, [(4 * width, thick), (4 * width + quarter, thick)], own, partner)
    near = lax.ppermute(both, "space", near_pairs)
    near_masks = lax.ppermute(masks, "space", near_pairs)
    (beyond,) = call(pick, [(2 * width, thick)], near)
    inner = lax.ppermute(beyond, "space", pair)
    (packed,) = call(pack, [(width + 8, thick)], own, partner, near, inner, scalars=(thresholds, group_weight))
    steps = (1,) if groups == 2 else (1, -1)
    beside = [
        lax.ppermute(
            packed, "proj", [(g, (g + s) % groups) for g in range(groups) if groups == 2 or 0 <= g + s < groups]
        )
        for s in steps
    ]
    tails = []
    if groups > 2:
        for k in range(1, groups):
            tails.append(lax.ppermute(packed, "proj", [((g + k) % groups, g) for g in range(groups)]))
    n_strips = 1 if groups == 2 else 2
    plane = (width, thick)
    filtered, mask_strips = call(
        functools.partial(filter_kernel, groups, size),
        [(PLACES - 2, *plane), (2, n_strips, *plane)],
        own, partner, near, inner, near_masks,
        scratch=[(PLACES, width + 16, thick)],
    )
    rows = size * groups
    table, z, w, edges, factors = call(
        functools.partial(main_kernel, groups, size),
        [(rows, thick), (groups, 4, *plane), (groups, 4, *plane), (groups, 2, *plane), (groups, 2, *plane)],
        own, partner, near_masks, packed, filtered, mask_strips, *beside, *tails,
        scratch=[(6, width + 16, thick), (4, width + 16, thick), (2, width + 16, thick)],
    )
    table = lax.all_to_all(table, ("proj", "space"), 0, 0, tiled=True)
    (out,) = call(functools.partial(finish, groups, size), [(depth, *plane)], table, z, w, edges, factors)
    return out


def solution(mesh):
    placed = (
        P("space", None, "proj"),
        P("space", None, "proj"),
        P("space", None, "proj"),
        P("space", None, None),
        P("space", None, None),
        P("proj"),
        P("proj"),
    )
    return jax.shard_map(
        local, mesh=mesh, in_specs=placed, out_specs=P("space", None, "proj"), check_vma=False
    )
```

```python
import functools
import math

import jax
import jax.numpy as jnp
from jax import lax
from jax.experimental import pallas as pl
from jax.experimental.pallas import tpu as pltpu
from jax.sharding import PartitionSpec as P

RMIN = 2.0
BETA = 8.0
EMIN = 0.05
PENALTY = 4.0

PLACES = 10
GROUP = 8
HALF = GROUP // 2
WIDE = 2 * GROUP
INNER = PLACES - 2


def pair_swap(size):
    return [(i, i ^ 1) for i in range(size)]


def near_swap(size):
    ups = [(i, i + 1) for i in range(1, size - 1, 2)]
    return ups + [(j, i) for i, j in ups]


def lanes_of(shape):
    return lax.broadcasted_iota(jnp.int32, shape, len(shape) - 1)


def turn(array, shift, axis):
    return pltpu.roll(array, shift % array.shape[axis], axis)


def squeeze(strips):
    rows, lanes = strips.shape[0] // 4, strips.shape[1]
    parts = [turn(strips[k * rows : (k + 1) * rows], k * lanes // 4, 1) for k in range(4)]
    block = lanes_of((rows, lanes)) // (lanes // 4)
    return functools.reduce(lambda out, k: jnp.where(block == k, parts[k], out), range(1, 4), parts[0])


def spread(squeezed):
    lanes = squeezed.shape[1]
    return jnp.concatenate([turn(squeezed, -k * lanes // 4, 1) for k in range(4)], axis=0)


def prepare(groups, load, support, mask_out):
    core = lax.rem(lax.axis_index("space"), 2)
    layer = lax.axis_index("proj")
    width, thick = load.shape[1], load.shape[2] // groups
    lane = lanes_of((width, thick))
    lower = lax.rem(lane, GROUP) < HALF
    has_left = layer > 0
    has_right = layer < groups - 1
    centre = pl.ds(pl.multiple_of(layer * thick, thick), thick)
    left = pl.ds(pl.multiple_of(jnp.maximum(layer - 1, 0) * thick, thick), thick)
    right = pl.ds(pl.multiple_of(jnp.minimum(layer + 1, groups - 1) * thick, thick), thick)
    strips = jnp.zeros((width, thick), jnp.float32)
    for place in range(2):
        plane = lax.rem(place + core, 2)
        for which, mask in enumerate((load, support)):
            held = 2 * which + place
            mask_out[held * width : (held + 1) * width] = mask[plane, :, centre].astype(jnp.float32)
            before = jnp.where(has_left, mask[plane, :, left].astype(jnp.float32), 0.0)
            after = jnp.where(has_right, mask[plane, :, right].astype(jnp.float32), 0.0)
            shift = held * GROUP + HALF
            outside = jnp.where(lower, turn(before, shift, 1), turn(after, shift, 1))
            strips = jnp.where(lane // GROUP == held, outside, strips)
    mask_out[4 * width :] = squeeze(strips)


def order(fixed, partner_fixed, thresholds, weights, out, scalars):
    row = lax.broadcasted_iota(jnp.int32, scalars.shape, 0)
    scalars[...] = jnp.where(row == 0, thresholds[0].astype(jnp.float32) / 1000.0, jnp.where(row == 1, weights[0], 0.0))
    core = lax.rem(lax.axis_index("space"), 2)
    width = fixed.shape[1]
    for place in range(2):
        plane = lax.rem(place + core, 2)
        out[place * width : (place + 1) * width] = fixed[plane]
        out[(2 + place) * width : (3 + place) * width] = partner_fixed[1 - plane]


def keep(array, out):
    out[...] = array[...]


def pick(near, out):
    out[...] = near[0 : out.shape[0]]


def plane_of(ref, k, width):
    return ref[k * width : (k + 1) * width]


def frame_of(own, near, inner):
    order = ((near, 2), (near, 3), (near, 1), (near, 0), (own, 0), (own, 1), (own, 3), (own, 2), (inner, 0), (inner, 1))
    return [plane_of(ref, k, near.shape[0] // 4) for ref, k in order]


def fold(strips, lower):
    half = strips.shape[0] // 2
    low = lax.rem(lanes_of((half, strips.shape[1])), GROUP) < HALF
    top, bottom = strips[:half], strips[half:]
    folded_low = jnp.where(low, top, turn(bottom, HALF, 1))
    folded_high = jnp.where(low, turn(bottom, -HALF, 1), top)
    return jnp.where(lower, folded_low, folded_high)


def unfold(folded, lower):
    return jnp.concatenate([folded, jnp.where(lower, turn(folded, -HALF, 1), turn(folded, HALF, 1))], axis=0)


def pack(groups, own, near, inner, inside, *outs):
    width, thick = inside.shape
    lane = lanes_of((width, thick))
    strips = jnp.zeros((width, thick), jnp.float32)
    for place, plane in enumerate(frame_of(own, near, inner)):
        strips = jnp.where(lane // GROUP == place, turn(plane, place * GROUP + HALF, 1), strips)
    inside[...] = strips
    for out, lower in zip(outs, (lax.axis_index("proj") == 0,) if groups == 2 else (True, False)):
        out[...] = fold(strips, lower)


def around_y(plane, first, last):
    return jnp.where(first, 0.0, turn(plane, 1, 0)) + jnp.where(last, 0.0, turn(plane, -1, 0))


class Spot:
    def __init__(self, groups, size, width, thick):
        self.groups, self.width, self.thick = groups, width, thick
        self.spot, self.layer = lax.axis_index("space"), lax.axis_index("proj")
        core = lax.rem(self.spot, 2)
        self.shape = (width, thick)
        self.lane = lanes_of(self.shape)
        row = lax.broadcasted_iota(jnp.int32, self.shape, 0)
        self.first, self.last = row == 0, row == width - 1
        self.at_left, self.at_right = self.lane == 0, self.lane == thick - 1
        self.where = self.lane // GROUP
        self.slot = lax.rem(self.lane, GROUP)
        self.lower = self.slot < HALF
        self.near_real = jnp.where(jnp.where(core == 0, self.spot > 0, self.spot < size - 1), 1.0, 0.0)
        self.inner_real = jnp.where(jnp.where(core == 0, self.spot < size - 2, self.spot > 1), 1.0, 0.0)
        self.real = [self.near_real] * 4 + [1.0] * 4 + [self.inner_real] * 2
        self.has_left = jnp.where(self.layer > 0, 1.0, 0.0)
        self.has_right = jnp.where(self.layer < groups - 1, 1.0, 0.0)
        self.n_strips = 1 if groups == 2 else 2
        self.is_right = self.layer == 0

    def real_at(self, places):
        return jnp.where(places < 4, self.near_real, jnp.where(places < 8, 1.0, self.inner_real))

    def strips(self, inside, outside):
        right = jnp.where(self.lower, inside, outside[-1])
        left = jnp.where(self.lower, outside[0], inside)
        return [jnp.where(self.is_right, right, left)] if self.n_strips == 1 else [left, right]

    def strip_z(self):
        left, right = (self.layer * self.thick + self.slot + shift for shift in (-HALF, self.thick - HALF))
        return [jnp.where(self.is_right, right, left)] if self.n_strips == 1 else [left, right]

    def sides(self):
        if self.n_strips == 1:
            return [(self.is_right, 1.0)]
        return [(False, self.has_left), (True, self.has_right)]

    def held(self, is_right):
        right, left = self.lane >= self.thick - HALF, self.lane < HALF
        if isinstance(is_right, bool):
            return right if is_right else left
        return jnp.where(is_right, self.lane, self.thick - 1 - self.lane) >= self.thick - HALF


def by_side(is_right, left, right):
    if isinstance(is_right, bool):
        return right if is_right else left
    return jnp.where(is_right, right, left)


def shifted(array, is_right, left, right):
    size = array.shape[1]
    return pltpu.roll(array, by_side(is_right, left % size, right % size), 1)


def of_strip(strip, is_right, place):
    start = (place - 1) * WIDE
    return shifted(strip, is_right, -(start + HALF), -(start + WIDE - HALF))


def count_terms(count_y, count_z):
    two, three = RMIN - math.sqrt(2.0), RMIN - math.sqrt(3.0)
    head = 2.0 + (count_y + count_z) + two * (count_y * count_z)
    side = 1.0 + two * (count_y + count_z) + three * (count_y * count_z)
    return head, side


def weights_of(at, packed, others, g):
    eta, weight = packed[0:1], packed[1:2]
    for k, other in enumerate(others):
        mine = lax.rem(at.layer + k + 1, at.groups) == g
        eta = jnp.where(mine, other[0:1], eta)
        weight = jnp.where(mine, other[1:2], weight)
    return eta, weight


def projection(eta):
    low = jnp.tanh(BETA * eta)
    over_bottom = 1.0 / (low + jnp.tanh(BETA * (1.0 - eta)))

    def stiffness(density, present):
        inner_part = jnp.tanh(BETA * (density - eta))
        value = (low + inner_part) * over_bottom
        return inner_part, value, (EMIN + (1.0 - EMIN) * (value * value * value)) * present

    def factor(inner_part, value, weight):
        slope = (BETA * over_bottom) * (1.0 - inner_part * inner_part)
        return (-0.5 * 3.0 * (1.0 - EMIN)) * weight * (value * value) * slope

    return stiffness, factor


def border(ref, width):
    ref[:, 0:8] = jnp.zeros((ref.shape[0], 8, ref.shape[2]), jnp.float32)
    ref[:, 8 + width :] = jnp.zeros((ref.shape[0], 8, ref.shape[2]), jnp.float32)


def to_left(at, plane):
    return jnp.where(at.at_left, 0.0, turn(plane, 1, 1))


def to_right(at, plane):
    return jnp.where(at.at_right, 0.0, turn(plane, -1, 1))


def own_columns(is_right, plane, place):
    start = (place - 1) * WIDE
    return shifted(plane, is_right, start + HALF, start + WIDE - HALF)


def density_kernel(groups, size, *refs):
    own, near, inner, scalars = refs[:4]
    others = refs[4 : len(refs) - 6]
    stiff_out, links_out, factor_out, wide_out, f_rows, s_rows = refs[len(refs) - 6 :]
    width, thick = near.shape[0] // 4, near.shape[1]
    at = Spot(groups, size, width, thick)
    two, three = RMIN - math.sqrt(2.0), RMIN - math.sqrt(3.0)
    planes = frame_of(own, near, inner)
    for ref in (f_rows, s_rows):
        border(ref, width)
    for place in range(PLACES):
        f_rows[place, 8 : 8 + width] = planes[place]

    count_y = jnp.where(at.first, 0.0, 1.0) + jnp.where(at.last, 0.0, 1.0)
    places_z = at.layer * thick + at.lane
    count_z = jnp.where(places_z >= 1, 1.0, 0.0) + jnp.where(places_z < groups * thick - 1, 1.0, 0.0)
    head, side = count_terms(count_y, count_z)
    over_two, over_one = 1.0 / (head + 2.0 * side), 1.0 / (head + side)
    straight, once, twice = [], [], []
    for place in range(PLACES):
        plane = planes[place]
        by_y = f_rows[place, 7 : 7 + width] + f_rows[place, 9 : 9 + width]
        straight.append(2.0 * plane + by_y)
        once.append(plane + two * by_y)
        twice.append(two * plane + three * by_y)
    filtered = {}
    for place in range(1, PLACES - 1):
        beside = once[place] + (twice[place - 1] + twice[place + 1])
        total = straight[place] + (once[place - 1] + once[place + 1]) + (to_left(at, beside) + to_right(at, beside))
        count_x = at.real[place - 1] + at.real[place + 1]
        filtered[place] = total * jnp.where(count_x > 1.5, over_two, over_one)

    block = at.lane // WIDE
    for k, (is_right, _) in enumerate(at.sides()):
        strip = jnp.zeros(at.shape, jnp.float32)
        for place in range(1, PLACES - 1):
            strip = jnp.where(block == place - 1, own_columns(is_right, filtered[place], place), strip)
        wide_out[k] = strip

    for g in range(groups):
        eta, weight = weights_of(at, scalars, others, g)
        stiffness, factor = projection(eta)
        stiff = {}
        for place in range(1, PLACES - 1):
            inner_part, value, stiff[place] = stiffness(filtered[place], at.real[place])
            if place in (4, 5):
                factor_out[g, place - 4] = factor(inner_part, value, weight)
            if 2 <= place < 8:
                s_rows[place - 2, 8 : 8 + width] = stiff[place]
                stiff_out[g, place - 2] = stiff[place]
        for place in range(2, 8):
            s = stiff[place]
            by_y = s_rows[place - 2, 7 : 7 + width] + s_rows[place - 2, 9 : 9 + width]
            by_z = to_left(at, s) + to_right(at, s)
            links_out[g, place - 2] = 3.0 * s + 0.5 * ((stiff[place - 1] + stiff[place + 1]) + by_z + by_y)


def inner_kernel(groups, size, *refs):
    stiff_in, links_in, own_masks, partner_masks, near_masks = refs[:5]
    totals_out, z_out, w_out, masks_out, s_rows, z_rows, w_rows = refs[5:]
    width, thick = stiff_in.shape[2:]
    at = Spot(groups, size, width, thick)
    for ref in (s_rows, z_rows, w_rows):
        border(ref, width)

    block, slot = at.lane // WIDE, lax.rem(at.lane, WIDE)

    def mask_planes(which):
        order = ((near_masks, 1), (near_masks, 0), (own_masks, 0), (own_masks, 1), (partner_masks, 1), (partner_masks, 0))
        return {place + 2: plane_of(ref, 2 * which + k, width) for place, (ref, k) in enumerate(order)}

    load, support = mask_planes(0), mask_planes(1)
    mine, theirs, nears = (spread(ref[4 * width :]) for ref in (own_masks, partner_masks, near_masks))
    sources = ((nears, 1), (nears, 0), (mine, 0), (mine, 1), (theirs, 1), (theirs, 0))
    for k, (is_right, _) in enumerate(at.sides()):
        beyond = by_side(is_right, slot, WIDE - 1 - slot) < HALF
        for which, mask in enumerate((load, support)):
            strip = jnp.zeros(at.shape, jnp.float32)
            for place, (source, held) in zip(range(2, 8), sources):
                start = (place - 1) * WIDE - (held + 2 * which) * GROUP
                outer = shifted(source, is_right, start, start + WIDE - GROUP)
                value = jnp.where(beyond, outer, own_columns(is_right, mask[place], place))
                strip = jnp.where(block == place - 1, value, strip)
            masks_out[which, k] = strip

    counted = jnp.ones(at.shape, jnp.float32)
    for is_right, present in at.sides():
        counted = jnp.where(at.held(is_right), 1.0 - present, counted)

    rows_out = 0
    for g in range(groups):
        stiff = {place: stiff_in[g, place - 2] for place in range(2, 8)}
        over, z, k_right = {}, {}, {}
        for place in range(2, 8):
            over[place] = at.real[place] / jnp.maximum(links_in[g, place - 2] + PENALTY * support[place], 0.1)
            z[place] = load[place] * over[place]
        for place in range(3, 7):
            s_rows[place - 3, 8 : 8 + width] = stiff[place]
            k_right[place] = stiff[place] + to_right(at, stiff[place])

        def image(field, rows, start, place, flow_before, flow_after):
            v, s = field[place], stiff[place]
            flow_z = k_right[place] * (v - to_right(at, v))
            total = (flow_after - flow_before) + (flow_z - jnp.where(at.at_left, -(s * v), turn(flow_z, 1, 1)))
            s_up, s_down = s_rows[place - 3, 7 : 7 + width], s_rows[place - 3, 9 : 9 + width]
            v_up, v_down = rows[place - start, 7 : 7 + width], rows[place - start, 9 : 9 + width]
            return total + ((s + s_up) * (v - v_up) + (s + s_down) * (v - v_down))

        def flow_x(field, place):
            return (stiff[place] + stiff[place + 1]) * (field[place] - field[place + 1])

        for place in range(3, 7):
            z_rows[place - 3, 8 : 8 + width] = z[place]
            z_out[g, place - 3] = z[place]
        flows = {place: flow_x(z, place) for place in range(2, 7)}
        q, w = {}, {}
        for place in range(3, 7):
            q[place] = 0.5 * image(z, z_rows, 3, place, flows[place - 1], flows[place])
            w[place] = q[place] * over[place]
            w_out[g, place - 3] = w[place]
        for place in (4, 5):
            w_rows[place - 4, 8 : 8 + width] = w[place]
        flows = {place: flow_x(w, place) for place in range(3, 6)}
        totals = [0.0, 0.0, 0.0, 0.0]
        for place in (4, 5):
            aw = 0.5 * image(w, w_rows, 4, place, flows[place - 1], flows[place])
            terms = (z[place], z[place] * q[place], q[place] * w[place], w[place] * aw)
            totals = [a + b for a, b in zip(totals, terms)]
        for total in totals:
            totals_out[rows_out : rows_out + 1] = jnp.sum(total * counted, axis=0, keepdims=True)
            rows_out += 1


def edge_kernel(groups, size, *refs):
    n_side = 1 if groups == 2 else 2
    inside, wide, masks, totals, factors, scalars = refs[:6]
    beside, others = refs[6 : 6 + n_side], refs[6 + n_side : len(refs) - 3]
    table, strip_out, factor_out = refs[len(refs) - 3 :]
    width, thick = inside.shape
    at = Spot(groups, size, width, thick)
    first, last = at.first, at.last
    two, three = RMIN - math.sqrt(2.0), RMIN - math.sqrt(3.0)

    outside = [unfold(ref[...], at.layer == 1 if groups == 2 else k == 0) for k, ref in enumerate(beside)]
    outside = [jnp.where(at.where < PLACES, v, 0.0) for v in outside]
    outside = [outside[0] * at.has_left, outside[-1] * at.has_right]
    fixed = at.strips(inside[...], outside)

    count_y = jnp.where(first, 0.0, 1.0) + jnp.where(last, 0.0, 1.0)
    count_x = at.real_at(at.where - 1) + at.real_at(at.where + 1)
    span_z = thick * groups
    block, slot = at.lane // WIDE, lax.rem(at.lane, WIDE)
    filtered, presents, counts = [], [], []
    for k, (strip, z_at, (is_right, present)) in enumerate(zip(fixed, at.strip_z(), at.sides())):
        by_y = around_y(strip, first, last)
        once = strip + two * by_y
        across = once + turn(two * strip + three * by_y, GROUP, 1) + turn(two * strip + three * by_y, -GROUP, 1)
        total = 2.0 * strip + by_y + turn(once, GROUP, 1) + turn(once, -GROUP, 1)
        total = total + turn(across, 1, 1) + turn(across, -1, 1)
        count_z = jnp.where(z_at >= 1, 1.0, 0.0) + jnp.where(z_at < span_z - 1, 1.0, 0.0)
        head, side = count_terms(count_y, count_z)
        total = total / (head + count_x * side)
        value = wide[k]
        better = by_side(is_right, slot, WIDE - 1 - slot) <= HALF
        for place in range(1, PLACES - 1):
            start = (place - 1) * WIDE - place * GROUP
            moved = shifted(total, is_right, start, start + WIDE - GROUP)
            value = jnp.where(better & (block == place - 1), moved, value)
        filtered.append(value)
        z_wide = at.layer * thick + slot + by_side(is_right, -HALF, thick - WIDE + HALF)
        presents.append(jnp.where((z_wide >= 0) & (z_wide < span_z), at.real_at(block + 1), 0.0))
        own = by_side(is_right, slot, WIDE - 1 - slot)
        own = (own >= HALF) & (own < 2 * HALF) & (block >= 3) & (block < 5)
        counts.append(jnp.where(own, present, 0.0))

    lane_row = lanes_of((1, thick))
    line = jnp.zeros((1, thick), jnp.float32)
    for g in range(groups):
        eta, weight = weights_of(at, scalars, others, g)
        stiffness, factor = projection(eta)
        sums = [totals[4 * g + k : 4 * g + k + 1] for k in range(4)]
        patched = [factors[g, 0], factors[g, 1]]
        for k, (is_right, present) in enumerate(at.sides()):
            inner_part, value, s = stiffness(filtered[k], presents[k])
            of_place = factor(inner_part, value, weight)
            for place in (0, 1):
                here = at.held(is_right) & (present > 0.5)
                patched[place] = jnp.where(here, of_strip(of_place, is_right, place + 4), patched[place])
            s_next, s_right = turn(s, -WIDE, 1), turn(s, -1, 1)
            s_up, s_down = jnp.where(first, 0.0, turn(s, 1, 0)), jnp.where(last, 0.0, turn(s, -1, 0))
            links = 6.0 * s + (s_next + turn(s, WIDE, 1)) + (s_right + turn(s, 1, 1)) + (s_up + s_down)
            inverse = presents[k] / jnp.maximum(0.5 * links + PENALTY * masks[1, k], 0.1)

            def image(v):
                flow_x = (s + s_next) * (v - turn(v, -WIDE, 1))
                flow_z = (s + s_right) * (v - turn(v, -1, 1))
                v_up, v_down = jnp.where(first, 0.0, turn(v, 1, 0)), jnp.where(last, 0.0, turn(v, -1, 0))
                total = (flow_x - turn(flow_x, WIDE, 1)) + (flow_z - turn(flow_z, 1, 1))
                return 0.5 * (total + ((s + s_up) * (v - v_up) + (s + s_down) * (v - v_down)))

            z = masks[0, k] * inverse
            q = image(z)
            w = q * inverse
            strip_out[g, 0, k] = z
            strip_out[g, 1, k] = w
            terms = (z, z * q, q * w, w * image(w))
            sums = [a + jnp.sum(b * counts[k], axis=0, keepdims=True) for a, b in zip(sums, terms)]
        for place in (0, 1):
            factor_out[g, place] = patched[place]
        for k, part in enumerate(sums):
            line = jnp.where(lane_row == 4 * g + k, jnp.sum(part, axis=1, keepdims=True), line)
    table[...] = jnp.broadcast_to(line, table.shape)


def finish(groups, size, table, z_in, w_in, strips, factors, out):
    width, thick = out.shape[1:]
    at = Spot(groups, size, width, thick)
    core = lax.rem(at.spot, 2)
    line = jnp.sum(table[...], axis=0, keepdims=True)
    lane_row = lanes_of((1, thick))
    total = [jnp.zeros(at.shape, jnp.float32), jnp.zeros(at.shape, jnp.float32)]
    for g in range(groups):
        m0, m1, m2, m3 = (
            jnp.sum(jnp.where(lane_row == 4 * g + k, line, 0.0), axis=1, keepdims=True) for k in range(4)
        )
        step_one = m0 / m1
        rz_next = step_one * step_one * m2 - m0
        factor = rz_next / m0
        curve = (m1 - 2.0 * step_one * m2 + step_one * step_one * m3) - factor * factor * m1
        step_two = rz_next / curve
        of_z = step_one + step_two * (1.0 + factor)
        of_w = -step_one * step_two
        u = [of_z * z_in[g, k] + of_w * w_in[g, k] for k in range(4)]
        ends = {1: [0.0, 0.0], 2: [0.0, 0.0]}
        for k, (is_right, present) in enumerate(at.sides()):
            strip = of_z * strips[g, 0, k] + of_w * strips[g, 1, k]
            here = at.held(is_right) & (present > 0.5)
            for place in range(4):
                part = of_strip(strip, is_right, place + 3)
                u[place] = jnp.where(here, part, u[place])
                if place in ends:
                    if at.n_strips == 1:
                        ends[place] = [part * at.has_left, part * at.has_right]
                    else:
                        ends[place][k] = part * present
        between = [u[k] - u[k + 1] for k in range(3)]
        for k in (1, 2):
            plane = u[k]
            left = turn(jnp.where(at.at_right, ends[k][0], plane), 1, 1)
            right = turn(jnp.where(at.at_left, ends[k][1], plane), -1, 1)
            up = jnp.where(at.first, 0.0, turn(plane, 1, 0))
            down = jnp.where(at.last, 0.0, turn(plane, -1, 0))
            steps = [between[k - 1], between[k]] + [plane - other for other in (left, right, up, down)]
            squares = [v * v for v in steps]
            total[k - 1] = total[k - 1] + factors[g, k - 1] * sum(squares[1:], squares[0])
    for k in range(2):
        out[lax.rem(k + core, 2)] = total[k]


def call(body, outs, *args, scalars=(), scratch=(), flops=0):
    smem = pl.BlockSpec(memory_space=pltpu.SMEM)
    return pl.pallas_call(
        body,
        out_shape=[jax.ShapeDtypeStruct(shape, jnp.float32) for shape in outs],
        in_specs=[pl.BlockSpec(memory_space=pltpu.VMEM)] * len(args) + [smem] * len(scalars),
        out_specs=[pl.BlockSpec(memory_space=pltpu.VMEM)] * len(outs),
        scratch_shapes=[pltpu.VMEM(shape, jnp.float32) for shape in scratch],
        cost_estimate=pl.CostEstimate(flops=flops, transcendentals=0, bytes_accessed=0) if flops else None,
        compiler_params=pltpu.CompilerParams(vmem_limit_bytes=32 * 1024 * 1024),
    )(*args, *scalars)


def local(design, solid_mask, void_mask, load_mask, support_mask, thresholds, group_weight):
    depth, width, thick = design.shape
    size, groups = lax.axis_size("space"), lax.axis_size("proj")
    quarter = width // 4
    pair, near_pairs = pair_swap(size), near_swap(size)
    fixed = jnp.where(solid_mask == 1, 1.0, jnp.where(void_mask == 1, 0.0, design))
    partner_fixed = lax.ppermute(fixed, "space", pair)
    (own_masks,) = call(
        functools.partial(prepare, groups), [(4 * width + quarter, thick)], load_mask, support_mask
    )
    own, scalars = call(
        order, [(4 * width, thick), (8, thick)], fixed, partner_fixed, scalars=(thresholds, group_weight)
    )
    others = [lax.ppermute(scalars, "proj", [((g + k) % groups, g) for g in range(groups)]) for k in range(1, groups)]
    partner_masks = lax.ppermute(own_masks, "space", pair)
    near = lax.ppermute(own, "space", near_pairs)
    near_masks = lax.ppermute(own_masks, "space", near_pairs)
    (beyond,) = call(pick, [(2 * width, thick)], near)
    inner = lax.ppermute(beyond, "space", pair)
    steps = (1,) if groups == 2 else (1, -1)
    inside, *packed = call(
        functools.partial(pack, groups),
        [(width, thick)] + [(width // 2, thick)] * len(steps),
        own, near, inner,
    )
    beside = [
        lax.ppermute(part, "proj", [(g, (g + s) % groups) for g in range(groups) if groups == 2 or 0 <= g + s < groups])
        for s, part in zip(steps, packed)
    ]
    others = [call(keep, [other.shape], other, flops=500_000_000)[0] for other in others]
    n_strips = 1 if groups == 2 else 2
    plane = (width, thick)
    six = (groups, 6, *plane)
    stiff, links, factors, wide = call(
        functools.partial(density_kernel, groups, size),
        [six, six, (groups, 2, *plane), (n_strips, *plane)],
        own, near, inner, scalars, *others,
        scratch=[(PLACES, width + 16, thick), (6, width + 16, thick)],
    )
    totals, z, w, mask_strips = call(
        functools.partial(inner_kernel, groups, size),
        [(-(-4 * groups // 8) * 8, thick), (groups, 4, *plane), (groups, 4, *plane), (2, n_strips, *plane)],
        stiff, links, own_masks, partner_masks, near_masks,
        scratch=[(4, width + 16, thick), (4, width + 16, thick), (2, width + 16, thick)],
    )
    table, strips, factors = call(
        functools.partial(edge_kernel, groups, size),
        [(size * groups, thick), (groups, 2, n_strips, *plane), (groups, 2, *plane)],
        inside, wide, mask_strips, totals, factors, scalars, *beside, *others,
    )
    table = lax.all_to_all(table, ("proj", "space"), 0, 0, tiled=True)
    (out,) = call(functools.partial(finish, groups, size), [(depth, *plane)], table, z, w, strips, factors)
    return out


def solution(mesh):
    placed = (
        P("space", None, "proj"),
        P("space", None, "proj"),
        P("space", None, "proj"),
        P("space", None, None),
        P("space", None, None),
        P("proj"),
        P("proj"),
    )
    return jax.shard_map(
        local, mesh=mesh, in_specs=placed, out_specs=P("space", None, "proj"), check_vma=False
    )
```

```python
import functools
import math

import jax
import jax.numpy as jnp
from jax import lax
from jax.experimental import pallas as pl
from jax.experimental.pallas import tpu as pltpu
from jax.sharding import PartitionSpec as P

RMIN = 2.0
BETA = 8.0
EMIN = 0.05
PENALTY = 4.0

PLACES = 10
GROUP = 8
HALF = GROUP // 2
WIDE = 2 * GROUP
INNER = PLACES - 2


def pair_swap(size):
    return [(i, i ^ 1) for i in range(size)]


def near_swap(size):
    ups = [(i, i + 1) for i in range(1, size - 1, 2)]
    return ups + [(j, i) for i, j in ups]


def both_axes(pairs, size, groups, step):
    return [
        (g * size + i, (g + step) % groups * size + j)
        for g in range(groups)
        for i, j in pairs
        if groups == 2 or 0 <= g + step < groups
    ]


def lanes_of(shape):
    return lax.broadcasted_iota(jnp.int32, shape, len(shape) - 1)


def turn(array, shift, axis):
    return pltpu.roll(array, shift % array.shape[axis], axis)


def squeeze(strips):
    rows, lanes = strips.shape[0] // 4, strips.shape[1]
    parts = [turn(strips[k * rows : (k + 1) * rows], k * lanes // 4, 1) for k in range(4)]
    block = lanes_of((rows, lanes)) // (lanes // 4)
    return functools.reduce(lambda out, k: jnp.where(block == k, parts[k], out), range(1, 4), parts[0])


def spread(squeezed):
    lanes = squeezed.shape[1]
    return jnp.concatenate([turn(squeezed, -k * lanes // 4, 1) for k in range(4)], axis=0)


def prepare(groups, fixed, load, support, out):
    core = lax.rem(lax.axis_index("space"), 2)
    layer = lax.axis_index("proj")
    width, thick = load.shape[1], load.shape[2] // groups
    lane = lanes_of((width, thick))
    lower = lax.rem(lane, GROUP) < HALF
    has_left = layer > 0
    has_right = layer < groups - 1
    centre = pl.ds(pl.multiple_of(layer * thick, thick), thick)
    left = pl.ds(pl.multiple_of(jnp.maximum(layer - 1, 0) * thick, thick), thick)
    right = pl.ds(pl.multiple_of(jnp.minimum(layer + 1, groups - 1) * thick, thick), thick)
    strips = jnp.zeros((width, thick), jnp.float32)
    for place in range(2):
        plane = lax.rem(place + core, 2)
        out[place * width : (place + 1) * width] = fixed[plane]
        for which, mask in enumerate((load, support)):
            held = 2 * which + place
            out[(2 + held) * width : (3 + held) * width] = mask[plane, :, centre].astype(jnp.float32)
            before = jnp.where(has_left, mask[plane, :, left].astype(jnp.float32), 0.0)
            after = jnp.where(has_right, mask[plane, :, right].astype(jnp.float32), 0.0)
            shift = held * GROUP + HALF
            outside = jnp.where(lower, turn(before, shift, 1), turn(after, shift, 1))
            strips = jnp.where(lane // GROUP == held, outside, strips)
    out[6 * width :] = squeeze(strips)


def join(own, partner, thresholds, weights, near_out, mask_out, scalars):
    rows = near_out.shape[0] // 2
    near_out[0:rows] = own[0:rows]
    near_out[rows:] = partner[0:rows]
    mask_out[...] = own[rows:]
    row = lax.broadcasted_iota(jnp.int32, scalars.shape, 0)
    scalars[...] = jnp.where(row == 0, thresholds[0].astype(jnp.float32) / 1000.0, jnp.where(row == 1, weights[0], 0.0))


def keep(array, *refs):
    refs[-1][...] = array[...]


def pick(near, *refs):
    out = refs[-1]
    out[...] = near[0 : out.shape[0]]


def plane_of(ref, k, width):
    return ref[k * width : (k + 1) * width]


def frame_of(own, near):
    order = ((near, 2), (near, 3), (near, 1), (near, 0), (own, 0), (own, 1), (own, 3), (own, 2))
    return [plane_of(ref, k, near.shape[0] // 4) for ref, k in order]


def fold(strips, lower):
    half = strips.shape[0] // 2
    low = lax.rem(lanes_of((half, strips.shape[1])), GROUP) < HALF
    top, bottom = strips[:half], strips[half:]
    folded_low = jnp.where(low, top, turn(bottom, HALF, 1))
    folded_high = jnp.where(low, turn(bottom, -HALF, 1), top)
    return jnp.where(lower, folded_low, folded_high)


def unfold(folded, lower):
    return jnp.concatenate([folded, jnp.where(lower, turn(folded, -HALF, 1), turn(folded, HALF, 1))], axis=0)


def pack(groups, own, near, inside, *outs):
    width, thick = inside.shape
    lane = lanes_of((width, thick))
    strips = jnp.zeros((width, thick), jnp.float32)
    for place, plane in enumerate(frame_of(own, near)):
        strips = jnp.where(lane // GROUP == place, turn(plane, place * GROUP + HALF, 1), strips)
    inside[...] = strips
    sides = (lax.axis_index("proj") == 0,) if groups == 2 else (True, False)
    for k, lower in enumerate(sides):
        outs[k][...] = fold(strips, lower)
        outs[len(sides) + k][...] = squeeze(fold(turn(strips, -2 * GROUP, 1), lower))


def around_y(plane, first, last):
    return jnp.where(first, 0.0, turn(plane, 1, 0)) + jnp.where(last, 0.0, turn(plane, -1, 0))


class Spot:
    def __init__(self, groups, size, width, thick):
        self.groups, self.width, self.thick = groups, width, thick
        self.spot, self.layer = lax.axis_index("space"), lax.axis_index("proj")
        core = lax.rem(self.spot, 2)
        self.shape = (width, thick)
        self.lane = lanes_of(self.shape)
        row = lax.broadcasted_iota(jnp.int32, self.shape, 0)
        self.first, self.last = row == 0, row == width - 1
        self.at_left, self.at_right = self.lane == 0, self.lane == thick - 1
        self.where = self.lane // GROUP
        self.slot = lax.rem(self.lane, GROUP)
        self.lower = self.slot < HALF
        self.near_real = jnp.where(jnp.where(core == 0, self.spot > 0, self.spot < size - 1), 1.0, 0.0)
        self.inner_real = jnp.where(jnp.where(core == 0, self.spot < size - 2, self.spot > 1), 1.0, 0.0)
        self.real = [self.near_real] * 4 + [1.0] * 4 + [self.inner_real] * 2
        self.has_left = jnp.where(self.layer > 0, 1.0, 0.0)
        self.has_right = jnp.where(self.layer < groups - 1, 1.0, 0.0)
        self.n_strips = 1 if groups == 2 else 2
        self.is_right = self.layer == 0

    def real_at(self, places):
        return jnp.where(places < 4, self.near_real, jnp.where(places < 8, 1.0, self.inner_real))

    def strips(self, inside, outside):
        right = jnp.where(self.lower, inside, outside[-1])
        left = jnp.where(self.lower, outside[0], inside)
        return [jnp.where(self.is_right, right, left)] if self.n_strips == 1 else [left, right]

    def strip_z(self):
        left, right = (self.layer * self.thick + self.slot + shift for shift in (-HALF, self.thick - HALF))
        return [jnp.where(self.is_right, right, left)] if self.n_strips == 1 else [left, right]

    def sides(self):
        if self.n_strips == 1:
            return [(self.is_right, 1.0)]
        return [(False, self.has_left), (True, self.has_right)]

    def held(self, is_right):
        right, left = self.lane >= self.thick - HALF, self.lane < HALF
        if isinstance(is_right, bool):
            return right if is_right else left
        return jnp.where(is_right, self.lane, self.thick - 1 - self.lane) >= self.thick - HALF


def by_side(is_right, left, right):
    if isinstance(is_right, bool):
        return right if is_right else left
    return jnp.where(is_right, right, left)


def shifted(array, is_right, left, right):
    size = array.shape[1]
    return pltpu.roll(array, by_side(is_right, left % size, right % size), 1)


def of_strip(strip, is_right, place):
    start = (place - 1) * WIDE
    return shifted(strip, is_right, -(start + HALF), -(start + WIDE - HALF))


def count_terms(count_y, count_z):
    two, three = RMIN - math.sqrt(2.0), RMIN - math.sqrt(3.0)
    head = 2.0 + (count_y + count_z) + two * (count_y * count_z)
    side = 1.0 + two * (count_y + count_z) + three * (count_y * count_z)
    return head, side


def weights_of(at, packed, others, g):
    eta, weight = packed[0:1], packed[1:2]
    for k, other in enumerate(others):
        mine = lax.rem(at.layer + k + 1, at.groups) == g
        eta = jnp.where(mine, other[0:1], eta)
        weight = jnp.where(mine, other[1:2], weight)
    return eta, weight


def projection(eta):
    low = jnp.tanh(BETA * eta)
    over_bottom = 1.0 / (low + jnp.tanh(BETA * (1.0 - eta)))

    def stiffness(density, present):
        inner_part = jnp.tanh(BETA * (density - eta))
        value = (low + inner_part) * over_bottom
        return inner_part, value, (EMIN + (1.0 - EMIN) * (value * value * value)) * present

    def factor(inner_part, value, weight):
        slope = (BETA * over_bottom) * (1.0 - inner_part * inner_part)
        return (-0.5 * 3.0 * (1.0 - EMIN)) * weight * (value * value) * slope

    return stiffness, factor


def border(ref, width):
    ref[:, 0:8] = jnp.zeros((ref.shape[0], 8, ref.shape[2]), jnp.float32)
    ref[:, 8 + width :] = jnp.zeros((ref.shape[0], 8, ref.shape[2]), jnp.float32)


def to_left(at, plane):
    return jnp.where(at.at_left, 0.0, turn(plane, 1, 1))


def to_right(at, plane):
    return jnp.where(at.at_right, 0.0, turn(plane, -1, 1))


def own_columns(is_right, plane, place):
    start = (place - 1) * WIDE
    return shifted(plane, is_right, start + HALF, start + WIDE - HALF)


def density_kernel(groups, size, *refs):
    own, near, inner, inside, scalars = refs[:5]
    others = refs[5 : len(refs) - 7]
    stiff_out, links_out, factor_out, wide_out, inside_out, f_rows, s_rows = refs[len(refs) - 7 :]
    width, thick = near.shape[0] // 4, near.shape[1]
    at = Spot(groups, size, width, thick)
    two, three = RMIN - math.sqrt(2.0), RMIN - math.sqrt(3.0)
    planes = frame_of(own, near) + [plane_of(inner, k, width) for k in (0, 1)]
    strip = inside[...]
    for place in (8, 9):
        strip = jnp.where(at.where == place, turn(planes[place], place * GROUP + HALF, 1), strip)
    inside_out[...] = strip
    for ref in (f_rows, s_rows):
        border(ref, width)
    for place in range(PLACES):
        f_rows[place, 8 : 8 + width] = planes[place]

    count_y = jnp.where(at.first, 0.0, 1.0) + jnp.where(at.last, 0.0, 1.0)
    places_z = at.layer * thick + at.lane
    count_z = jnp.where(places_z >= 1, 1.0, 0.0) + jnp.where(places_z < groups * thick - 1, 1.0, 0.0)
    head, side = count_terms(count_y, count_z)
    over_two, over_one = 1.0 / (head + 2.0 * side), 1.0 / (head + side)
    straight, once, twice = [], [], []
    for place in range(PLACES):
        plane = planes[place]
        by_y = f_rows[place, 7 : 7 + width] + f_rows[place, 9 : 9 + width]
        straight.append(2.0 * plane + by_y)
        once.append(plane + two * by_y)
        twice.append(two * plane + three * by_y)
    filtered = {}
    for place in range(1, PLACES - 1):
        beside = once[place] + (twice[place - 1] + twice[place + 1])
        total = straight[place] + (once[place - 1] + once[place + 1]) + (to_left(at, beside) + to_right(at, beside))
        count_x = at.real[place - 1] + at.real[place + 1]
        filtered[place] = total * jnp.where(count_x > 1.5, over_two, over_one)

    block = at.lane // WIDE
    for k, (is_right, _) in enumerate(at.sides()):
        strip = jnp.zeros(at.shape, jnp.float32)
        for place in range(1, PLACES - 1):
            strip = jnp.where(block == place - 1, own_columns(is_right, filtered[place], place), strip)
        wide_out[k] = strip

    for g in range(groups):
        eta, weight = weights_of(at, scalars, others, g)
        stiffness, factor = projection(eta)
        stiff = {}
        for place in range(1, PLACES - 1):
            inner_part, value, stiff[place] = stiffness(filtered[place], at.real[place])
            if place in (4, 5):
                factor_out[g, place - 4] = factor(inner_part, value, weight)
            if 2 <= place < 8:
                s_rows[place - 2, 8 : 8 + width] = stiff[place]
                stiff_out[g, place - 2] = stiff[place]
        for place in range(2, 8):
            s = stiff[place]
            by_y = s_rows[place - 2, 7 : 7 + width] + s_rows[place - 2, 9 : 9 + width]
            by_z = to_left(at, s) + to_right(at, s)
            links_out[g, place - 2] = 3.0 * s + 0.5 * ((stiff[place - 1] + stiff[place + 1]) + by_z + by_y)


def inner_kernel(groups, size, *refs):
    stiff_in, links_in, own_masks, partner, near_masks = refs[:5]
    totals_out, z_out, w_out, masks_out, s_rows, z_rows, w_rows = refs[5:]
    width, thick = stiff_in.shape[2:]
    partner_masks = partner.at[2 * width :]
    at = Spot(groups, size, width, thick)
    for ref in (s_rows, z_rows, w_rows):
        border(ref, width)

    block, slot = at.lane // WIDE, lax.rem(at.lane, WIDE)

    def mask_planes(which):
        order = ((near_masks, 1), (near_masks, 0), (own_masks, 0), (own_masks, 1), (partner_masks, 1), (partner_masks, 0))
        return {place + 2: plane_of(ref, 2 * which + k, width) for place, (ref, k) in enumerate(order)}

    load, support = mask_planes(0), mask_planes(1)
    mine, theirs, nears = (spread(ref[4 * width :]) for ref in (own_masks, partner_masks, near_masks))
    sources = ((nears, 1), (nears, 0), (mine, 0), (mine, 1), (theirs, 1), (theirs, 0))
    for k, (is_right, _) in enumerate(at.sides()):
        beyond = by_side(is_right, slot, WIDE - 1 - slot) < HALF
        for which, mask in enumerate((load, support)):
            strip = jnp.zeros(at.shape, jnp.float32)
            for place, (source, held) in zip(range(2, 8), sources):
                start = (place - 1) * WIDE - (held + 2 * which) * GROUP
                outer = shifted(source, is_right, start, start + WIDE - GROUP)
                value = jnp.where(beyond, outer, own_columns(is_right, mask[place], place))
                strip = jnp.where(block == place - 1, value, strip)
            masks_out[which, k] = strip

    counted = jnp.ones(at.shape, jnp.float32)
    for is_right, present in at.sides():
        counted = jnp.where(at.held(is_right), 1.0 - present, counted)

    rows_out = 0
    for g in range(groups):
        stiff = {place: stiff_in[g, place - 2] for place in range(2, 8)}
        over, z, k_right = {}, {}, {}
        for place in range(2, 8):
            over[place] = at.real[place] / jnp.maximum(links_in[g, place - 2] + PENALTY * support[place], 0.1)
            z[place] = load[place] * over[place]
        for place in range(3, 7):
            s_rows[place - 3, 8 : 8 + width] = stiff[place]
            k_right[place] = stiff[place] + to_right(at, stiff[place])

        def image(field, rows, start, place, flow_before, flow_after):
            v, s = field[place], stiff[place]
            flow_z = k_right[place] * (v - to_right(at, v))
            total = (flow_after - flow_before) + (flow_z - jnp.where(at.at_left, -(s * v), turn(flow_z, 1, 1)))
            s_up, s_down = s_rows[place - 3, 7 : 7 + width], s_rows[place - 3, 9 : 9 + width]
            v_up, v_down = rows[place - start, 7 : 7 + width], rows[place - start, 9 : 9 + width]
            return total + ((s + s_up) * (v - v_up) + (s + s_down) * (v - v_down))

        def flow_x(field, place):
            return (stiff[place] + stiff[place + 1]) * (field[place] - field[place + 1])

        for place in range(3, 7):
            z_rows[place - 3, 8 : 8 + width] = z[place]
            z_out[g, place - 3] = z[place]
        flows = {place: flow_x(z, place) for place in range(2, 7)}
        q, w = {}, {}
        for place in range(3, 7):
            q[place] = 0.5 * image(z, z_rows, 3, place, flows[place - 1], flows[place])
            w[place] = q[place] * over[place]
            w_out[g, place - 3] = w[place]
        for place in (4, 5):
            w_rows[place - 4, 8 : 8 + width] = w[place]
        flows = {place: flow_x(w, place) for place in range(3, 6)}
        totals = [0.0, 0.0, 0.0, 0.0]
        for place in (4, 5):
            aw = 0.5 * image(w, w_rows, 4, place, flows[place - 1], flows[place])
            terms = (z[place], z[place] * q[place], q[place] * w[place], w[place] * aw)
            totals = [a + b for a, b in zip(totals, terms)]
        for total in totals:
            totals_out[rows_out : rows_out + 1] = jnp.sum(total * counted, axis=0, keepdims=True)
            rows_out += 1


def edge_kernel(groups, size, *refs):
    n_side = 1 if groups == 2 else 2
    inside, wide, masks, totals, factors, scalars = refs[:6]
    beside, crossed = refs[6 : 6 + n_side], refs[6 + n_side : 6 + 2 * n_side]
    others = refs[6 + 2 * n_side : len(refs) - 3]
    table, strip_out, factor_out = refs[len(refs) - 3 :]
    width, thick = inside.shape
    at = Spot(groups, size, width, thick)
    first, last = at.first, at.last
    two, three = RMIN - math.sqrt(2.0), RMIN - math.sqrt(3.0)

    outside = []
    for k in range(n_side):
        lower = at.layer == 1 if groups == 2 else k == 0
        strip, back = unfold(beside[k][...], lower), unfold(spread(crossed[k][...]), lower)
        strip = jnp.where(at.where == 8, turn(back, 7 * GROUP, 1), strip)
        strip = jnp.where(at.where == 9, turn(back, 9 * GROUP, 1), strip)
        outside.append(jnp.where(at.where < PLACES, strip, 0.0))
    outside = [outside[0] * at.has_left, outside[-1] * at.has_right]
    fixed = at.strips(inside[...], outside)

    count_y = jnp.where(first, 0.0, 1.0) + jnp.where(last, 0.0, 1.0)
    count_x = at.real_at(at.where - 1) + at.real_at(at.where + 1)
    span_z = thick * groups
    block, slot = at.lane // WIDE, lax.rem(at.lane, WIDE)
    filtered, presents, counts = [], [], []
    for k, (strip, z_at, (is_right, present)) in enumerate(zip(fixed, at.strip_z(), at.sides())):
        by_y = around_y(strip, first, last)
        once = strip + two * by_y
        across = once + turn(two * strip + three * by_y, GROUP, 1) + turn(two * strip + three * by_y, -GROUP, 1)
        total = 2.0 * strip + by_y + turn(once, GROUP, 1) + turn(once, -GROUP, 1)
        total = total + turn(across, 1, 1) + turn(across, -1, 1)
        count_z = jnp.where(z_at >= 1, 1.0, 0.0) + jnp.where(z_at < span_z - 1, 1.0, 0.0)
        head, side = count_terms(count_y, count_z)
        total = total / (head + count_x * side)
        value = wide[k]
        better = by_side(is_right, slot, WIDE - 1 - slot) <= HALF
        for place in range(1, PLACES - 1):
            start = (place - 1) * WIDE - place * GROUP
            moved = shifted(total, is_right, start, start + WIDE - GROUP)
            value = jnp.where(better & (block == place - 1), moved, value)
        filtered.append(value)
        z_wide = at.layer * thick + slot + by_side(is_right, -HALF, thick - WIDE + HALF)
        presents.append(jnp.where((z_wide >= 0) & (z_wide < span_z), at.real_at(block + 1), 0.0))
        own = by_side(is_right, slot, WIDE - 1 - slot)
        own = (own >= HALF) & (own < 2 * HALF) & (block >= 3) & (block < 5)
        counts.append(jnp.where(own, present, 0.0))

    lane_row = lanes_of((1, thick))
    line = jnp.zeros((1, thick), jnp.float32)
    for g in range(groups):
        eta, weight = weights_of(at, scalars, others, g)
        stiffness, factor = projection(eta)
        sums = [totals[4 * g + k : 4 * g + k + 1] for k in range(4)]
        patched = [factors[g, 0], factors[g, 1]]
        for k, (is_right, present) in enumerate(at.sides()):
            inner_part, value, s = stiffness(filtered[k], presents[k])
            of_place = factor(inner_part, value, weight)
            for place in (0, 1):
                here = at.held(is_right) & (present > 0.5)
                patched[place] = jnp.where(here, of_strip(of_place, is_right, place + 4), patched[place])
            s_next, s_right = turn(s, -WIDE, 1), turn(s, -1, 1)
            s_up, s_down = jnp.where(first, 0.0, turn(s, 1, 0)), jnp.where(last, 0.0, turn(s, -1, 0))
            links = 6.0 * s + (s_next + turn(s, WIDE, 1)) + (s_right + turn(s, 1, 1)) + (s_up + s_down)
            inverse = presents[k] / jnp.maximum(0.5 * links + PENALTY * masks[1, k], 0.1)

            def image(v):
                flow_x = (s + s_next) * (v - turn(v, -WIDE, 1))
                flow_z = (s + s_right) * (v - turn(v, -1, 1))
                v_up, v_down = jnp.where(first, 0.0, turn(v, 1, 0)), jnp.where(last, 0.0, turn(v, -1, 0))
                total = (flow_x - turn(flow_x, WIDE, 1)) + (flow_z - turn(flow_z, 1, 1))
                return 0.5 * (total + ((s + s_up) * (v - v_up) + (s + s_down) * (v - v_down)))

            z = masks[0, k] * inverse
            q = image(z)
            w = q * inverse
            strip_out[g, 0, k] = z
            strip_out[g, 1, k] = w
            terms = (z, z * q, q * w, w * image(w))
            sums = [a + jnp.sum(b * counts[k], axis=0, keepdims=True) for a, b in zip(sums, terms)]
        for place in (0, 1):
            factor_out[g, place] = patched[place]
        for k, part in enumerate(sums):
            line = jnp.where(lane_row == 4 * g + k, jnp.sum(part, axis=1, keepdims=True), line)
    table[...] = jnp.broadcast_to(line, table.shape)


def finish(groups, size, table, z_in, w_in, strips, factors, out):
    width, thick = out.shape[1:]
    at = Spot(groups, size, width, thick)
    core = lax.rem(at.spot, 2)
    line = jnp.sum(table[...], axis=0, keepdims=True)
    lane_row = lanes_of((1, thick))
    total = [jnp.zeros(at.shape, jnp.float32), jnp.zeros(at.shape, jnp.float32)]
    for g in range(groups):
        m0, m1, m2, m3 = (
            jnp.sum(jnp.where(lane_row == 4 * g + k, line, 0.0), axis=1, keepdims=True) for k in range(4)
        )
        step_one = m0 / m1
        rz_next = step_one * step_one * m2 - m0
        factor = rz_next / m0
        curve = (m1 - 2.0 * step_one * m2 + step_one * step_one * m3) - factor * factor * m1
        step_two = rz_next / curve
        of_z = step_one + step_two * (1.0 + factor)
        of_w = -step_one * step_two
        u = [of_z * z_in[g, k] + of_w * w_in[g, k] for k in range(4)]
        ends = {1: [0.0, 0.0], 2: [0.0, 0.0]}
        for k, (is_right, present) in enumerate(at.sides()):
            strip = of_z * strips[g, 0, k] + of_w * strips[g, 1, k]
            here = at.held(is_right) & (present > 0.5)
            for place in range(4):
                part = of_strip(strip, is_right, place + 3)
                u[place] = jnp.where(here, part, u[place])
                if place in ends:
                    if at.n_strips == 1:
                        ends[place] = [part * at.has_left, part * at.has_right]
                    else:
                        ends[place][k] = part * present
        between = [u[k] - u[k + 1] for k in range(3)]
        for k in (1, 2):
            plane = u[k]
            left = turn(jnp.where(at.at_right, ends[k][0], plane), 1, 1)
            right = turn(jnp.where(at.at_left, ends[k][1], plane), -1, 1)
            up = jnp.where(at.first, 0.0, turn(plane, 1, 0))
            down = jnp.where(at.last, 0.0, turn(plane, -1, 0))
            steps = [between[k - 1], between[k]] + [plane - other for other in (left, right, up, down)]
            squares = [v * v for v in steps]
            total[k - 1] = total[k - 1] + factors[g, k - 1] * sum(squares[1:], squares[0])
    for k in range(2):
        out[lax.rem(k + core, 2)] = total[k]


def call(body, outs, *args, scalars=(), scratch=(), flops=0):
    smem = pl.BlockSpec(memory_space=pltpu.SMEM)
    return pl.pallas_call(
        body,
        out_shape=[jax.ShapeDtypeStruct(shape, jnp.float32) for shape in outs],
        in_specs=[pl.BlockSpec(memory_space=pltpu.VMEM)] * len(args) + [smem] * len(scalars),
        out_specs=[pl.BlockSpec(memory_space=pltpu.VMEM)] * len(outs),
        scratch_shapes=[pltpu.VMEM(shape, jnp.float32) for shape in scratch],
        cost_estimate=pl.CostEstimate(flops=flops, transcendentals=0, bytes_accessed=0) if flops else None,
        compiler_params=pltpu.CompilerParams(vmem_limit_bytes=32 * 1024 * 1024),
    )(*args, *scalars)


def local(design, solid_mask, void_mask, load_mask, support_mask, thresholds, group_weight):
    depth, width, thick = design.shape
    size, groups = lax.axis_size("space"), lax.axis_size("proj")
    quarter = width // 4
    pair, near_pairs = pair_swap(size), near_swap(size)
    fixed = jnp.where(solid_mask == 1, 1.0, jnp.where(void_mask == 1, 0.0, design))
    (packed_own,) = call(
        functools.partial(prepare, groups), [(6 * width + quarter, thick)], fixed, load_mask, support_mask
    )
    partner = lax.ppermute(packed_own, "space", pair)
    own, own_masks, scalars = call(
        join, [(4 * width, thick), (4 * width + quarter, thick), (8, thick)], packed_own, partner,
        scalars=(thresholds, group_weight),
    )
    others = [lax.ppermute(scalars, "proj", [((g + k) % groups, g) for g in range(groups)]) for k in range(1, groups)]
    near = lax.ppermute(own, "space", near_pairs)
    near_masks = lax.ppermute(own_masks, "space", near_pairs)
    others = [call(keep, [other.shape], other, flops=880_000_000)[0] for other in others]
    steps = (1,) if groups == 2 else (1, -1)
    inside, *packed = call(
        functools.partial(pack, groups),
        [(width, thick)] + [(width // 2, thick)] * len(steps) + [(width // 8, thick)] * len(steps),
        own, near,
    )
    straight = [(i, i) for i in range(size)]
    both = ("proj", "space")
    beside = [lax.ppermute(v, both, both_axes(straight, size, groups, k)) for k, v in zip(steps, packed)]
    crossed = [lax.ppermute(v, both, both_axes(pair, size, groups, k)) for k, v in zip(steps, packed[len(steps) :])]
    (beyond,) = call(pick, [(2 * width, thick)], near, inside, *others)
    inner = lax.ppermute(beyond, "space", pair)
    n_strips = 1 if groups == 2 else 2
    plane = (width, thick)
    six = (groups, 6, *plane)
    stiff, links, factors, wide, inside = call(
        functools.partial(density_kernel, groups, size),
        [six, six, (groups, 2, *plane), (n_strips, *plane), plane],
        own, near, inner, inside, scalars, *others,
        scratch=[(PLACES, width + 16, thick), (6, width + 16, thick)],
    )
    totals, z, w, mask_strips = call(
        functools.partial(inner_kernel, groups, size),
        [(-(-4 * groups // 8) * 8, thick), (groups, 4, *plane), (groups, 4, *plane), (2, n_strips, *plane)],
        stiff, links, own_masks, partner, near_masks,
        scratch=[(4, width + 16, thick), (4, width + 16, thick), (2, width + 16, thick)],
    )
    beside, crossed = ([call(keep, [v.shape], v, totals)[0] for v in vs] for vs in (beside, crossed))
    table, strips, factors = call(
        functools.partial(edge_kernel, groups, size),
        [(size * groups, thick), (groups, 2, n_strips, *plane), (groups, 2, *plane)],
        inside, wide, mask_strips, totals, factors, scalars, *beside, *crossed, *others,
    )
    table = lax.all_to_all(table, ("proj", "space"), 0, 0, tiled=True)
    (out,) = call(functools.partial(finish, groups, size), [(depth, *plane)], table, z, w, strips, factors)
    return out


def solution(mesh):
    placed = (
        P("space", None, "proj"),
        P("space", None, "proj"),
        P("space", None, "proj"),
        P("space", None, None),
        P("space", None, None),
        P("proj"),
        P("proj"),
    )
    return jax.shard_map(
        local, mesh=mesh, in_specs=placed, out_specs=P("space", None, "proj"), check_vma=False
    )
```

```python
import functools
import math

import jax
import jax.numpy as jnp
from jax import lax
from jax.experimental import pallas as pl
from jax.experimental.pallas import tpu as pltpu
from jax.sharding import PartitionSpec as P

RMIN = 2.0
BETA = 8.0
EMIN = 0.05
PENALTY = 4.0

PLACES = 10
GROUP = 8
HALF = GROUP // 2
WIDE = 2 * GROUP
INNER = PLACES - 2


def pair_swap(size):
    return [(i, i ^ 1) for i in range(size)]


def near_swap(size):
    ups = [(i, i + 1) for i in range(1, size - 1, 2)]
    return ups + [(j, i) for i, j in ups]


def both_axes(pairs, size, groups, step):
    return [
        (g * size + i, (g + step) % groups * size + j)
        for g in range(groups)
        for i, j in pairs
        if groups == 2 or 0 <= g + step < groups
    ]


def lanes_of(shape):
    return lax.broadcasted_iota(jnp.int32, shape, len(shape) - 1)


def turn(array, shift, axis):
    return pltpu.roll(array, shift % array.shape[axis], axis)


def squeeze(strips):
    rows, lanes = strips.shape[0] // 4, strips.shape[1]
    parts = [turn(strips[k * rows : (k + 1) * rows], k * lanes // 4, 1) for k in range(4)]
    block = lanes_of((rows, lanes)) // (lanes // 4)
    return functools.reduce(lambda out, k: jnp.where(block == k, parts[k], out), range(1, 4), parts[0])


def spread(squeezed):
    lanes = squeezed.shape[1]
    return jnp.concatenate([turn(squeezed, -k * lanes // 4, 1) for k in range(4)], axis=0)


def prepare(groups, fixed, load, support, out):
    core = lax.rem(lax.axis_index("space"), 2)
    layer = lax.axis_index("proj")
    width, thick = load.shape[1], load.shape[2] // groups
    lane = lanes_of((width, thick))
    lower = lax.rem(lane, GROUP) < HALF
    has_left = layer > 0
    has_right = layer < groups - 1
    centre = pl.ds(pl.multiple_of(layer * thick, thick), thick)
    left = pl.ds(pl.multiple_of(jnp.maximum(layer - 1, 0) * thick, thick), thick)
    right = pl.ds(pl.multiple_of(jnp.minimum(layer + 1, groups - 1) * thick, thick), thick)
    strips = jnp.zeros((width, thick), jnp.float32)
    for place in range(2):
        plane = lax.rem(place + core, 2)
        out[place * width : (place + 1) * width] = fixed[plane]
        for which, mask in enumerate((load, support)):
            held = 2 * which + place
            out[(2 + held) * width : (3 + held) * width] = mask[plane, :, centre].astype(jnp.float32)
            before = jnp.where(has_left, mask[plane, :, left].astype(jnp.float32), 0.0)
            after = jnp.where(has_right, mask[plane, :, right].astype(jnp.float32), 0.0)
            shift = held * GROUP + HALF
            outside = jnp.where(lower, turn(before, shift, 1), turn(after, shift, 1))
            strips = jnp.where(lane // GROUP == held, outside, strips)
    out[6 * width :] = squeeze(strips)


def join(own, partner, thresholds, weights, near_out, mask_out, scalars):
    rows = near_out.shape[0] // 2
    near_out[0:rows] = own[0:rows]
    near_out[rows:] = partner[0:rows]
    mask_out[...] = own[rows:]
    row = lax.broadcasted_iota(jnp.int32, scalars.shape, 0)
    scalars[...] = jnp.where(row == 0, thresholds[0].astype(jnp.float32) / 1000.0, jnp.where(row == 1, weights[0], 0.0))


def keep(array, *refs):
    refs[-1][...] = array[...]


def pick(near, *refs):
    out = refs[-1]
    out[...] = near[0 : out.shape[0]]


def plane_of(ref, k, width):
    return ref[k * width : (k + 1) * width]


def frame_of(own, near):
    order = ((near, 2), (near, 3), (near, 1), (near, 0), (own, 0), (own, 1), (own, 3), (own, 2))
    return [plane_of(ref, k, near.shape[0] // 4) for ref, k in order]


def fold(strips, lower):
    half = strips.shape[0] // 2
    low = lax.rem(lanes_of((half, strips.shape[1])), GROUP) < HALF
    top, bottom = strips[:half], strips[half:]
    folded_low = jnp.where(low, top, turn(bottom, HALF, 1))
    folded_high = jnp.where(low, turn(bottom, -HALF, 1), top)
    return jnp.where(lower, folded_low, folded_high)


def unfold(folded, lower):
    return jnp.concatenate([folded, jnp.where(lower, turn(folded, -HALF, 1), turn(folded, HALF, 1))], axis=0)


def pack(groups, own, near, inside, *outs):
    width, thick = inside.shape
    lane = lanes_of((width, thick))
    strips = jnp.zeros((width, thick), jnp.float32)
    for place, plane in enumerate(frame_of(own, near)):
        strips = jnp.where(lane // GROUP == place, turn(plane, place * GROUP + HALF, 1), strips)
    inside[...] = strips
    sides = (lax.axis_index("proj") == 0,) if groups == 2 else (True, False)
    for k, lower in enumerate(sides):
        outs[k][...] = fold(strips, lower)
        outs[len(sides) + k][...] = squeeze(fold(turn(strips, -2 * GROUP, 1), lower))


def around_y(plane, first, last):
    return jnp.where(first, 0.0, turn(plane, 1, 0)) + jnp.where(last, 0.0, turn(plane, -1, 0))


class Spot:
    def __init__(self, groups, size, width, thick):
        self.groups, self.width, self.thick = groups, width, thick
        self.spot, self.layer = lax.axis_index("space"), lax.axis_index("proj")
        core = lax.rem(self.spot, 2)
        self.shape = (width, thick)
        self.lane = lanes_of(self.shape)
        row = lax.broadcasted_iota(jnp.int32, self.shape, 0)
        self.first, self.last = row == 0, row == width - 1
        self.at_left, self.at_right = self.lane == 0, self.lane == thick - 1
        self.where = self.lane // GROUP
        self.slot = lax.rem(self.lane, GROUP)
        self.lower = self.slot < HALF
        self.near_real = jnp.where(jnp.where(core == 0, self.spot > 0, self.spot < size - 1), 1.0, 0.0)
        self.inner_real = jnp.where(jnp.where(core == 0, self.spot < size - 2, self.spot > 1), 1.0, 0.0)
        self.real = [self.near_real] * 4 + [1.0] * 4 + [self.inner_real] * 2
        self.has_left = jnp.where(self.layer > 0, 1.0, 0.0)
        self.has_right = jnp.where(self.layer < groups - 1, 1.0, 0.0)
        self.n_strips = 1 if groups == 2 else 2
        self.is_right = self.layer == 0

    def real_at(self, places):
        return jnp.where(places < 4, self.near_real, jnp.where(places < 8, 1.0, self.inner_real))

    def strips(self, inside, outside):
        right = jnp.where(self.lower, inside, outside[-1])
        left = jnp.where(self.lower, outside[0], inside)
        return [jnp.where(self.is_right, right, left)] if self.n_strips == 1 else [left, right]

    def strip_z(self):
        left, right = (self.layer * self.thick + self.slot + shift for shift in (-HALF, self.thick - HALF))
        return [jnp.where(self.is_right, right, left)] if self.n_strips == 1 else [left, right]

    def sides(self):
        if self.n_strips == 1:
            return [(self.is_right, 1.0)]
        return [(False, self.has_left), (True, self.has_right)]

    def held(self, is_right):
        right, left = self.lane >= self.thick - HALF, self.lane < HALF
        if isinstance(is_right, bool):
            return right if is_right else left
        return jnp.where(is_right, self.lane, self.thick - 1 - self.lane) >= self.thick - HALF


def by_side(is_right, left, right):
    if isinstance(is_right, bool):
        return right if is_right else left
    return jnp.where(is_right, right, left)


def shifted(array, is_right, left, right):
    size = array.shape[1]
    return pltpu.roll(array, by_side(is_right, left % size, right % size), 1)


def of_strip(strip, is_right, place):
    start = (place - 1) * WIDE
    return shifted(strip, is_right, -(start + HALF), -(start + WIDE - HALF))


def count_terms(count_y, count_z):
    two, three = RMIN - math.sqrt(2.0), RMIN - math.sqrt(3.0)
    head = 2.0 + (count_y + count_z) + two * (count_y * count_z)
    side = 1.0 + two * (count_y + count_z) + three * (count_y * count_z)
    return head, side


def weights_of(at, packed, others, g):
    eta, weight = packed[0:1], packed[1:2]
    for k, other in enumerate(others):
        mine = lax.rem(at.layer + k + 1, at.groups) == g
        eta = jnp.where(mine, other[0:1], eta)
        weight = jnp.where(mine, other[1:2], weight)
    return eta, weight


def projection(eta):
    low = jnp.tanh(BETA * eta)
    over_bottom = 1.0 / (low + jnp.tanh(BETA * (1.0 - eta)))

    def stiffness(density, present):
        inner_part = jnp.tanh(BETA * (density - eta))
        value = (low + inner_part) * over_bottom
        return inner_part, value, (EMIN + (1.0 - EMIN) * (value * value * value)) * present

    def factor(inner_part, value, weight):
        slope = (BETA * over_bottom) * (1.0 - inner_part * inner_part)
        return (-0.5 * 3.0 * (1.0 - EMIN)) * weight * (value * value) * slope

    return stiffness, factor


def border(ref, width):
    ref[:, 0:8] = jnp.zeros((ref.shape[0], 8, ref.shape[2]), jnp.float32)
    ref[:, 8 + width :] = jnp.zeros((ref.shape[0], 8, ref.shape[2]), jnp.float32)


def to_left(at, plane):
    return jnp.where(at.at_left, 0.0, turn(plane, 1, 1))


def to_right(at, plane):
    return jnp.where(at.at_right, 0.0, turn(plane, -1, 1))


def own_columns(is_right, plane, place):
    start = (place - 1) * WIDE
    return shifted(plane, is_right, start + HALF, start + WIDE - HALF)


def density_kernel(groups, size, *refs):
    own, near, inner, inside, scalars = refs[:5]
    others = refs[5 : len(refs) - 7]
    stiff_out, links_out, factor_out, wide_out, inside_out, f_rows, s_rows = refs[len(refs) - 7 :]
    width, thick = near.shape[0] // 4, near.shape[1]
    at = Spot(groups, size, width, thick)
    two, three = RMIN - math.sqrt(2.0), RMIN - math.sqrt(3.0)
    planes = frame_of(own, near) + [plane_of(inner, k, width) for k in (0, 1)]
    strip = inside[...]
    for place in (8, 9):
        strip = jnp.where(at.where == place, turn(planes[place], place * GROUP + HALF, 1), strip)
    inside_out[...] = strip
    for ref in (f_rows, s_rows):
        border(ref, width)
    for place in range(PLACES):
        f_rows[place, 8 : 8 + width] = planes[place]

    count_y = jnp.where(at.first, 0.0, 1.0) + jnp.where(at.last, 0.0, 1.0)
    places_z = at.layer * thick + at.lane
    count_z = jnp.where(places_z >= 1, 1.0, 0.0) + jnp.where(places_z < groups * thick - 1, 1.0, 0.0)
    head, side = count_terms(count_y, count_z)
    over_two, over_one = 1.0 / (head + 2.0 * side), 1.0 / (head + side)
    straight, once, twice = [], [], []
    for place in range(PLACES):
        plane = planes[place]
        by_y = f_rows[place, 7 : 7 + width] + f_rows[place, 9 : 9 + width]
        straight.append(2.0 * plane + by_y)
        once.append(plane + two * by_y)
        twice.append(two * plane + three * by_y)
    filtered = {}
    for place in range(1, PLACES - 1):
        beside = once[place] + (twice[place - 1] + twice[place + 1])
        total = straight[place] + (once[place - 1] + once[place + 1]) + (to_left(at, beside) + to_right(at, beside))
        count_x = at.real[place - 1] + at.real[place + 1]
        filtered[place] = total * jnp.where(count_x > 1.5, over_two, over_one)

    block = at.lane // WIDE
    for k, (is_right, _) in enumerate(at.sides()):
        strip = jnp.zeros(at.shape, jnp.float32)
        for place in range(1, PLACES - 1):
            strip = jnp.where(block == place - 1, own_columns(is_right, filtered[place], place), strip)
        wide_out[k] = strip

    for g in range(groups):
        eta, weight = weights_of(at, scalars, others, g)
        stiffness, factor = projection(eta)
        stiff = {}
        for place in range(1, PLACES - 1):
            inner_part, value, stiff[place] = stiffness(filtered[place], at.real[place])
            if place in (4, 5):
                factor_out[g, place - 4] = factor(inner_part, value, weight)
            if 2 <= place < 8:
                s_rows[place - 2, 8 : 8 + width] = stiff[place]
                stiff_out[g, place - 2] = stiff[place]
        for place in range(2, 8):
            s = stiff[place]
            by_y = s_rows[place - 2, 7 : 7 + width] + s_rows[place - 2, 9 : 9 + width]
            by_z = to_left(at, s) + to_right(at, s)
            links_out[g, place - 2] = 3.0 * s + 0.5 * ((stiff[place - 1] + stiff[place + 1]) + by_z + by_y)


def image_of(at, stiff, rows_of_stiff, field, rows, place, before, after):
    v, s = field[place], stiff[place]
    width = at.width

    def beside(ref_and_start, first):
        ref, start = ref_and_start
        return ref[place - start, first : first + width]

    k_right = s + to_right(at, s)
    flow_z = k_right * (v - to_right(at, v))
    total = (after - before) + (flow_z - jnp.where(at.at_left, -(s * v), turn(flow_z, 1, 1)))
    s_up, s_down = beside(rows_of_stiff, 7), beside(rows_of_stiff, 9)
    v_up, v_down = beside(rows, 7), beside(rows, 9)
    return total + ((s + s_up) * (v - v_up) + (s + s_down) * (v - v_down))


def flow_x(stiff, field, place):
    return (stiff[place] + stiff[place + 1]) * (field[place] - field[place + 1])


def start_of(at, links, load, support, place):
    over = at.real[place] / jnp.maximum(links + PENALTY * support, 0.1)
    return over, load * over


def mask_strips_of(at, is_right, strip, which, parts):
    block, slot = at.lane // WIDE, lax.rem(at.lane, WIDE)
    beyond = by_side(is_right, slot, WIDE - 1 - slot) < HALF
    for place, plane, source, held in parts:
        start = (place - 1) * WIDE - (held + 2 * which) * GROUP
        outer = shifted(source, is_right, start, start + WIDE - GROUP)
        value = jnp.where(beyond, outer, own_columns(is_right, plane, place))
        strip = jnp.where(block == place - 1, value, strip)
    return strip


def own_kernel(groups, size, *refs):
    stiff_in, links_in, own_masks, partner = refs[:4]
    z_out, w_out, q_out, over_out, masks_out, s_rows, z_rows = refs[4:]
    width, thick = stiff_in.shape[2:]
    partner_masks = partner.at[2 * width :]
    at = Spot(groups, size, width, thick)
    for ref in (s_rows, z_rows):
        border(ref, width)
    order = ((own_masks, 0), (own_masks, 1), (partner_masks, 1), (partner_masks, 0))
    load, support = (
        {place + 4: plane_of(ref, 2 * which + k, width) for place, (ref, k) in enumerate(order)} for which in (0, 1)
    )
    mine, theirs = spread(own_masks[4 * width :]), spread(partner_masks[4 * width :])
    for k, (is_right, _) in enumerate(at.sides()):
        for which, mask in enumerate((load, support)):
            sources = ((mine, 0), (mine, 1), (theirs, 1), (theirs, 0))
            parts = [(place + 4, mask[place + 4], *source) for place, source in enumerate(sources)]
            masks_out[which, k] = mask_strips_of(at, is_right, jnp.zeros(at.shape, jnp.float32), which, parts)

    for g in range(groups):
        stiff = {place: stiff_in[g, place - 2] for place in range(4, 8)}
        over, z = {}, {}
        for place in range(4, 8):
            over[place], z[place] = start_of(at, links_in[g, place - 2], load[place], support[place], place)
            z_out[g, place - 4] = z[place]
        over_out[g] = over[4]
        for place in (5, 6):
            s_rows[place - 5, 8 : 8 + width] = stiff[place]
            z_rows[place - 5, 8 : 8 + width] = z[place]
        flows = {place: flow_x(stiff, z, place) for place in (4, 5, 6)}
        for place in (5, 6):
            q = 0.5 * image_of(at, stiff, (s_rows, 5), z, (z_rows, 5), place, flows[place - 1], flows[place])
            w_out[g, place - 5] = q * over[place]
            if place == 5:
                q_out[g] = q


def near_kernel(groups, size, *refs):
    stiff_in, links_in, near_masks, z_in, w_in, q_in, over_in, masks_in = refs[:8]
    totals_out, z_out, w_out, masks_out, s_rows, z_rows, w_rows = refs[8:]
    width, thick = stiff_in.shape[2:]
    at = Spot(groups, size, width, thick)
    for ref in (s_rows, z_rows, w_rows):
        border(ref, width)
    load, support = (
        {place: plane_of(near_masks, 2 * which + 3 - place, width) for place in (2, 3)} for which in (0, 1)
    )
    nears = spread(near_masks[4 * width :])
    for k, (is_right, _) in enumerate(at.sides()):
        for which, mask in enumerate((load, support)):
            parts = [(place, mask[place], nears, 3 - place) for place in (2, 3)]
            masks_out[which, k] = mask_strips_of(at, is_right, masks_in[which, k], which, parts)

    counted = jnp.ones(at.shape, jnp.float32)
    for is_right, present in at.sides():
        counted = jnp.where(at.held(is_right), 1.0 - present, counted)

    rows_out = 0
    for g in range(groups):
        stiff = {place: stiff_in[g, place - 2] for place in range(2, 7)}
        z = {4: z_in[g, 0], 5: z_in[g, 1]}
        over = {4: over_in[g]}
        for place in (2, 3):
            over[place], z[place] = start_of(at, links_in[g, place - 2], load[place], support[place], place)
        z_out[g] = z[3]
        for place in (3, 4, 5):
            s_rows[place - 3, 8 : 8 + width] = stiff[place]
        for place in (3, 4):
            z_rows[place - 3, 8 : 8 + width] = z[place]
        flows = {place: flow_x(stiff, z, place) for place in (2, 3, 4)}
        q, w = {5: q_in[g]}, {5: w_in[g, 0], 6: w_in[g, 1]}
        for place in (3, 4):
            q[place] = 0.5 * image_of(at, stiff, (s_rows, 3), z, (z_rows, 3), place, flows[place - 1], flows[place])
            w[place] = q[place] * over[place]
            w_out[g, place - 3] = w[place]
        for place in (4, 5):
            w_rows[place - 4, 8 : 8 + width] = w[place]
        flows = {place: flow_x(stiff, w, place) for place in (3, 4, 5)}
        totals = [0.0, 0.0, 0.0, 0.0]
        for place in (4, 5):
            aw = 0.5 * image_of(at, stiff, (s_rows, 3), w, (w_rows, 4), place, flows[place - 1], flows[place])
            terms = (z[place], z[place] * q[place], q[place] * w[place], w[place] * aw)
            totals = [a + b for a, b in zip(totals, terms)]
        for total in totals:
            totals_out[rows_out : rows_out + 1] = jnp.sum(total * counted, axis=0, keepdims=True)
            rows_out += 1


def edge_kernel(groups, size, *refs):
    n_side = 1 if groups == 2 else 2
    inside, wide, masks, totals, factors, scalars = refs[:6]
    beside, crossed = refs[6 : 6 + n_side], refs[6 + n_side : 6 + 2 * n_side]
    others = refs[6 + 2 * n_side : len(refs) - 3]
    table, strip_out, factor_out = refs[len(refs) - 3 :]
    width, thick = inside.shape
    at = Spot(groups, size, width, thick)
    first, last = at.first, at.last
    two, three = RMIN - math.sqrt(2.0), RMIN - math.sqrt(3.0)

    outside = []
    for k in range(n_side):
        lower = at.layer == 1 if groups == 2 else k == 0
        strip, back = unfold(beside[k][...], lower), unfold(spread(crossed[k][...]), lower)
        strip = jnp.where(at.where == 8, turn(back, 7 * GROUP, 1), strip)
        strip = jnp.where(at.where == 9, turn(back, 9 * GROUP, 1), strip)
        outside.append(jnp.where(at.where < PLACES, strip, 0.0))
    outside = [outside[0] * at.has_left, outside[-1] * at.has_right]
    fixed = at.strips(inside[...], outside)

    count_y = jnp.where(first, 0.0, 1.0) + jnp.where(last, 0.0, 1.0)
    count_x = at.real_at(at.where - 1) + at.real_at(at.where + 1)
    span_z = thick * groups
    block, slot = at.lane // WIDE, lax.rem(at.lane, WIDE)
    filtered, presents, counts = [], [], []
    for k, (strip, z_at, (is_right, present)) in enumerate(zip(fixed, at.strip_z(), at.sides())):
        by_y = around_y(strip, first, last)
        once = strip + two * by_y
        across = once + turn(two * strip + three * by_y, GROUP, 1) + turn(two * strip + three * by_y, -GROUP, 1)
        total = 2.0 * strip + by_y + turn(once, GROUP, 1) + turn(once, -GROUP, 1)
        total = total + turn(across, 1, 1) + turn(across, -1, 1)
        count_z = jnp.where(z_at >= 1, 1.0, 0.0) + jnp.where(z_at < span_z - 1, 1.0, 0.0)
        head, side = count_terms(count_y, count_z)
        total = total / (head + count_x * side)
        value = wide[k]
        better = by_side(is_right, slot, WIDE - 1 - slot) <= HALF
        for place in range(1, PLACES - 1):
            start = (place - 1) * WIDE - place * GROUP
            moved = shifted(total, is_right, start, start + WIDE - GROUP)
            value = jnp.where(better & (block == place - 1), moved, value)
        filtered.append(value)
        z_wide = at.layer * thick + slot + by_side(is_right, -HALF, thick - WIDE + HALF)
        presents.append(jnp.where((z_wide >= 0) & (z_wide < span_z), at.real_at(block + 1), 0.0))
        own = by_side(is_right, slot, WIDE - 1 - slot)
        own = (own >= HALF) & (own < 2 * HALF) & (block >= 3) & (block < 5)
        counts.append(jnp.where(own, present, 0.0))

    lane_row = lanes_of((1, thick))
    line = jnp.zeros((1, thick), jnp.float32)
    for g in range(groups):
        eta, weight = weights_of(at, scalars, others, g)
        stiffness, factor = projection(eta)
        sums = [totals[4 * g + k : 4 * g + k + 1] for k in range(4)]
        patched = [factors[g, 0], factors[g, 1]]
        for k, (is_right, present) in enumerate(at.sides()):
            inner_part, value, s = stiffness(filtered[k], presents[k])
            of_place = factor(inner_part, value, weight)
            for place in (0, 1):
                here = at.held(is_right) & (present > 0.5)
                patched[place] = jnp.where(here, of_strip(of_place, is_right, place + 4), patched[place])
            s_next, s_right = turn(s, -WIDE, 1), turn(s, -1, 1)
            s_up, s_down = jnp.where(first, 0.0, turn(s, 1, 0)), jnp.where(last, 0.0, turn(s, -1, 0))
            links = 6.0 * s + (s_next + turn(s, WIDE, 1)) + (s_right + turn(s, 1, 1)) + (s_up + s_down)
            inverse = presents[k] / jnp.maximum(0.5 * links + PENALTY * masks[1, k], 0.1)

            def image(v):
                flow_x = (s + s_next) * (v - turn(v, -WIDE, 1))
                flow_z = (s + s_right) * (v - turn(v, -1, 1))
                v_up, v_down = jnp.where(first, 0.0, turn(v, 1, 0)), jnp.where(last, 0.0, turn(v, -1, 0))
                total = (flow_x - turn(flow_x, WIDE, 1)) + (flow_z - turn(flow_z, 1, 1))
                return 0.5 * (total + ((s + s_up) * (v - v_up) + (s + s_down) * (v - v_down)))

            z = masks[0, k] * inverse
            q = image(z)
            w = q * inverse
            strip_out[g, 0, k] = z
            strip_out[g, 1, k] = w
            terms = (z, z * q, q * w, w * image(w))
            sums = [a + jnp.sum(b * counts[k], axis=0, keepdims=True) for a, b in zip(sums, terms)]
        for place in (0, 1):
            factor_out[g, place] = patched[place]
        for k, part in enumerate(sums):
            line = jnp.where(lane_row == 4 * g + k, jnp.sum(part, axis=1, keepdims=True), line)
    table[...] = jnp.broadcast_to(line, table.shape)


def finish(groups, size, table, z_near, z_own, w_near, w_own, strips, factors, out):
    width, thick = out.shape[1:]
    at = Spot(groups, size, width, thick)
    core = lax.rem(at.spot, 2)
    line = jnp.sum(table[...], axis=0, keepdims=True)
    lane_row = lanes_of((1, thick))
    total = [jnp.zeros(at.shape, jnp.float32), jnp.zeros(at.shape, jnp.float32)]
    for g in range(groups):
        m0, m1, m2, m3 = (
            jnp.sum(jnp.where(lane_row == 4 * g + k, line, 0.0), axis=1, keepdims=True) for k in range(4)
        )
        step_one = m0 / m1
        rz_next = step_one * step_one * m2 - m0
        factor = rz_next / m0
        curve = (m1 - 2.0 * step_one * m2 + step_one * step_one * m3) - factor * factor * m1
        step_two = rz_next / curve
        of_z = step_one + step_two * (1.0 + factor)
        of_w = -step_one * step_two
        z = [z_near[g], z_own[g, 0], z_own[g, 1], z_own[g, 2]]
        w = [w_near[g, 0], w_near[g, 1], w_own[g, 0], w_own[g, 1]]
        u = [of_z * v + of_w * t for v, t in zip(z, w)]
        ends = {1: [0.0, 0.0], 2: [0.0, 0.0]}
        for k, (is_right, present) in enumerate(at.sides()):
            strip = of_z * strips[g, 0, k] + of_w * strips[g, 1, k]
            here = at.held(is_right) & (present > 0.5)
            for place in range(4):
                part = of_strip(strip, is_right, place + 3)
                u[place] = jnp.where(here, part, u[place])
                if place in ends:
                    if at.n_strips == 1:
                        ends[place] = [part * at.has_left, part * at.has_right]
                    else:
                        ends[place][k] = part * present
        between = [u[k] - u[k + 1] for k in range(3)]
        for k in (1, 2):
            plane = u[k]
            left = turn(jnp.where(at.at_right, ends[k][0], plane), 1, 1)
            right = turn(jnp.where(at.at_left, ends[k][1], plane), -1, 1)
            up = jnp.where(at.first, 0.0, turn(plane, 1, 0))
            down = jnp.where(at.last, 0.0, turn(plane, -1, 0))
            steps = [between[k - 1], between[k]] + [plane - other for other in (left, right, up, down)]
            squares = [v * v for v in steps]
            total[k - 1] = total[k - 1] + factors[g, k - 1] * sum(squares[1:], squares[0])
    for k in range(2):
        out[lax.rem(k + core, 2)] = total[k]


def call(body, outs, *args, scalars=(), scratch=(), flops=0):
    smem = pl.BlockSpec(memory_space=pltpu.SMEM)
    return pl.pallas_call(
        body,
        out_shape=[jax.ShapeDtypeStruct(shape, jnp.float32) for shape in outs],
        in_specs=[pl.BlockSpec(memory_space=pltpu.VMEM)] * len(args) + [smem] * len(scalars),
        out_specs=[pl.BlockSpec(memory_space=pltpu.VMEM)] * len(outs),
        scratch_shapes=[pltpu.VMEM(shape, jnp.float32) for shape in scratch],
        cost_estimate=pl.CostEstimate(flops=flops, transcendentals=0, bytes_accessed=0) if flops else None,
        compiler_params=pltpu.CompilerParams(vmem_limit_bytes=32 * 1024 * 1024),
    )(*args, *scalars)


def local(design, solid_mask, void_mask, load_mask, support_mask, thresholds, group_weight):
    depth, width, thick = design.shape
    size, groups = lax.axis_size("space"), lax.axis_size("proj")
    quarter = width // 4
    pair, near_pairs = pair_swap(size), near_swap(size)
    fixed = jnp.where(solid_mask == 1, 1.0, jnp.where(void_mask == 1, 0.0, design))
    (packed_own,) = call(
        functools.partial(prepare, groups), [(6 * width + quarter, thick)], fixed, load_mask, support_mask
    )
    partner = lax.ppermute(packed_own, "space", pair)
    own, own_masks, scalars = call(
        join, [(4 * width, thick), (4 * width + quarter, thick), (8, thick)], packed_own, partner,
        scalars=(thresholds, group_weight),
    )
    others = [lax.ppermute(scalars, "proj", [((g + k) % groups, g) for g in range(groups)]) for k in range(1, groups)]
    near = lax.ppermute(own, "space", near_pairs)
    near_masks = lax.ppermute(own_masks, "space", near_pairs)
    others = [call(keep, [other.shape], other, flops=880_000_000)[0] for other in others]
    steps = (1,) if groups == 2 else (1, -1)
    inside, *packed = call(
        functools.partial(pack, groups),
        [(width, thick)] + [(width // 2, thick)] * len(steps) + [(width // 8, thick)] * len(steps),
        own, near,
    )
    straight = [(i, i) for i in range(size)]
    both = ("proj", "space")
    beside = [lax.ppermute(v, both, both_axes(straight, size, groups, k)) for k, v in zip(steps, packed)]
    crossed = [lax.ppermute(v, both, both_axes(pair, size, groups, k)) for k, v in zip(steps, packed[len(steps) :])]
    (beyond,) = call(pick, [(2 * width, thick)], near, inside, *others)
    inner = lax.ppermute(beyond, "space", pair)
    n_strips = 1 if groups == 2 else 2
    plane = (width, thick)
    six = (groups, 6, *plane)
    stiff, links, factors, wide, inside = call(
        functools.partial(density_kernel, groups, size),
        [six, six, (groups, 2, *plane), (n_strips, *plane), plane],
        own, near, inner, inside, scalars, *others,
        scratch=[(PLACES, width + 16, thick), (6, width + 16, thick)],
    )
    one, two, four = (groups, *plane), (groups, 2, *plane), (groups, 4, *plane)
    strips_shape = (2, n_strips, *plane)
    z_own, w_own, q_own, over_own, mask_strips = call(
        functools.partial(own_kernel, groups, size),
        [four, two, one, one, strips_shape],
        stiff, links, own_masks, partner,
        scratch=[(2, width + 16, thick), (2, width + 16, thick)],
    )
    totals, z_near, w_near, mask_strips = call(
        functools.partial(near_kernel, groups, size),
        [(-(-4 * groups // 8) * 8, thick), one, two, strips_shape],
        stiff, links, near_masks, z_own, w_own, q_own, over_own, mask_strips,
        scratch=[(3, width + 16, thick), (2, width + 16, thick), (2, width + 16, thick)],
    )
    beside, crossed = ([call(keep, [v.shape], v, totals)[0] for v in vs] for vs in (beside, crossed))
    table, strips, factors = call(
        functools.partial(edge_kernel, groups, size),
        [(size * groups, thick), (groups, 2, n_strips, *plane), (groups, 2, *plane)],
        inside, wide, mask_strips, totals, factors, scalars, *beside, *crossed, *others,
    )
    table = lax.all_to_all(table, ("proj", "space"), 0, 0, tiled=True)
    (out,) = call(functools.partial(finish, groups, size), [(depth, *plane)], table, z_near, z_own, w_near, w_own, strips, factors)
    return out


def solution(mesh):
    placed = (
        P("space", None, "proj"),
        P("space", None, "proj"),
        P("space", None, "proj"),
        P("space", None, None),
        P("space", None, None),
        P("proj"),
        P("proj"),
    )
    return jax.shard_map(
        local, mesh=mesh, in_specs=placed, out_specs=P("space", None, "proj"), check_vma=False
    )
```

```python
import functools
import math

import jax
import jax.numpy as jnp
from jax import lax
from jax.experimental import pallas as pl
from jax.experimental.pallas import tpu as pltpu
from jax.sharding import PartitionSpec as P

RMIN = 2.0
BETA = 8.0
EMIN = 0.05
PENALTY = 4.0

PLACES = 10
GROUP = 8
HALF = GROUP // 2
WIDE = 2 * GROUP
INNER = PLACES - 2


def pair_swap(size):
    return [(i, i ^ 1) for i in range(size)]


def near_swap(size):
    ups = [(i, i + 1) for i in range(1, size - 1, 2)]
    return ups + [(j, i) for i, j in ups]


def both_axes(pairs, size, groups, step):
    return [
        (g * size + i, (g + step) % groups * size + j)
        for g in range(groups)
        for i, j in pairs
        if groups == 2 or 0 <= g + step < groups
    ]


def lanes_of(shape):
    return lax.broadcasted_iota(jnp.int32, shape, len(shape) - 1)


def turn(array, shift, axis):
    return pltpu.roll(array, shift % array.shape[axis], axis)


def squeeze(strips):
    rows, lanes = strips.shape[0] // 4, strips.shape[1]
    parts = [turn(strips[k * rows : (k + 1) * rows], k * lanes // 4, 1) for k in range(4)]
    block = lanes_of((rows, lanes)) // (lanes // 4)
    return functools.reduce(lambda out, k: jnp.where(block == k, parts[k], out), range(1, 4), parts[0])


def spread(squeezed, start=0):
    lanes = squeezed.shape[1]
    return jnp.concatenate([turn(squeezed, start - k * lanes // 4, 1) for k in range(4)], axis=0)


def prepare(groups, fixed, load, support, out):
    core = lax.rem(lax.axis_index("space"), 2)
    layer = lax.axis_index("proj")
    width, thick = load.shape[1], load.shape[2] // groups
    lane = lanes_of((width, thick))
    lower = lax.rem(lane, GROUP) < HALF
    has_left = layer > 0
    has_right = layer < groups - 1
    centre = pl.ds(pl.multiple_of(layer * thick, thick), thick)
    left = pl.ds(pl.multiple_of(jnp.maximum(layer - 1, 0) * thick, thick), thick)
    right = pl.ds(pl.multiple_of(jnp.minimum(layer + 1, groups - 1) * thick, thick), thick)
    strips = jnp.zeros((width, thick), jnp.float32)
    for place in range(2):
        plane = lax.rem(place + core, 2)
        out[place * width : (place + 1) * width] = fixed[plane]
        for which, mask in enumerate((load, support)):
            held = 2 * which + place
            out[(2 + held) * width : (3 + held) * width] = mask[plane, :, centre].astype(jnp.float32)
            before = jnp.where(has_left, mask[plane, :, left].astype(jnp.float32), 0.0)
            after = jnp.where(has_right, mask[plane, :, right].astype(jnp.float32), 0.0)
            shift = held * GROUP + HALF
            outside = jnp.where(lower, turn(before, shift, 1), turn(after, shift, 1))
            strips = jnp.where(lane // GROUP == held, outside, strips)
    out[6 * width :] = squeeze(strips)


def join(own, partner, thresholds, weights, near_out, mask_out, scalars):
    rows = near_out.shape[0] // 2
    near_out[0:rows] = own[0:rows]
    near_out[rows:] = partner[0:rows]
    mask_out[...] = own[rows:]
    row = lax.broadcasted_iota(jnp.int32, scalars.shape, 0)
    scalars[...] = jnp.where(row == 0, thresholds[0].astype(jnp.float32) / 1000.0, jnp.where(row == 1, weights[0], 0.0))


def keep(array, *refs):
    refs[-1][...] = array[...]


def pick(near, *refs):
    out = refs[-1]
    out[...] = near[0 : out.shape[0]]


def plane_of(ref, k, width):
    return ref[k * width : (k + 1) * width]


def frame_of(own, near):
    order = ((near, 2), (near, 3), (near, 1), (near, 0), (own, 0), (own, 1), (own, 3), (own, 2))
    return [plane_of(ref, k, near.shape[0] // 4) for ref, k in order]


def folded(planes, lower):
    half, lanes = planes[0].shape[0] // 2, planes[0].shape[1]
    lane = lanes_of((half, lanes))
    low, group = lax.rem(lane, GROUP) < HALF, lane // GROUP
    out = jnp.zeros((half, lanes), jnp.float32)
    for place, plane in enumerate(planes):
        start = place * GROUP + HALF
        top, bottom = turn(plane[:half], start, 1), plane[half:]
        of_lower = jnp.where(low, top, turn(bottom, start + HALF, 1))
        of_upper = jnp.where(low, turn(bottom, start - HALF, 1), top)
        out = jnp.where(group == place, jnp.where(lower, of_lower, of_upper), out)
    return out


def unfold(folded, lower):
    return jnp.concatenate([folded, jnp.where(lower, turn(folded, -HALF, 1), turn(folded, HALF, 1))], axis=0)


def pack(groups, own, near, *outs):
    planes = frame_of(own, near)
    sides = (lax.axis_index("proj") == 0,) if groups == 2 else (True, False)
    for k, lower in enumerate(sides):
        outs[k][...] = folded(planes, lower)
        outs[len(sides) + k][...] = squeeze(folded([planes[3], planes[2]], lower))


def around_y(plane, first, last):
    return jnp.where(first, 0.0, turn(plane, 1, 0)) + jnp.where(last, 0.0, turn(plane, -1, 0))


class Spot:
    def __init__(self, groups, size, width, thick):
        self.groups, self.width, self.thick = groups, width, thick
        self.spot, self.layer = lax.axis_index("space"), lax.axis_index("proj")
        core = lax.rem(self.spot, 2)
        self.shape = (width, thick)
        self.lane = lanes_of(self.shape)
        row = lax.broadcasted_iota(jnp.int32, self.shape, 0)
        self.first, self.last = row == 0, row == width - 1
        self.at_left, self.at_right = self.lane == 0, self.lane == thick - 1
        self.where = self.lane // GROUP
        self.slot = lax.rem(self.lane, GROUP)
        self.lower = self.slot < HALF
        self.near_real = jnp.where(jnp.where(core == 0, self.spot > 0, self.spot < size - 1), 1.0, 0.0)
        self.inner_real = jnp.where(jnp.where(core == 0, self.spot < size - 2, self.spot > 1), 1.0, 0.0)
        self.real = [self.near_real] * 4 + [1.0] * 4 + [self.inner_real] * 2
        self.has_left = jnp.where(self.layer > 0, 1.0, 0.0)
        self.has_right = jnp.where(self.layer < groups - 1, 1.0, 0.0)
        self.n_strips = 1 if groups == 2 else 2
        self.is_right = self.layer == 0

    def real_at(self, places):
        return jnp.where(places < 4, self.near_real, jnp.where(places < 8, 1.0, self.inner_real))

    def strips(self, inside, outside):
        right = jnp.where(self.lower, inside, outside[-1])
        left = jnp.where(self.lower, outside[0], inside)
        return [jnp.where(self.is_right, right, left)] if self.n_strips == 1 else [left, right]

    def strip_z(self):
        left, right = (self.layer * self.thick + self.slot + shift for shift in (-HALF, self.thick - HALF))
        return [jnp.where(self.is_right, right, left)] if self.n_strips == 1 else [left, right]

    def sides(self):
        if self.n_strips == 1:
            return [(self.is_right, 1.0)]
        return [(False, self.has_left), (True, self.has_right)]

    def wide(self, is_right):
        lane = lax.rem(self.lane + by_side(is_right, 0, WIDE // 2), self.thick)
        return lane // WIDE, lax.rem(lane, WIDE)

    def held(self, is_right):
        right, left = self.lane >= self.thick - HALF, self.lane < HALF
        if isinstance(is_right, bool):
            return right if is_right else left
        return jnp.where(is_right, self.lane, self.thick - 1 - self.lane) >= self.thick - HALF


def by_side(is_right, left, right):
    if isinstance(is_right, bool):
        return right if is_right else left
    return jnp.where(is_right, right, left)


def of_strip(strip, place):
    return turn(strip, -((place - 1) * WIDE + HALF), 1)


def count_terms(count_y, count_z):
    two, three = RMIN - math.sqrt(2.0), RMIN - math.sqrt(3.0)
    head = 2.0 + (count_y + count_z) + two * (count_y * count_z)
    side = 1.0 + two * (count_y + count_z) + three * (count_y * count_z)
    return head, side


def weights_of(at, packed, others, g):
    eta, weight = packed[0:1], packed[1:2]
    for k, other in enumerate(others):
        mine = lax.rem(at.layer + k + 1, at.groups) == g
        eta = jnp.where(mine, other[0:1], eta)
        weight = jnp.where(mine, other[1:2], weight)
    return eta, weight


def projection(eta):
    low = jnp.tanh(BETA * eta)
    over_bottom = 1.0 / (low + jnp.tanh(BETA * (1.0 - eta)))

    def stiffness(density, present):
        inner_part = jnp.tanh(BETA * (density - eta))
        value = (low + inner_part) * over_bottom
        return inner_part, value, (EMIN + (1.0 - EMIN) * (value * value * value)) * present

    def factor(inner_part, value, weight):
        slope = (BETA * over_bottom) * (1.0 - inner_part * inner_part)
        return (-0.5 * 3.0 * (1.0 - EMIN)) * weight * (value * value) * slope

    return stiffness, factor


def border(ref, width):
    ref[:, 0:8] = jnp.zeros((ref.shape[0], 8, ref.shape[2]), jnp.float32)
    ref[:, 8 + width :] = jnp.zeros((ref.shape[0], 8, ref.shape[2]), jnp.float32)


def to_left(at, plane):
    return jnp.where(at.at_left, 0.0, turn(plane, 1, 1))


def to_right(at, plane):
    return jnp.where(at.at_right, 0.0, turn(plane, -1, 1))


def own_columns(plane, place):
    return turn(plane, (place - 1) * WIDE + HALF, 1)


def density_kernel(groups, size, *refs):
    own, near, inner, scalars = refs[:4]
    others = refs[4 : len(refs) - 7]
    stiff_out, links_out, factor_out, wide_out, inside_out, f_rows, s_rows = refs[len(refs) - 7 :]
    width, thick = near.shape[0] // 4, near.shape[1]
    at = Spot(groups, size, width, thick)
    two, three = RMIN - math.sqrt(2.0), RMIN - math.sqrt(3.0)
    planes = frame_of(own, near) + [plane_of(inner, k, width) for k in (0, 1)]
    strip = jnp.zeros(at.shape, jnp.float32)
    for place in range(PLACES):
        strip = jnp.where(at.where == place, turn(planes[place], place * GROUP + HALF, 1), strip)
    inside_out[...] = strip
    for ref in (f_rows, s_rows):
        border(ref, width)
    for place in range(PLACES):
        f_rows[place, 8 : 8 + width] = planes[place]

    count_y = jnp.where(at.first, 0.0, 1.0) + jnp.where(at.last, 0.0, 1.0)
    places_z = at.layer * thick + at.lane
    count_z = jnp.where(places_z >= 1, 1.0, 0.0) + jnp.where(places_z < groups * thick - 1, 1.0, 0.0)
    head, side = count_terms(count_y, count_z)
    over_two, over_one = 1.0 / (head + 2.0 * side), 1.0 / (head + side)
    straight, once, twice = [], [], []
    for place in range(PLACES):
        plane = planes[place]
        by_y = f_rows[place, 7 : 7 + width] + f_rows[place, 9 : 9 + width]
        straight.append(2.0 * plane + by_y)
        once.append(plane + two * by_y)
        twice.append(two * plane + three * by_y)
    filtered = {}
    for place in range(1, PLACES - 1):
        beside = once[place] + (twice[place - 1] + twice[place + 1])
        total = straight[place] + (once[place - 1] + once[place + 1]) + (to_left(at, beside) + to_right(at, beside))
        count_x = at.real[place - 1] + at.real[place + 1]
        filtered[place] = total * jnp.where(count_x > 1.5, over_two, over_one)

    for k, (is_right, _) in enumerate(at.sides()):
        block, _ = at.wide(is_right)
        strip = jnp.zeros(at.shape, jnp.float32)
        for place in range(1, PLACES - 1):
            strip = jnp.where(block == place - 1, own_columns(filtered[place], place), strip)
        wide_out[k] = strip

    for g in range(groups):
        eta, weight = weights_of(at, scalars, others, g)
        stiffness, factor = projection(eta)
        stiff = {}
        for place in range(1, PLACES - 1):
            inner_part, value, stiff[place] = stiffness(filtered[place], at.real[place])
            if place in (4, 5):
                factor_out[g, place - 4] = factor(inner_part, value, weight)
            if 2 <= place < 8:
                s_rows[place - 2, 8 : 8 + width] = stiff[place]
                stiff_out[g, place - 2] = stiff[place]
        for place in range(2, 8):
            s = stiff[place]
            by_y = s_rows[place - 2, 7 : 7 + width] + s_rows[place - 2, 9 : 9 + width]
            by_z = to_left(at, s) + to_right(at, s)
            links_out[g, place - 2] = 3.0 * s + 0.5 * ((stiff[place - 1] + stiff[place + 1]) + by_z + by_y)


def image_of(at, stiff, rows_of_stiff, field, rows, place, before, after):
    v, s = field[place], stiff[place]
    width = at.width

    def beside(ref_and_start, first):
        ref, start = ref_and_start
        return ref[place - start, first : first + width]

    k_right = s + to_right(at, s)
    flow_z = k_right * (v - to_right(at, v))
    total = (after - before) + (flow_z - jnp.where(at.at_left, -(s * v), turn(flow_z, 1, 1)))
    s_up, s_down = beside(rows_of_stiff, 7), beside(rows_of_stiff, 9)
    v_up, v_down = beside(rows, 7), beside(rows, 9)
    return total + ((s + s_up) * (v - v_up) + (s + s_down) * (v - v_down))


def flow_x(stiff, field, place):
    return (stiff[place] + stiff[place + 1]) * (field[place] - field[place + 1])


def start_of(at, links, load, support, place):
    over = at.real[place] / jnp.maximum(links + PENALTY * support, 0.1)
    return over, load * over


def mask_strips_of(at, is_right, strip, which, parts):
    block, slot = at.wide(is_right)
    beyond = by_side(is_right, slot, WIDE - 1 - slot) < HALF
    for place, plane, source, held in parts:
        start = (place - 1) * WIDE - (held + 2 * which) * GROUP
        value = jnp.where(beyond, turn(source, start, 1), own_columns(plane, place))
        strip = jnp.where(block == place - 1, value, strip)
    return strip


def own_kernel(groups, size, *refs):
    stiff_in, links_in, own_masks, partner = refs[:4]
    z_out, w_out, q_out, over_out, masks_out, s_rows, z_rows = refs[4:]
    width, thick = stiff_in.shape[2:]
    partner_masks = partner.at[2 * width :]
    at = Spot(groups, size, width, thick)
    for ref in (s_rows, z_rows):
        border(ref, width)
    order = ((own_masks, 0), (own_masks, 1), (partner_masks, 1), (partner_masks, 0))
    load, support = (
        {place + 4: plane_of(ref, 2 * which + k, width) for place, (ref, k) in enumerate(order)} for which in (0, 1)
    )
    mine, theirs = spread(own_masks[4 * width :]), spread(partner_masks[4 * width :])
    for k, (is_right, _) in enumerate(at.sides()):
        for which, mask in enumerate((load, support)):
            sources = ((mine, 0), (mine, 1), (theirs, 1), (theirs, 0))
            parts = [(place + 4, mask[place + 4], *source) for place, source in enumerate(sources)]
            masks_out[which, k] = mask_strips_of(at, is_right, jnp.zeros(at.shape, jnp.float32), which, parts)

    for g in range(groups):
        stiff = {place: stiff_in[g, place - 2] for place in range(4, 8)}
        over, z = {}, {}
        for place in range(4, 8):
            over[place], z[place] = start_of(at, links_in[g, place - 2], load[place], support[place], place)
            z_out[g, place - 4] = z[place]
        over_out[g] = over[4]
        for place in (5, 6):
            s_rows[place - 5, 8 : 8 + width] = stiff[place]
            z_rows[place - 5, 8 : 8 + width] = z[place]
        flows = {place: flow_x(stiff, z, place) for place in (4, 5, 6)}
        for place in (5, 6):
            q = 0.5 * image_of(at, stiff, (s_rows, 5), z, (z_rows, 5), place, flows[place - 1], flows[place])
            w_out[g, place - 5] = q * over[place]
            if place == 5:
                q_out[g] = q


def near_kernel(groups, size, *refs):
    stiff_in, links_in, near_masks, z_in, w_in, q_in, over_in, masks_in = refs[:8]
    totals_out, z_out, w_out, masks_out, s_rows, z_rows, w_rows = refs[8:]
    width, thick = stiff_in.shape[2:]
    at = Spot(groups, size, width, thick)
    for ref in (s_rows, z_rows, w_rows):
        border(ref, width)
    load, support = (
        {place: plane_of(near_masks, 2 * which + 3 - place, width) for place in (2, 3)} for which in (0, 1)
    )
    nears = spread(near_masks[4 * width :])
    for k, (is_right, _) in enumerate(at.sides()):
        for which, mask in enumerate((load, support)):
            parts = [(place, mask[place], nears, 3 - place) for place in (2, 3)]
            masks_out[which, k] = mask_strips_of(at, is_right, masks_in[which, k], which, parts)

    counted = jnp.ones(at.shape, jnp.float32)
    for is_right, present in at.sides():
        counted = jnp.where(at.held(is_right), 1.0 - present, counted)

    rows_out = 0
    for g in range(groups):
        stiff = {place: stiff_in[g, place - 2] for place in range(2, 7)}
        z = {4: z_in[g, 0], 5: z_in[g, 1]}
        over = {4: over_in[g]}
        for place in (2, 3):
            over[place], z[place] = start_of(at, links_in[g, place - 2], load[place], support[place], place)
        z_out[g] = z[3]
        for place in (3, 4, 5):
            s_rows[place - 3, 8 : 8 + width] = stiff[place]
        for place in (3, 4):
            z_rows[place - 3, 8 : 8 + width] = z[place]
        flows = {place: flow_x(stiff, z, place) for place in (2, 3, 4)}
        q, w = {5: q_in[g]}, {5: w_in[g, 0], 6: w_in[g, 1]}
        for place in (3, 4):
            q[place] = 0.5 * image_of(at, stiff, (s_rows, 3), z, (z_rows, 3), place, flows[place - 1], flows[place])
            w[place] = q[place] * over[place]
            w_out[g, place - 3] = w[place]
        for place in (4, 5):
            w_rows[place - 4, 8 : 8 + width] = w[place]
        flows = {place: flow_x(stiff, w, place) for place in (3, 4, 5)}
        totals = [0.0, 0.0, 0.0, 0.0]
        for place in (4, 5):
            aw = 0.5 * image_of(at, stiff, (s_rows, 3), w, (w_rows, 4), place, flows[place - 1], flows[place])
            terms = (z[place], z[place] * q[place], q[place] * w[place], w[place] * aw)
            totals = [a + b for a, b in zip(totals, terms)]
        for total in totals:
            totals_out[rows_out : rows_out + 1] = jnp.sum(total * counted, axis=0, keepdims=True)
            rows_out += 1


def edge_kernel(groups, size, *refs):
    n_side = 1 if groups == 2 else 2
    inside, wide, masks, totals, factors, scalars = refs[:6]
    beside, crossed = refs[6 : 6 + n_side], refs[6 + n_side : 6 + 2 * n_side]
    others = refs[6 + 2 * n_side : len(refs) - 3]
    table, strip_out, factor_out = refs[len(refs) - 3 :]
    width, thick = inside.shape
    at = Spot(groups, size, width, thick)
    first, last = at.first, at.last
    two, three = RMIN - math.sqrt(2.0), RMIN - math.sqrt(3.0)

    outside = []
    for k in range(n_side):
        lower = at.layer == 1 if groups == 2 else k == 0
        group = lanes_of(beside[k].shape) // GROUP
        strip = jnp.where(group < 8, beside[k][...], spread(crossed[k][...], 8 * GROUP))
        outside.append(unfold(jnp.where(group < PLACES, strip, 0.0), lower))
    outside = [outside[0] * at.has_left, outside[-1] * at.has_right]
    fixed = at.strips(inside[...], outside)

    count_y = jnp.where(first, 0.0, 1.0) + jnp.where(last, 0.0, 1.0)
    count_x = at.real_at(at.where - 1) + at.real_at(at.where + 1)
    span_z = thick * groups
    filtered, presents, counts = [], [], []
    for k, (strip, z_at, (is_right, present)) in enumerate(zip(fixed, at.strip_z(), at.sides())):
        by_y = around_y(strip, first, last)
        once = strip + two * by_y
        twice = two * strip + three * by_y
        total = 2.0 * strip + by_y
        for step in (GROUP, -GROUP, 1, -1):
            total = total + turn(once, step, 1)
        for step in (GROUP + 1, GROUP - 1, 1 - GROUP, -1 - GROUP):
            total = total + turn(twice, step, 1)
        count_z = jnp.where(z_at >= 1, 1.0, 0.0) + jnp.where(z_at < span_z - 1, 1.0, 0.0)
        head, side = count_terms(count_y, count_z)
        total = total / (head + count_x * side)
        value = wide[k]
        block, slot = at.wide(is_right)
        better = by_side(is_right, slot, WIDE - 1 - slot) <= HALF
        for place in range(1, PLACES - 1):
            moved = turn(total, (place - 1) * WIDE - place * GROUP, 1)
            value = jnp.where(better & (block == place - 1), moved, value)
        filtered.append(value)
        z_wide = at.layer * thick + slot + by_side(is_right, -HALF, thick - WIDE + HALF)
        presents.append(jnp.where((z_wide >= 0) & (z_wide < span_z), at.real_at(block + 1), 0.0))
        own = by_side(is_right, slot, WIDE - 1 - slot)
        own = (own >= HALF) & (own < 2 * HALF) & (block >= 3) & (block < 5)
        counts.append(jnp.where(own, present, 0.0))

    def around(v):
        up, down = jnp.where(first, 0.0, turn(v, 1, 0)), jnp.where(last, 0.0, turn(v, -1, 0))
        return [turn(v, shift, 1) for shift in (WIDE, -WIDE, 1, -1)] + [up, down]

    lane_row = lanes_of((1, thick))
    line = jnp.zeros((1, thick), jnp.float32)
    for g in range(groups):
        eta, weight = weights_of(at, scalars, others, g)
        stiffness, factor = projection(eta)
        sums = [totals[4 * g + k : 4 * g + k + 1] for k in range(4)]
        patched = [factors[g, 0], factors[g, 1]]
        for k, (is_right, present) in enumerate(at.sides()):
            inner_part, value, s = stiffness(filtered[k], presents[k])
            of_place = factor(inner_part, value, weight)
            for place in (0, 1):
                here = at.held(is_right) & (present > 0.5)
                patched[place] = jnp.where(here, of_strip(of_place, place + 4), patched[place])
            beside_s = around(s)
            links = 6.0 * s + sum(beside_s[1:], beside_s[0])
            inverse = presents[k] / jnp.maximum(0.5 * links + PENALTY * masks[1, k], 0.1)
            pairs = [s + other for other in beside_s]

            def image(v):
                terms = [pair * (v - other) for pair, other in zip(pairs, around(v))]
                return 0.5 * ((terms[0] + terms[1]) + (terms[2] + terms[3]) + (terms[4] + terms[5]))

            z = masks[0, k] * inverse
            q = image(z)
            w = q * inverse
            strip_out[g, 0, k] = z
            strip_out[g, 1, k] = w
            terms = (z, z * q, q * w, w * image(w))
            sums = [a + jnp.sum(b * counts[k], axis=0, keepdims=True) for a, b in zip(sums, terms)]
        for place in (0, 1):
            factor_out[g, place] = patched[place]
        for k, part in enumerate(sums):
            line = jnp.where(lane_row == 4 * g + k, jnp.sum(part, axis=1, keepdims=True), line)
    table[...] = jnp.broadcast_to(line, table.shape)


def finish(groups, size, table, z_near, z_own, w_near, w_own, strips, factors, out):
    width, thick = out.shape[1:]
    at = Spot(groups, size, width, thick)
    core = lax.rem(at.spot, 2)
    line = jnp.sum(table[...], axis=0, keepdims=True)
    lane_row = lanes_of((1, thick))
    total = [jnp.zeros(at.shape, jnp.float32), jnp.zeros(at.shape, jnp.float32)]
    for g in range(groups):
        m0, m1, m2, m3 = (
            jnp.sum(jnp.where(lane_row == 4 * g + k, line, 0.0), axis=1, keepdims=True) for k in range(4)
        )
        step_one = m0 / m1
        rz_next = step_one * step_one * m2 - m0
        factor = rz_next / m0
        curve = (m1 - 2.0 * step_one * m2 + step_one * step_one * m3) - factor * factor * m1
        step_two = rz_next / curve
        of_z = step_one + step_two * (1.0 + factor)
        of_w = -step_one * step_two
        z = [z_near[g], z_own[g, 0], z_own[g, 1], z_own[g, 2]]
        w = [w_near[g, 0], w_near[g, 1], w_own[g, 0], w_own[g, 1]]
        u = [of_z * v + of_w * t for v, t in zip(z, w)]
        ends = {1: [0.0, 0.0], 2: [0.0, 0.0]}
        for k, (is_right, present) in enumerate(at.sides()):
            strip = of_z * strips[g, 0, k] + of_w * strips[g, 1, k]
            here = at.held(is_right) & (present > 0.5)
            for place in range(4):
                part = of_strip(strip, place + 3)
                u[place] = jnp.where(here, part, u[place])
                if place in ends:
                    if at.n_strips == 1:
                        ends[place] = [part * at.has_left, part * at.has_right]
                    else:
                        ends[place][k] = part * present
        between = [u[k] - u[k + 1] for k in range(3)]
        for k in (1, 2):
            plane = u[k]
            left = turn(jnp.where(at.at_right, ends[k][0], plane), 1, 1)
            right = turn(jnp.where(at.at_left, ends[k][1], plane), -1, 1)
            up = jnp.where(at.first, 0.0, turn(plane, 1, 0))
            down = jnp.where(at.last, 0.0, turn(plane, -1, 0))
            steps = [between[k - 1], between[k]] + [plane - other for other in (left, right, up, down)]
            squares = [v * v for v in steps]
            total[k - 1] = total[k - 1] + factors[g, k - 1] * sum(squares[1:], squares[0])
    for k in range(2):
        out[lax.rem(k + core, 2)] = total[k]


def call(body, outs, *args, scalars=(), scratch=(), flops=0):
    smem = pl.BlockSpec(memory_space=pltpu.SMEM)
    return pl.pallas_call(
        body,
        out_shape=[jax.ShapeDtypeStruct(shape, jnp.float32) for shape in outs],
        in_specs=[pl.BlockSpec(memory_space=pltpu.VMEM)] * len(args) + [smem] * len(scalars),
        out_specs=[pl.BlockSpec(memory_space=pltpu.VMEM)] * len(outs),
        scratch_shapes=[pltpu.VMEM(shape, jnp.float32) for shape in scratch],
        cost_estimate=pl.CostEstimate(flops=flops, transcendentals=0, bytes_accessed=0) if flops else None,
        compiler_params=pltpu.CompilerParams(vmem_limit_bytes=32 * 1024 * 1024),
    )(*args, *scalars)


def local(design, solid_mask, void_mask, load_mask, support_mask, thresholds, group_weight):
    depth, width, thick = design.shape
    size, groups = lax.axis_size("space"), lax.axis_size("proj")
    quarter = width // 4
    pair, near_pairs = pair_swap(size), near_swap(size)
    fixed = jnp.where(solid_mask == 1, 1.0, jnp.where(void_mask == 1, 0.0, design))
    (packed_own,) = call(
        functools.partial(prepare, groups), [(6 * width + quarter, thick)], fixed, load_mask, support_mask
    )
    partner = lax.ppermute(packed_own, "space", pair)
    own, own_masks, scalars = call(
        join, [(4 * width, thick), (4 * width + quarter, thick), (8, thick)], packed_own, partner,
        scalars=(thresholds, group_weight),
    )
    others = [lax.ppermute(scalars, "proj", [((g + k) % groups, g) for g in range(groups)]) for k in range(1, groups)]
    near = lax.ppermute(own, "space", near_pairs)
    near_masks = lax.ppermute(own_masks, "space", near_pairs)
    others = [call(keep, [other.shape], other, flops=880_000_000)[0] for other in others]
    steps = (1,) if groups == 2 else (1, -1)
    packed = call(
        functools.partial(pack, groups),
        [(width // 2, thick)] * len(steps) + [(width // 8, thick)] * len(steps),
        own, near,
    )
    straight = [(i, i) for i in range(size)]
    both = ("proj", "space")
    beside = [lax.ppermute(v, both, both_axes(straight, size, groups, k)) for k, v in zip(steps, packed)]
    crossed = [lax.ppermute(v, both, both_axes(pair, size, groups, k)) for k, v in zip(steps, packed[len(steps) :])]
    (beyond,) = call(pick, [(2 * width, thick)], near, packed[0], *others)
    inner = lax.ppermute(beyond, "space", pair)
    n_strips = 1 if groups == 2 else 2
    plane = (width, thick)
    six = (groups, 6, *plane)
    stiff, links, factors, wide, inside = call(
        functools.partial(density_kernel, groups, size),
        [six, six, (groups, 2, *plane), (n_strips, *plane), plane],
        own, near, inner, scalars, *others,
        scratch=[(PLACES, width + 16, thick), (6, width + 16, thick)],
    )
    one, two, four = (groups, *plane), (groups, 2, *plane), (groups, 4, *plane)
    strips_shape = (2, n_strips, *plane)
    z_own, w_own, q_own, over_own, mask_strips = call(
        functools.partial(own_kernel, groups, size),
        [four, two, one, one, strips_shape],
        stiff, links, own_masks, partner,
        scratch=[(2, width + 16, thick), (2, width + 16, thick)],
    )
    totals, z_near, w_near, mask_strips = call(
        functools.partial(near_kernel, groups, size),
        [(-(-4 * groups // 8) * 8, thick), one, two, strips_shape],
        stiff, links, near_masks, z_own, w_own, q_own, over_own, mask_strips,
        scratch=[(3, width + 16, thick), (2, width + 16, thick), (2, width + 16, thick)],
    )
    beside, crossed = ([call(keep, [v.shape], v, totals)[0] for v in vs] for vs in (beside, crossed))
    table, strips, factors = call(
        functools.partial(edge_kernel, groups, size),
        [(size * groups, thick), (groups, 2, n_strips, *plane), (groups, 2, *plane)],
        inside, wide, mask_strips, totals, factors, scalars, *beside, *crossed, *others,
    )
    table = lax.all_to_all(table, ("proj", "space"), 0, 0, tiled=True)
    (out,) = call(functools.partial(finish, groups, size), [(depth, *plane)], table, z_near, z_own, w_near, w_own, strips, factors)
    return out


def solution(mesh):
    placed = (
        P("space", None, "proj"),
        P("space", None, "proj"),
        P("space", None, "proj"),
        P("space", None, None),
        P("space", None, None),
        P("proj"),
        P("proj"),
    )
    return jax.shard_map(
        local, mesh=mesh, in_specs=placed, out_specs=P("space", None, "proj"), check_vma=False
    )
```

```python
import functools
import math

import jax
import jax.numpy as jnp
from jax import lax
from jax.experimental import pallas as pl
from jax.experimental.pallas import tpu as pltpu
from jax.sharding import PartitionSpec as P

RMIN = 2.0
BETA = 8.0
EMIN = 0.05
PENALTY = 4.0

PLACES = 10
GROUP = 8
HALF = GROUP // 2
WIDE = 2 * GROUP
INNER = PLACES - 2


def pair_swap(size):
    return [(i, i ^ 1) for i in range(size)]


def near_swap(size):
    ups = [(i, i + 1) for i in range(1, size - 1, 2)]
    return ups + [(j, i) for i, j in ups]


def both_axes(pairs, size, groups, step):
    return [
        (g * size + i, (g + step) % groups * size + j)
        for g in range(groups)
        for i, j in pairs
        if groups == 2 or 0 <= g + step < groups
    ]


def lanes_of(shape):
    return lax.broadcasted_iota(jnp.int32, shape, len(shape) - 1)


def turn(array, shift, axis):
    return pltpu.roll(array, shift % array.shape[axis], axis)


def squeeze(strips):
    rows, lanes = strips.shape[0] // 4, strips.shape[1]
    parts = [turn(strips[k * rows : (k + 1) * rows], k * lanes // 4, 1) for k in range(4)]
    block = lanes_of((rows, lanes)) // (lanes // 4)
    return functools.reduce(lambda out, k: jnp.where(block == k, parts[k], out), range(1, 4), parts[0])


def spread(squeezed, start=0):
    lanes = squeezed.shape[1]
    return jnp.concatenate([turn(squeezed, start - k * lanes // 4, 1) for k in range(4)], axis=0)


def prepare(groups, fixed, load, support, out):
    core = lax.rem(lax.axis_index("space"), 2)
    layer = lax.axis_index("proj")
    width, thick = load.shape[1], load.shape[2] // groups
    lane = lanes_of((width, thick))
    lower = lax.rem(lane, GROUP) < HALF
    has_left = layer > 0
    has_right = layer < groups - 1
    centre = pl.ds(pl.multiple_of(layer * thick, thick), thick)
    left = pl.ds(pl.multiple_of(jnp.maximum(layer - 1, 0) * thick, thick), thick)
    right = pl.ds(pl.multiple_of(jnp.minimum(layer + 1, groups - 1) * thick, thick), thick)
    strips = jnp.zeros((width, thick), jnp.float32)
    for place in range(2):
        plane = lax.rem(place + core, 2)
        out[place * width : (place + 1) * width] = fixed[plane]
        for which, mask in enumerate((load, support)):
            held = 2 * which + place
            out[(2 + held) * width : (3 + held) * width] = mask[plane, :, centre].astype(jnp.float32)
            before = jnp.where(has_left, mask[plane, :, left].astype(jnp.float32), 0.0)
            after = jnp.where(has_right, mask[plane, :, right].astype(jnp.float32), 0.0)
            shift = held * GROUP + HALF
            outside = jnp.where(lower, turn(before, shift, 1), turn(after, shift, 1))
            strips = jnp.where(lane // GROUP == held, outside, strips)
    out[6 * width :] = squeeze(strips)


def join(own, partner, thresholds, weights, near_out, mask_out, scalars):
    rows = near_out.shape[0] // 2
    near_out[0:rows] = own[0:rows]
    near_out[rows:] = partner[0:rows]
    mask_out[...] = own[rows:]
    row = lax.broadcasted_iota(jnp.int32, scalars.shape, 0)
    scalars[...] = jnp.where(row == 0, thresholds[0].astype(jnp.float32) / 1000.0, jnp.where(row == 1, weights[0], 0.0))


def keep(array, *refs):
    refs[-1][...] = array[...]


def pick(near, *refs):
    out = refs[-1]
    out[...] = near[0 : out.shape[0]]


def plane_of(ref, k, width):
    return ref[k * width : (k + 1) * width]


def frame_of(own, near):
    order = ((near, 2), (near, 3), (near, 1), (near, 0), (own, 0), (own, 1), (own, 3), (own, 2))
    return [plane_of(ref, k, near.shape[0] // 4) for ref, k in order]


def folded(planes, lower):
    half, lanes = planes[0].shape[0] // 2, planes[0].shape[1]
    lane = lanes_of((half, lanes))
    low, group = lax.rem(lane, GROUP) < HALF, lane // GROUP
    out = jnp.zeros((half, lanes), jnp.float32)
    for place, plane in enumerate(planes):
        start = place * GROUP + HALF
        top, bottom = turn(plane[:half], start, 1), plane[half:]
        of_lower = jnp.where(low, top, turn(bottom, start + HALF, 1))
        of_upper = jnp.where(low, turn(bottom, start - HALF, 1), top)
        out = jnp.where(group == place, jnp.where(lower, of_lower, of_upper), out)
    return out


def unfold(folded, lower):
    return jnp.concatenate([folded, jnp.where(lower, turn(folded, -HALF, 1), turn(folded, HALF, 1))], axis=0)


def pack(groups, own, near, *outs):
    planes = frame_of(own, near)
    sides = (lax.axis_index("proj") == 0,) if groups == 2 else (True, False)
    for k, lower in enumerate(sides):
        outs[k][...] = folded(planes, lower)
        outs[len(sides) + k][...] = squeeze(folded([planes[3], planes[2]], lower))


def around_y(plane, first, last):
    return jnp.where(first, 0.0, turn(plane, 1, 0)) + jnp.where(last, 0.0, turn(plane, -1, 0))


class Spot:
    def __init__(self, groups, size, width, thick):
        self.groups, self.width, self.thick = groups, width, thick
        self.spot, self.layer = lax.axis_index("space"), lax.axis_index("proj")
        core = lax.rem(self.spot, 2)
        self.shape = (width, thick)
        self.lane = lanes_of(self.shape)
        row = lax.broadcasted_iota(jnp.int32, self.shape, 0)
        self.first, self.last = row == 0, row == width - 1
        self.at_left, self.at_right = self.lane == 0, self.lane == thick - 1
        self.where = self.lane // GROUP
        self.slot = lax.rem(self.lane, GROUP)
        self.lower = self.slot < HALF
        self.near_real = jnp.where(jnp.where(core == 0, self.spot > 0, self.spot < size - 1), 1.0, 0.0)
        self.inner_real = jnp.where(jnp.where(core == 0, self.spot < size - 2, self.spot > 1), 1.0, 0.0)
        self.real = [self.near_real] * 4 + [1.0] * 4 + [self.inner_real] * 2
        self.has_left = jnp.where(self.layer > 0, 1.0, 0.0)
        self.has_right = jnp.where(self.layer < groups - 1, 1.0, 0.0)
        self.n_strips = 1 if groups == 2 else 2
        self.is_right = self.layer == 0

    def real_at(self, places):
        return jnp.where(places < 4, self.near_real, jnp.where(places < 8, 1.0, self.inner_real))

    def strips(self, inside, outside):
        right = jnp.where(self.lower, inside, outside[-1])
        left = jnp.where(self.lower, outside[0], inside)
        return [jnp.where(self.is_right, right, left)] if self.n_strips == 1 else [left, right]

    def strip_z(self):
        left, right = (self.layer * self.thick + self.slot + shift for shift in (-HALF, self.thick - HALF))
        return [jnp.where(self.is_right, right, left)] if self.n_strips == 1 else [left, right]

    def sides(self):
        if self.n_strips == 1:
            return [(self.is_right, 1.0)]
        return [(False, self.has_left), (True, self.has_right)]

    def wide(self, is_right):
        lane = lax.rem(self.lane + by_side(is_right, 0, WIDE // 2), self.thick)
        return lane // WIDE, lax.rem(lane, WIDE)

    def held(self, is_right):
        right, left = self.lane >= self.thick - HALF, self.lane < HALF
        if isinstance(is_right, bool):
            return right if is_right else left
        return jnp.where(is_right, self.lane, self.thick - 1 - self.lane) >= self.thick - HALF


def by_side(is_right, left, right):
    if isinstance(is_right, bool):
        return right if is_right else left
    return jnp.where(is_right, right, left)


def of_strip(strip, place):
    return turn(strip, -((place - 1) * WIDE + HALF), 1)


def count_terms(count_y, count_z):
    two, three = RMIN - math.sqrt(2.0), RMIN - math.sqrt(3.0)
    head = 2.0 + (count_y + count_z) + two * (count_y * count_z)
    side = 1.0 + two * (count_y + count_z) + three * (count_y * count_z)
    return head, side


def weights_of(at, packed, others, g):
    eta, weight = packed[0:1], packed[1:2]
    for k, other in enumerate(others):
        mine = lax.rem(at.layer + k + 1, at.groups) == g
        eta = jnp.where(mine, other[0:1], eta)
        weight = jnp.where(mine, other[1:2], weight)
    return eta, weight


def projection(eta):
    low = jnp.tanh(BETA * eta)
    over_bottom = 1.0 / (low + jnp.tanh(BETA * (1.0 - eta)))

    def stiffness(density, present):
        inner_part = jnp.tanh(BETA * (density - eta))
        value = (low + inner_part) * over_bottom
        return inner_part, value, (EMIN + (1.0 - EMIN) * (value * value * value)) * present

    def factor(inner_part, value, weight):
        slope = (BETA * over_bottom) * (1.0 - inner_part * inner_part)
        return (-0.5 * 3.0 * (1.0 - EMIN)) * weight * (value * value) * slope

    return stiffness, factor


def border(ref, width):
    ref[:, 0:8] = jnp.zeros((ref.shape[0], 8, ref.shape[2]), jnp.float32)
    ref[:, 8 + width :] = jnp.zeros((ref.shape[0], 8, ref.shape[2]), jnp.float32)


def to_left(at, plane):
    return jnp.where(at.at_left, 0.0, turn(plane, 1, 1))


def to_right(at, plane):
    return jnp.where(at.at_right, 0.0, turn(plane, -1, 1))


def own_columns(plane, place):
    return turn(plane, (place - 1) * WIDE + HALF, 1)


def density_kernel(groups, size, *refs):
    own, near, inner, scalars = refs[:4]
    others = refs[4 : len(refs) - 7]
    stiff_out, links_out, factor_out, wide_out, inside_out, f_rows, s_rows = refs[len(refs) - 7 :]
    width, thick = near.shape[0] // 4, near.shape[1]
    at = Spot(groups, size, width, thick)
    two, three = RMIN - math.sqrt(2.0), RMIN - math.sqrt(3.0)
    planes = frame_of(own, near) + [plane_of(inner, k, width) for k in (0, 1)]
    strip = jnp.zeros(at.shape, jnp.float32)
    for place in range(PLACES):
        strip = jnp.where(at.where == place, turn(planes[place], place * GROUP + HALF, 1), strip)
    inside_out[...] = strip
    for ref in (f_rows, s_rows):
        border(ref, width)
    for place in range(PLACES):
        f_rows[place, 8 : 8 + width] = planes[place]

    count_y = jnp.where(at.first, 0.0, 1.0) + jnp.where(at.last, 0.0, 1.0)
    places_z = at.layer * thick + at.lane
    count_z = jnp.where(places_z >= 1, 1.0, 0.0) + jnp.where(places_z < groups * thick - 1, 1.0, 0.0)
    head, side = count_terms(count_y, count_z)
    over_two, over_one = 1.0 / (head + 2.0 * side), 1.0 / (head + side)
    straight, once, twice = [], [], []
    for place in range(PLACES):
        plane = planes[place]
        by_y = f_rows[place, 7 : 7 + width] + f_rows[place, 9 : 9 + width]
        straight.append(2.0 * plane + by_y)
        once.append(plane + two * by_y)
        twice.append(two * plane + three * by_y)
    filtered = {}
    for place in range(1, PLACES - 1):
        beside = once[place] + (twice[place - 1] + twice[place + 1])
        total = straight[place] + (once[place - 1] + once[place + 1]) + (to_left(at, beside) + to_right(at, beside))
        count_x = at.real[place - 1] + at.real[place + 1]
        filtered[place] = total * jnp.where(count_x > 1.5, over_two, over_one)

    for k, (is_right, _) in enumerate(at.sides()):
        block, _ = at.wide(is_right)
        strip = jnp.zeros(at.shape, jnp.float32)
        for place in range(1, PLACES - 1):
            strip = jnp.where(block == place - 1, own_columns(filtered[place], place), strip)
        wide_out[k] = strip

    for g in range(groups):
        eta, weight = weights_of(at, scalars, others, g)
        stiffness, factor = projection(eta)
        stiff = {}
        for place in range(1, PLACES - 1):
            inner_part, value, stiff[place] = stiffness(filtered[place], at.real[place])
            if place in (4, 5):
                factor_out[g, place - 4] = factor(inner_part, value, weight)
            if 2 <= place < 8:
                s_rows[place - 2, 8 : 8 + width] = stiff[place]
                stiff_out[g, place - 2] = stiff[place]
        for place in range(2, 8):
            s = stiff[place]
            by_y = s_rows[place - 2, 7 : 7 + width] + s_rows[place - 2, 9 : 9 + width]
            by_z = to_left(at, s) + to_right(at, s)
            links_out[g, place - 2] = 3.0 * s + 0.5 * ((stiff[place - 1] + stiff[place + 1]) + by_z + by_y)


def image_of(at, stiff, rows_of_stiff, field, rows, place, before, after):
    v, s = field[place], stiff[place]
    width = at.width

    def beside(ref_and_start, first):
        ref, start = ref_and_start
        return ref[place - start, first : first + width]

    k_right = s + to_right(at, s)
    flow_z = k_right * (v - to_right(at, v))
    total = (after - before) + (flow_z - jnp.where(at.at_left, -(s * v), turn(flow_z, 1, 1)))
    s_up, s_down = beside(rows_of_stiff, 7), beside(rows_of_stiff, 9)
    v_up, v_down = beside(rows, 7), beside(rows, 9)
    return total + ((s + s_up) * (v - v_up) + (s + s_down) * (v - v_down))


def flow_x(stiff, field, place):
    return (stiff[place] + stiff[place + 1]) * (field[place] - field[place + 1])


def start_of(at, links, load, support, place):
    over = at.real[place] / jnp.maximum(links + PENALTY * support, 0.1)
    return over, load * over


def mask_strips_of(at, is_right, strip, which, parts):
    block, slot = at.wide(is_right)
    beyond = by_side(is_right, slot, WIDE - 1 - slot) < HALF
    for place, plane, source, held in parts:
        start = (place - 1) * WIDE - (held + 2 * which) * GROUP
        value = jnp.where(beyond, turn(source, start, 1), own_columns(plane, place))
        strip = jnp.where(block == place - 1, value, strip)
    return strip


def own_kernel(groups, size, *refs):
    stiff_in, links_in, own_masks, partner = refs[:4]
    z_out, w_out, q_out, over_out, masks_out, s_rows, z_rows = refs[4:]
    width, thick = stiff_in.shape[2:]
    partner_masks = partner.at[2 * width :]
    at = Spot(groups, size, width, thick)
    for ref in (s_rows, z_rows):
        border(ref, width)
    order = ((own_masks, 0), (own_masks, 1), (partner_masks, 1), (partner_masks, 0))
    load, support = (
        {place + 4: plane_of(ref, 2 * which + k, width) for place, (ref, k) in enumerate(order)} for which in (0, 1)
    )
    mine, theirs = spread(own_masks[4 * width :]), spread(partner_masks[4 * width :])
    for k, (is_right, _) in enumerate(at.sides()):
        for which, mask in enumerate((load, support)):
            sources = ((mine, 0), (mine, 1), (theirs, 1), (theirs, 0))
            parts = [(place + 4, mask[place + 4], *source) for place, source in enumerate(sources)]
            masks_out[which, k] = mask_strips_of(at, is_right, jnp.zeros(at.shape, jnp.float32), which, parts)

    for g in range(groups):
        stiff = {place: stiff_in[g, place - 2] for place in range(4, 8)}
        over, z = {}, {}
        for place in range(4, 8):
            over[place], z[place] = start_of(at, links_in[g, place - 2], load[place], support[place], place)
            z_out[g, place - 4] = z[place]
        over_out[g] = over[4]
        for place in (5, 6):
            s_rows[place - 5, 8 : 8 + width] = stiff[place]
            z_rows[place - 5, 8 : 8 + width] = z[place]
        flows = {place: flow_x(stiff, z, place) for place in (4, 5, 6)}
        for place in (5, 6):
            q = 0.5 * image_of(at, stiff, (s_rows, 5), z, (z_rows, 5), place, flows[place - 1], flows[place])
            w_out[g, place - 5] = q * over[place]
            if place == 5:
                q_out[g] = q


def near_kernel(groups, size, *refs):
    stiff_in, links_in, near_masks, z_in, w_in, q_in, over_in, masks_in = refs[:8]
    totals_out, z_out, w_out, masks_out, s_rows, z_rows, w_rows = refs[8:]
    width, thick = stiff_in.shape[2:]
    at = Spot(groups, size, width, thick)
    for ref in (s_rows, z_rows, w_rows):
        border(ref, width)
    load, support = (
        {place: plane_of(near_masks, 2 * which + 3 - place, width) for place in (2, 3)} for which in (0, 1)
    )
    nears = spread(near_masks[4 * width :])
    for k, (is_right, _) in enumerate(at.sides()):
        for which, mask in enumerate((load, support)):
            parts = [(place, mask[place], nears, 3 - place) for place in (2, 3)]
            masks_out[which, k] = mask_strips_of(at, is_right, masks_in[which, k], which, parts)

    counted = jnp.ones(at.shape, jnp.float32)
    for is_right, present in at.sides():
        counted = jnp.where(at.held(is_right), 1.0 - present, counted)

    rows_out = 0
    for g in range(groups):
        stiff = {place: stiff_in[g, place - 2] for place in range(2, 7)}
        z = {4: z_in[g, 0], 5: z_in[g, 1]}
        over = {4: over_in[g]}
        for place in (2, 3):
            over[place], z[place] = start_of(at, links_in[g, place - 2], load[place], support[place], place)
        z_out[g] = z[3]
        for place in (3, 4, 5):
            s_rows[place - 3, 8 : 8 + width] = stiff[place]
        for place in (3, 4):
            z_rows[place - 3, 8 : 8 + width] = z[place]
        flows = {place: flow_x(stiff, z, place) for place in (2, 3, 4)}
        q, w = {5: q_in[g]}, {5: w_in[g, 0], 6: w_in[g, 1]}
        for place in (3, 4):
            q[place] = 0.5 * image_of(at, stiff, (s_rows, 3), z, (z_rows, 3), place, flows[place - 1], flows[place])
            w[place] = q[place] * over[place]
            w_out[g, place - 3] = w[place]
        for place in (4, 5):
            w_rows[place - 4, 8 : 8 + width] = w[place]
        flows = {place: flow_x(stiff, w, place) for place in (3, 4, 5)}
        totals = [0.0, 0.0, 0.0, 0.0]
        for place in (4, 5):
            aw = 0.5 * image_of(at, stiff, (s_rows, 3), w, (w_rows, 4), place, flows[place - 1], flows[place])
            terms = (z[place], z[place] * q[place], q[place] * w[place], w[place] * aw)
            totals = [a + b for a, b in zip(totals, terms)]
        for total in totals:
            totals_out[rows_out : rows_out + 1] = jnp.sum(total * counted, axis=0, keepdims=True)
            rows_out += 1


def edge_kernel(groups, size, *refs):
    n_side = 1 if groups == 2 else 2
    inside, wide, masks, totals, factors, scalars = refs[:6]
    beside, crossed = refs[6 : 6 + n_side], refs[6 + n_side : 6 + 2 * n_side]
    others = refs[6 + 2 * n_side : len(refs) - 3]
    table, strip_out, factor_out = refs[len(refs) - 3 :]
    width, thick = inside.shape
    at = Spot(groups, size, width, thick)
    first, last = at.first, at.last
    two, three = RMIN - math.sqrt(2.0), RMIN - math.sqrt(3.0)

    outside = []
    for k in range(n_side):
        lower = at.layer == 1 if groups == 2 else k == 0
        group = lanes_of(beside[k].shape) // GROUP
        strip = jnp.where(group < 8, beside[k][...], spread(crossed[k][...], 8 * GROUP))
        outside.append(unfold(jnp.where(group < PLACES, strip, 0.0), lower))
    outside = [outside[0] * at.has_left, outside[-1] * at.has_right]
    fixed = at.strips(inside[...], outside)

    count_y = jnp.where(first, 0.0, 1.0) + jnp.where(last, 0.0, 1.0)
    count_x = at.real_at(at.where - 1) + at.real_at(at.where + 1)
    span_z = thick * groups
    filtered, presents, counts = [], [], []
    for k, (strip, z_at, (is_right, present)) in enumerate(zip(fixed, at.strip_z(), at.sides())):
        by_y = around_y(strip, first, last)
        once = strip + two * by_y
        twice = two * strip + three * by_y
        total = 2.0 * strip + by_y
        for step in (GROUP, -GROUP, 1, -1):
            total = total + turn(once, step, 1)
        for step in (GROUP + 1, GROUP - 1, 1 - GROUP, -1 - GROUP):
            total = total + turn(twice, step, 1)
        count_z = jnp.where(z_at >= 1, 1.0, 0.0) + jnp.where(z_at < span_z - 1, 1.0, 0.0)
        head, side = count_terms(count_y, count_z)
        total = total / (head + count_x * side)
        value = wide[k]
        block, slot = at.wide(is_right)
        better = by_side(is_right, slot, WIDE - 1 - slot) <= HALF
        for place in range(1, PLACES - 1):
            moved = turn(total, (place - 1) * WIDE - place * GROUP, 1)
            value = jnp.where(better & (block == place - 1), moved, value)
        filtered.append(value)
        z_wide = at.layer * thick + slot + by_side(is_right, -HALF, thick - WIDE + HALF)
        presents.append(jnp.where((z_wide >= 0) & (z_wide < span_z), at.real_at(block + 1), 0.0))
        own = by_side(is_right, slot, WIDE - 1 - slot)
        own = (own >= HALF) & (own < 2 * HALF) & (block >= 3) & (block < 5)
        counts.append(jnp.where(own, present, 0.0))

    def around(v):
        up, down = jnp.where(first, 0.0, turn(v, 1, 0)), jnp.where(last, 0.0, turn(v, -1, 0))
        return [turn(v, shift, 1) for shift in (WIDE, -WIDE, 1, -1)] + [up, down]

    lane_row = lanes_of((1, thick))
    line = jnp.zeros((1, thick), jnp.float32)
    for g in range(groups):
        eta, weight = weights_of(at, scalars, others, g)
        stiffness, factor = projection(eta)
        sums = [totals[4 * g + k : 4 * g + k + 1] for k in range(4)]
        patched = [factors[g, 0], factors[g, 1]]
        for k, (is_right, present) in enumerate(at.sides()):
            inner_part, value, s = stiffness(filtered[k], presents[k])
            of_place = factor(inner_part, value, weight)
            for place in (0, 1):
                here = at.held(is_right) & (present > 0.5)
                patched[place] = jnp.where(here, of_strip(of_place, place + 4), patched[place])
            beside_s = around(s)
            links = 6.0 * s + sum(beside_s[1:], beside_s[0])
            inverse = presents[k] / jnp.maximum(0.5 * links + PENALTY * masks[1, k], 0.1)
            pairs = [s + other for other in beside_s]

            def image(v):
                terms = [pair * (v - other) for pair, other in zip(pairs, around(v))]
                return 0.5 * ((terms[0] + terms[1]) + (terms[2] + terms[3]) + (terms[4] + terms[5]))

            z = masks[0, k] * inverse
            q = image(z)
            w = q * inverse
            strip_out[g, 0, k] = z
            strip_out[g, 1, k] = w
            terms = (z, z * q, q * w, w * image(w))
            sums = [a + jnp.sum(b * counts[k], axis=0, keepdims=True) for a, b in zip(sums, terms)]
        for place in (0, 1):
            factor_out[g, place] = patched[place]
        for k, part in enumerate(sums):
            line = jnp.where(lane_row == 4 * g + k, jnp.sum(part, axis=1, keepdims=True), line)
    table[...] = jnp.broadcast_to(line, table.shape)


def finish(groups, size, table, z_near, z_own, w_near, w_own, strips, factors, out):
    width, thick = out.shape[1:]
    at = Spot(groups, size, width, thick)
    core = lax.rem(at.spot, 2)
    line = jnp.sum(table[...], axis=0, keepdims=True)
    lane_row = lanes_of((1, thick))
    total = [jnp.zeros(at.shape, jnp.float32), jnp.zeros(at.shape, jnp.float32)]
    for g in range(groups):
        m0, m1, m2, m3 = (
            jnp.sum(jnp.where(lane_row == 4 * g + k, line, 0.0), axis=1, keepdims=True) for k in range(4)
        )
        step_one = m0 / m1
        rz_next = step_one * step_one * m2 - m0
        factor = rz_next / m0
        curve = (m1 - 2.0 * step_one * m2 + step_one * step_one * m3) - factor * factor * m1
        step_two = rz_next / curve
        of_z = step_one + step_two * (1.0 + factor)
        of_w = -step_one * step_two
        z = [z_near[g], z_own[g, 0], z_own[g, 1], z_own[g, 2]]
        w = [w_near[g, 0], w_near[g, 1], w_own[g, 0], w_own[g, 1]]
        u = [of_z * v + of_w * t for v, t in zip(z, w)]
        ends = {1: [0.0, 0.0], 2: [0.0, 0.0]}
        for k, (is_right, present) in enumerate(at.sides()):
            strip = of_z * strips[g, 0, k] + of_w * strips[g, 1, k]
            here = at.held(is_right) & (present > 0.5)
            for place in range(4):
                part = of_strip(strip, place + 3)
                u[place] = jnp.where(here, part, u[place])
                if place in ends:
                    if at.n_strips == 1:
                        ends[place] = [part * at.has_left, part * at.has_right]
                    else:
                        ends[place][k] = part * present
        between = [u[k] - u[k + 1] for k in range(3)]
        for k in (1, 2):
            plane = u[k]
            left = turn(jnp.where(at.at_right, ends[k][0], plane), 1, 1)
            right = turn(jnp.where(at.at_left, ends[k][1], plane), -1, 1)
            up = jnp.where(at.first, 0.0, turn(plane, 1, 0))
            down = jnp.where(at.last, 0.0, turn(plane, -1, 0))
            steps = [between[k - 1], between[k]] + [plane - other for other in (left, right, up, down)]
            squares = [v * v for v in steps]
            total[k - 1] = total[k - 1] + factors[g, k - 1] * sum(squares[1:], squares[0])
    for k in range(2):
        out[lax.rem(k + core, 2)] = total[k]


def call(body, outs, *args, scalars=(), scratch=(), flops=0):
    smem = pl.BlockSpec(memory_space=pltpu.SMEM)
    return pl.pallas_call(
        body,
        out_shape=[jax.ShapeDtypeStruct(shape, jnp.float32) for shape in outs],
        in_specs=[pl.BlockSpec(memory_space=pltpu.VMEM)] * len(args) + [smem] * len(scalars),
        out_specs=[pl.BlockSpec(memory_space=pltpu.VMEM)] * len(outs),
        scratch_shapes=[pltpu.VMEM(shape, jnp.float32) for shape in scratch],
        cost_estimate=pl.CostEstimate(flops=flops, transcendentals=0, bytes_accessed=0) if flops else None,
        compiler_params=pltpu.CompilerParams(vmem_limit_bytes=32 * 1024 * 1024),
    )(*args, *scalars)


def local(design, solid_mask, void_mask, load_mask, support_mask, thresholds, group_weight):
    depth, width, thick = design.shape
    size, groups = lax.axis_size("space"), lax.axis_size("proj")
    quarter = width // 4
    pair, near_pairs = pair_swap(size), near_swap(size)
    fixed = jnp.where(solid_mask == 1, 1.0, jnp.where(void_mask == 1, 0.0, design))
    (packed_own,) = call(
        functools.partial(prepare, groups), [(6 * width + quarter, thick)], fixed, load_mask, support_mask
    )
    partner = lax.ppermute(packed_own, "space", pair)
    own, own_masks, scalars = call(
        join, [(4 * width, thick), (4 * width + quarter, thick), (8, thick)], packed_own, partner,
        scalars=(thresholds, group_weight),
    )
    others = [lax.ppermute(scalars, "proj", [((g + k) % groups, g) for g in range(groups)]) for k in range(1, groups)]
    near = lax.ppermute(own, "space", near_pairs)
    near_masks = lax.ppermute(own_masks, "space", near_pairs)
    others = [call(keep, [other.shape], other, flops=1_650_000_000)[0] for other in others]
    steps = (1,) if groups == 2 else (1, -1)
    packed = call(
        functools.partial(pack, groups),
        [(width // 2, thick)] * len(steps) + [(width // 8, thick)] * len(steps),
        own, near,
    )
    straight = [(i, i) for i in range(size)]
    both = ("proj", "space")
    beside = [lax.ppermute(v, both, both_axes(straight, size, groups, k)) for k, v in zip(steps, packed)]
    crossed = [lax.ppermute(v, both, both_axes(pair, size, groups, k)) for k, v in zip(steps, packed[len(steps) :])]
    (beyond,) = call(pick, [(2 * width, thick)], near, packed[0])
    inner = lax.ppermute(beyond, "space", pair)
    n_strips = 1 if groups == 2 else 2
    plane = (width, thick)
    six = (groups, 6, *plane)
    stiff, links, factors, wide, inside = call(
        functools.partial(density_kernel, groups, size),
        [six, six, (groups, 2, *plane), (n_strips, *plane), plane],
        own, near, inner, scalars, *others,
        flops=1,
        scratch=[(PLACES, width + 16, thick), (6, width + 16, thick)],
    )
    one, two, four = (groups, *plane), (groups, 2, *plane), (groups, 4, *plane)
    strips_shape = (2, n_strips, *plane)
    z_own, w_own, q_own, over_own, mask_strips = call(
        functools.partial(own_kernel, groups, size),
        [four, two, one, one, strips_shape],
        stiff, links, own_masks, partner,
        flops=1,
        scratch=[(2, width + 16, thick), (2, width + 16, thick)],
    )
    totals, z_near, w_near, mask_strips = call(
        functools.partial(near_kernel, groups, size),
        [(-(-4 * groups // 8) * 8, thick), one, two, strips_shape],
        stiff, links, near_masks, z_own, w_own, q_own, over_own, mask_strips,
        flops=1,
        scratch=[(3, width + 16, thick), (2, width + 16, thick), (2, width + 16, thick)],
    )
    beside, crossed = ([call(keep, [v.shape], v, totals)[0] for v in vs] for vs in (beside, crossed))
    table, strips, factors = call(
        functools.partial(edge_kernel, groups, size),
        [(size * groups, thick), (groups, 2, n_strips, *plane), (groups, 2, *plane)],
        inside, wide, mask_strips, totals, factors, scalars, *beside, *crossed, *others,
    )
    table = lax.all_to_all(table, ("proj", "space"), 0, 0, tiled=True)
    (out,) = call(functools.partial(finish, groups, size), [(depth, *plane)], table, z_near, z_own, w_near, w_own, strips, factors)
    return out


def solution(mesh):
    placed = (
        P("space", None, "proj"),
        P("space", None, "proj"),
        P("space", None, "proj"),
        P("space", None, None),
        P("space", None, None),
        P("proj"),
        P("proj"),
    )
    return jax.shard_map(
        local, mesh=mesh, in_specs=placed, out_specs=P("space", None, "proj"), check_vma=False
    )
```

```python
import functools
import math

import jax
import jax.numpy as jnp
from jax import lax
from jax.experimental import pallas as pl
from jax.experimental.pallas import tpu as pltpu
from jax.sharding import PartitionSpec as P

RMIN = 2.0
BETA = 8.0
EMIN = 0.05
PENALTY = 4.0

PLACES = 10
GROUP = 8
HALF = GROUP // 2
WIDE = 2 * GROUP
INNER = PLACES - 2


def pair_swap(size):
    return [(i, i ^ 1) for i in range(size)]


def near_swap(size):
    ups = [(i, i + 1) for i in range(1, size - 1, 2)]
    return ups + [(j, i) for i, j in ups]


def both_axes(pairs, size, groups, step):
    return [
        (g * size + i, (g + step) % groups * size + j)
        for g in range(groups)
        for i, j in pairs
        if groups == 2 or 0 <= g + step < groups
    ]


def lanes_of(shape):
    return lax.broadcasted_iota(jnp.int32, shape, len(shape) - 1)


def turn(array, shift, axis):
    return pltpu.roll(array, shift % array.shape[axis], axis)


def squeeze(strips):
    rows, lanes = strips.shape[0] // 4, strips.shape[1]
    parts = [turn(strips[k * rows : (k + 1) * rows], k * lanes // 4, 1) for k in range(4)]
    block = lanes_of((rows, lanes)) // (lanes // 4)
    return functools.reduce(lambda out, k: jnp.where(block == k, parts[k], out), range(1, 4), parts[0])


def spread(squeezed, start=0):
    lanes = squeezed.shape[1]
    return jnp.concatenate([turn(squeezed, start - k * lanes // 4, 1) for k in range(4)], axis=0)


def prepare(groups, fixed, load, support, out):
    core = lax.rem(lax.axis_index("space"), 2)
    layer = lax.axis_index("proj")
    width, thick = load.shape[1], load.shape[2] // groups
    lane = lanes_of((width, thick))
    lower = lax.rem(lane, GROUP) < HALF
    has_left = layer > 0
    has_right = layer < groups - 1
    centre = pl.ds(pl.multiple_of(layer * thick, thick), thick)
    left = pl.ds(pl.multiple_of(jnp.maximum(layer - 1, 0) * thick, thick), thick)
    right = pl.ds(pl.multiple_of(jnp.minimum(layer + 1, groups - 1) * thick, thick), thick)
    strips = jnp.zeros((width, thick), jnp.float32)
    for place in range(2):
        plane = lax.rem(place + core, 2)
        out[place * width : (place + 1) * width] = fixed[plane]
        for which, mask in enumerate((load, support)):
            held = 2 * which + place
            out[(2 + held) * width : (3 + held) * width] = mask[plane, :, centre].astype(jnp.float32)
            before = jnp.where(has_left, mask[plane, :, left].astype(jnp.float32), 0.0)
            after = jnp.where(has_right, mask[plane, :, right].astype(jnp.float32), 0.0)
            shift = held * GROUP + HALF
            outside = jnp.where(lower, turn(before, shift, 1), turn(after, shift, 1))
            strips = jnp.where(lane // GROUP == held, outside, strips)
    out[6 * width :] = squeeze(strips)


def join(own, partner, thresholds, weights, near_out, mask_out, scalars):
    rows = near_out.shape[0] // 2
    near_out[0:rows] = own[0:rows]
    near_out[rows:] = partner[0:rows]
    mask_out[...] = own[rows:]
    row = lax.broadcasted_iota(jnp.int32, scalars.shape, 0)
    scalars[...] = jnp.where(row == 0, thresholds[0].astype(jnp.float32) / 1000.0, jnp.where(row == 1, weights[0], 0.0))


def keep(array, *refs):
    refs[-1][...] = array[...]


def pick(near, *refs):
    out = refs[-1]
    out[...] = near[0 : out.shape[0]]


def plane_of(ref, k, width):
    return ref[k * width : (k + 1) * width]


def frame_of(own, near):
    order = ((near, 2), (near, 3), (near, 1), (near, 0), (own, 0), (own, 1), (own, 3), (own, 2))
    return [plane_of(ref, k, near.shape[0] // 4) for ref, k in order]


def folded(planes, lower):
    half, lanes = planes[0].shape[0] // 2, planes[0].shape[1]
    lane = lanes_of((half, lanes))
    low, group = lax.rem(lane, GROUP) < HALF, lane // GROUP
    out = jnp.zeros((half, lanes), jnp.float32)
    for place, plane in enumerate(planes):
        start = place * GROUP + HALF
        top, bottom = turn(plane[:half], start, 1), plane[half:]
        of_lower = jnp.where(low, top, turn(bottom, start + HALF, 1))
        of_upper = jnp.where(low, turn(bottom, start - HALF, 1), top)
        out = jnp.where(group == place, jnp.where(lower, of_lower, of_upper), out)
    return out


def unfold(folded, lower):
    return jnp.concatenate([folded, jnp.where(lower, turn(folded, -HALF, 1), turn(folded, HALF, 1))], axis=0)


def pack(groups, own, near, *outs):
    planes = frame_of(own, near)
    sides = (lax.axis_index("proj") == 0,) if groups == 2 else (True, False)
    for k, lower in enumerate(sides):
        outs[k][...] = folded(planes, lower)
        outs[len(sides) + k][...] = squeeze(folded([planes[3], planes[2]], lower))


def around_y(plane, first, last):
    return jnp.where(first, 0.0, turn(plane, 1, 0)) + jnp.where(last, 0.0, turn(plane, -1, 0))


class Spot:
    def __init__(self, groups, size, width, thick):
        self.groups, self.width, self.thick = groups, width, thick
        self.spot, self.layer = lax.axis_index("space"), lax.axis_index("proj")
        core = lax.rem(self.spot, 2)
        self.shape = (width, thick)
        self.lane = lanes_of(self.shape)
        row = lax.broadcasted_iota(jnp.int32, self.shape, 0)
        self.first, self.last = row == 0, row == width - 1
        self.at_left, self.at_right = self.lane == 0, self.lane == thick - 1
        self.where = self.lane // GROUP
        self.slot = lax.rem(self.lane, GROUP)
        self.lower = self.slot < HALF
        self.near_real = jnp.where(jnp.where(core == 0, self.spot > 0, self.spot < size - 1), 1.0, 0.0)
        self.inner_real = jnp.where(jnp.where(core == 0, self.spot < size - 2, self.spot > 1), 1.0, 0.0)
        self.real = [self.near_real] * 4 + [1.0] * 4 + [self.inner_real] * 2
        self.has_left = jnp.where(self.layer > 0, 1.0, 0.0)
        self.has_right = jnp.where(self.layer < groups - 1, 1.0, 0.0)
        self.n_strips = 1 if groups == 2 else 2
        self.is_right = self.layer == 0

    def real_at(self, places):
        return jnp.where(places < 4, self.near_real, jnp.where(places < 8, 1.0, self.inner_real))

    def strips(self, inside, outside):
        right = jnp.where(self.lower, inside, outside[-1])
        left = jnp.where(self.lower, outside[0], inside)
        return [jnp.where(self.is_right, right, left)] if self.n_strips == 1 else [left, right]

    def strip_z(self):
        left, right = (self.layer * self.thick + self.slot + shift for shift in (-HALF, self.thick - HALF))
        return [jnp.where(self.is_right, right, left)] if self.n_strips == 1 else [left, right]

    def sides(self):
        if self.n_strips == 1:
            return [(self.is_right, 1.0)]
        return [(False, self.has_left), (True, self.has_right)]

    def wide(self, is_right):
        lane = lax.rem(self.lane + by_side(is_right, 0, WIDE // 2), self.thick)
        return lane // WIDE, lax.rem(lane, WIDE)

    def counted(self):
        counted = jnp.ones(self.shape, jnp.float32)
        for is_right, present in self.sides():
            counted = jnp.where(self.held(is_right), 1.0 - present, counted)
        return counted

    def held(self, is_right):
        right, left = self.lane >= self.thick - HALF, self.lane < HALF
        if isinstance(is_right, bool):
            return right if is_right else left
        return jnp.where(is_right, self.lane, self.thick - 1 - self.lane) >= self.thick - HALF


def by_side(is_right, left, right):
    if isinstance(is_right, bool):
        return right if is_right else left
    return jnp.where(is_right, right, left)


def of_strip(strip, place):
    return turn(strip, -((place - 1) * WIDE + HALF), 1)


def count_terms(count_y, count_z):
    two, three = RMIN - math.sqrt(2.0), RMIN - math.sqrt(3.0)
    head = 2.0 + (count_y + count_z) + two * (count_y * count_z)
    side = 1.0 + two * (count_y + count_z) + three * (count_y * count_z)
    return head, side


def weights_of(at, packed, others, g):
    eta, weight = packed[0:1], packed[1:2]
    for k, other in enumerate(others):
        mine = lax.rem(at.layer + k + 1, at.groups) == g
        eta = jnp.where(mine, other[0:1], eta)
        weight = jnp.where(mine, other[1:2], weight)
    return eta, weight


def projection(eta):
    low = jnp.tanh(BETA * eta)
    over_bottom = 1.0 / (low + jnp.tanh(BETA * (1.0 - eta)))

    def stiffness(density, present):
        inner_part = jnp.tanh(BETA * (density - eta))
        value = (low + inner_part) * over_bottom
        return inner_part, value, (EMIN + (1.0 - EMIN) * (value * value * value)) * present

    def factor(inner_part, value, weight):
        slope = (BETA * over_bottom) * (1.0 - inner_part * inner_part)
        return (-0.5 * 3.0 * (1.0 - EMIN)) * weight * (value * value) * slope

    return stiffness, factor


def border(ref, width):
    ref[:, 0:8] = jnp.zeros((ref.shape[0], 8, ref.shape[2]), jnp.float32)
    ref[:, 8 + width :] = jnp.zeros((ref.shape[0], 8, ref.shape[2]), jnp.float32)


def to_left(at, plane):
    return jnp.where(at.at_left, 0.0, turn(plane, 1, 1))


def to_right(at, plane):
    return jnp.where(at.at_right, 0.0, turn(plane, -1, 1))


def own_columns(plane, place):
    return turn(plane, (place - 1) * WIDE + HALF, 1)


def density_kernel(groups, size, *refs):
    own, near, inner, scalars = refs[:4]
    others = refs[4 : len(refs) - 7]
    stiff_out, links_out, factor_out, wide_out, inside_out, f_rows, s_rows = refs[len(refs) - 7 :]
    width, thick = near.shape[0] // 4, near.shape[1]
    at = Spot(groups, size, width, thick)
    two, three = RMIN - math.sqrt(2.0), RMIN - math.sqrt(3.0)
    planes = frame_of(own, near) + [plane_of(inner, k, width) for k in (0, 1)]
    strip = jnp.zeros(at.shape, jnp.float32)
    for place in range(PLACES):
        strip = jnp.where(at.where == place, turn(planes[place], place * GROUP + HALF, 1), strip)
    inside_out[...] = strip
    for ref in (f_rows, s_rows):
        border(ref, width)
    for place in range(PLACES):
        f_rows[place, 8 : 8 + width] = planes[place]

    count_y = jnp.where(at.first, 0.0, 1.0) + jnp.where(at.last, 0.0, 1.0)
    places_z = at.layer * thick + at.lane
    count_z = jnp.where(places_z >= 1, 1.0, 0.0) + jnp.where(places_z < groups * thick - 1, 1.0, 0.0)
    head, side = count_terms(count_y, count_z)
    over_two, over_one = 1.0 / (head + 2.0 * side), 1.0 / (head + side)
    straight, once, twice = [], [], []
    for place in range(PLACES):
        plane = planes[place]
        by_y = f_rows[place, 7 : 7 + width] + f_rows[place, 9 : 9 + width]
        straight.append(2.0 * plane + by_y)
        once.append(plane + two * by_y)
        twice.append(two * plane + three * by_y)
    filtered = {}
    for place in range(1, PLACES - 1):
        beside = once[place] + (twice[place - 1] + twice[place + 1])
        total = straight[place] + (once[place - 1] + once[place + 1]) + (to_left(at, beside) + to_right(at, beside))
        count_x = at.real[place - 1] + at.real[place + 1]
        filtered[place] = total * jnp.where(count_x > 1.5, over_two, over_one)

    for k, (is_right, _) in enumerate(at.sides()):
        block, _ = at.wide(is_right)
        strip = jnp.zeros(at.shape, jnp.float32)
        for place in range(1, PLACES - 1):
            strip = jnp.where(block == place - 1, own_columns(filtered[place], place), strip)
        wide_out[k] = strip

    for g in range(groups):
        eta, weight = weights_of(at, scalars, others, g)
        stiffness, factor = projection(eta)
        stiff = {}
        for place in range(1, PLACES - 1):
            inner_part, value, stiff[place] = stiffness(filtered[place], at.real[place])
            if place in (4, 5):
                factor_out[g, place - 4] = factor(inner_part, value, weight)
            if 2 <= place < 8:
                s_rows[place - 2, 8 : 8 + width] = stiff[place]
                stiff_out[g, place - 2] = stiff[place]
        for place in range(2, 8):
            s = stiff[place]
            by_y = s_rows[place - 2, 7 : 7 + width] + s_rows[place - 2, 9 : 9 + width]
            by_z = to_left(at, s) + to_right(at, s)
            links_out[g, place - 2] = 3.0 * s + 0.5 * ((stiff[place - 1] + stiff[place + 1]) + by_z + by_y)


def image_of(at, stiff, rows_of_stiff, field, rows, place, before, after):
    v, s = field[place], stiff[place]
    width = at.width

    def beside(ref_and_start, first):
        ref, start = ref_and_start
        return ref[place - start, first : first + width]

    k_right = s + to_right(at, s)
    flow_z = k_right * (v - to_right(at, v))
    total = (after - before) + (flow_z - jnp.where(at.at_left, -(s * v), turn(flow_z, 1, 1)))
    s_up, s_down = beside(rows_of_stiff, 7), beside(rows_of_stiff, 9)
    v_up, v_down = beside(rows, 7), beside(rows, 9)
    return total + ((s + s_up) * (v - v_up) + (s + s_down) * (v - v_down))


def flow_x(stiff, field, place):
    return (stiff[place] + stiff[place + 1]) * (field[place] - field[place + 1])


def start_of(at, links, load, support, place):
    over = at.real[place] / jnp.maximum(links + PENALTY * support, 0.1)
    return over, load * over


def mask_strips_of(at, is_right, strip, which, parts):
    block, slot = at.wide(is_right)
    beyond = by_side(is_right, slot, WIDE - 1 - slot) < HALF
    for place, plane, source, held in parts:
        start = (place - 1) * WIDE - (held + 2 * which) * GROUP
        value = jnp.where(beyond, turn(source, start, 1), own_columns(plane, place))
        strip = jnp.where(block == place - 1, value, strip)
    return strip


def own_kernel(groups, size, *refs):
    stiff_in, links_in, own_masks, partner = refs[:4]
    z_out, w_out, q_out, over_out, totals_out, masks_out, s_rows, z_rows, w_rows = refs[4:]
    width, thick = stiff_in.shape[2:]
    partner_masks = partner.at[2 * width :]
    at = Spot(groups, size, width, thick)
    for ref in (s_rows, z_rows, w_rows):
        border(ref, width)
    order = ((own_masks, 0), (own_masks, 1), (partner_masks, 1), (partner_masks, 0))
    load, support = (
        {place + 4: plane_of(ref, 2 * which + k, width) for place, (ref, k) in enumerate(order)} for which in (0, 1)
    )
    mine, theirs = spread(own_masks[4 * width :]), spread(partner_masks[4 * width :])
    for k, (is_right, _) in enumerate(at.sides()):
        for which, mask in enumerate((load, support)):
            sources = ((mine, 0), (mine, 1), (theirs, 1), (theirs, 0))
            parts = [(place + 4, mask[place + 4], *source) for place, source in enumerate(sources)]
            masks_out[which, k] = mask_strips_of(at, is_right, jnp.zeros(at.shape, jnp.float32), which, parts)

    counted = at.counted()
    for g in range(groups):
        stiff = {place: stiff_in[g, place - 2] for place in range(4, 8)}
        over, z = {}, {}
        for place in range(4, 8):
            over[place], z[place] = start_of(at, links_in[g, place - 2], load[place], support[place], place)
            z_out[g, place - 4] = z[place]
        over_out[g] = over[4]
        for place in (4, 5, 6):
            s_rows[place - 4, 8 : 8 + width] = stiff[place]
            z_rows[place - 4, 8 : 8 + width] = z[place]
        flows = {3: 0.0} | {place: flow_x(stiff, z, place) for place in (4, 5, 6)}
        q, w = {}, {}
        for place in (4, 5, 6):
            q[place] = 0.5 * image_of(at, stiff, (s_rows, 4), z, (z_rows, 4), place, flows[place - 1], flows[place])
        for place in (5, 6):
            w[place] = q[place] * over[place]
            w_out[g, place - 5] = w[place]
        q_out[g] = q[4]
        w_rows[0, 8 : 8 + width] = w[5]
        aw = 0.5 * image_of(at, stiff, (s_rows, 4), w, (w_rows, 5), 5, 0.0, flow_x(stiff, w, 5))
        terms = (z[4] + z[5], z[5] * q[5], q[5] * w[5], w[5] * aw)
        for k, term in enumerate(terms):
            totals_out[4 * g + k : 4 * g + k + 1] = jnp.sum(term * counted, axis=0, keepdims=True)


def near_kernel(groups, size, *refs):
    stiff_in, links_in, near_masks, z_in, w_in, q_in, over_in, totals_in, masks_in = refs[:9]
    totals_out, z_out, w_out, masks_out, s_rows, z_rows, w_rows = refs[9:]
    width, thick = stiff_in.shape[2:]
    at = Spot(groups, size, width, thick)
    for ref in (s_rows, z_rows, w_rows):
        border(ref, width)
    load, support = (
        {place: plane_of(near_masks, 2 * which + 3 - place, width) for place in (2, 3)} for which in (0, 1)
    )
    nears = spread(near_masks[4 * width :])
    for k, (is_right, _) in enumerate(at.sides()):
        for which, mask in enumerate((load, support)):
            parts = [(place, mask[place], nears, 3 - place) for place in (2, 3)]
            masks_out[which, k] = mask_strips_of(at, is_right, masks_in[which, k], which, parts)

    counted = at.counted()
    for g in range(groups):
        stiff = {place: stiff_in[g, place - 2] for place in range(2, 6)}
        z = {4: z_in[g, 0]}
        over = {4: over_in[g]}
        for place in (2, 3):
            over[place], z[place] = start_of(at, links_in[g, place - 2], load[place], support[place], place)
        z_out[g] = z[3]
        for place in (3, 4):
            s_rows[place - 3, 8 : 8 + width] = stiff[place]
        z_rows[0, 8 : 8 + width] = z[3]
        flows = {place: flow_x(stiff, z, place) for place in (2, 3)}
        q = 0.5 * image_of(at, stiff, (s_rows, 3), z, (z_rows, 3), 3, flows[2], flows[3])
        q = {3: q, 4: q_in[g] - 0.5 * flows[3]}
        w = {place: q[place] * over[place] for place in (3, 4)} | {5: w_in[g, 0]}
        for place in (3, 4):
            w_out[g, place - 3] = w[place]
        w_rows[0, 8 : 8 + width] = w[4]
        flows = {place: flow_x(stiff, w, place) for place in (3, 4)}
        aw = 0.5 * image_of(at, stiff, (s_rows, 3), w, (w_rows, 4), 4, flows[3], flows[4])
        terms = (None, z[4] * q[4], q[4] * w[4], w[4] * aw - w[5] * (0.5 * flows[4]))
        for k, term in enumerate(terms):
            row = totals_in[4 * g + k : 4 * g + k + 1]
            if term is not None:
                row = row + jnp.sum(term * counted, axis=0, keepdims=True)
            totals_out[4 * g + k : 4 * g + k + 1] = row


def edge_kernel(groups, size, *refs):
    n_side = 1 if groups == 2 else 2
    inside, wide, masks, totals, factors, scalars = refs[:6]
    beside, crossed = refs[6 : 6 + n_side], refs[6 + n_side : 6 + 2 * n_side]
    others = refs[6 + 2 * n_side : len(refs) - 3]
    table, strip_out, factor_out = refs[len(refs) - 3 :]
    width, thick = inside.shape
    at = Spot(groups, size, width, thick)
    first, last = at.first, at.last
    two, three = RMIN - math.sqrt(2.0), RMIN - math.sqrt(3.0)

    outside = []
    for k in range(n_side):
        lower = at.layer == 1 if groups == 2 else k == 0
        group = lanes_of(beside[k].shape) // GROUP
        strip = jnp.where(group < 8, beside[k][...], spread(crossed[k][...], 8 * GROUP))
        outside.append(unfold(jnp.where(group < PLACES, strip, 0.0), lower))
    outside = [outside[0] * at.has_left, outside[-1] * at.has_right]
    fixed = at.strips(inside[...], outside)

    count_y = jnp.where(first, 0.0, 1.0) + jnp.where(last, 0.0, 1.0)
    count_x = at.real_at(at.where - 1) + at.real_at(at.where + 1)
    span_z = thick * groups
    filtered, presents, counts = [], [], []
    for k, (strip, z_at, (is_right, present)) in enumerate(zip(fixed, at.strip_z(), at.sides())):
        by_y = around_y(strip, first, last)
        once = strip + two * by_y
        twice = two * strip + three * by_y
        total = 2.0 * strip + by_y
        for step in (GROUP, -GROUP, 1, -1):
            total = total + turn(once, step, 1)
        for step in (GROUP + 1, GROUP - 1, 1 - GROUP, -1 - GROUP):
            total = total + turn(twice, step, 1)
        count_z = jnp.where(z_at >= 1, 1.0, 0.0) + jnp.where(z_at < span_z - 1, 1.0, 0.0)
        head, side = count_terms(count_y, count_z)
        total = total / (head + count_x * side)
        value = wide[k]
        block, slot = at.wide(is_right)
        better = by_side(is_right, slot, WIDE - 1 - slot) <= HALF
        for place in range(1, PLACES - 1):
            moved = turn(total, (place - 1) * WIDE - place * GROUP, 1)
            value = jnp.where(better & (block == place - 1), moved, value)
        filtered.append(value)
        z_wide = at.layer * thick + slot + by_side(is_right, -HALF, thick - WIDE + HALF)
        presents.append(jnp.where((z_wide >= 0) & (z_wide < span_z), at.real_at(block + 1), 0.0))
        own = by_side(is_right, slot, WIDE - 1 - slot)
        own = (own >= HALF) & (own < 2 * HALF) & (block >= 3) & (block < 5)
        counts.append(jnp.where(own, present, 0.0))

    def around(v):
        up, down = jnp.where(first, 0.0, turn(v, 1, 0)), jnp.where(last, 0.0, turn(v, -1, 0))
        return [turn(v, shift, 1) for shift in (WIDE, -WIDE, 1, -1)] + [up, down]

    lane_row = lanes_of((1, thick))
    line = jnp.zeros((1, thick), jnp.float32)
    for g in range(groups):
        eta, weight = weights_of(at, scalars, others, g)
        stiffness, factor = projection(eta)
        sums = [totals[4 * g + k : 4 * g + k + 1] for k in range(4)]
        patched = [factors[g, 0], factors[g, 1]]
        for k, (is_right, present) in enumerate(at.sides()):
            inner_part, value, s = stiffness(filtered[k], presents[k])
            of_place = factor(inner_part, value, weight)
            for place in (0, 1):
                here = at.held(is_right) & (present > 0.5)
                patched[place] = jnp.where(here, of_strip(of_place, place + 4), patched[place])
            beside_s = around(s)
            links = 6.0 * s + sum(beside_s[1:], beside_s[0])
            inverse = presents[k] / jnp.maximum(0.5 * links + PENALTY * masks[1, k], 0.1)
            pairs = [s + other for other in beside_s]

            def image(v):
                terms = [pair * (v - other) for pair, other in zip(pairs, around(v))]
                return 0.5 * ((terms[0] + terms[1]) + (terms[2] + terms[3]) + (terms[4] + terms[5]))

            z = masks[0, k] * inverse
            q = image(z)
            w = q * inverse
            strip_out[g, 0, k] = z
            strip_out[g, 1, k] = w
            terms = (z, z * q, q * w, w * image(w))
            sums = [a + jnp.sum(b * counts[k], axis=0, keepdims=True) for a, b in zip(sums, terms)]
        for place in (0, 1):
            factor_out[g, place] = patched[place]
        for k, part in enumerate(sums):
            line = jnp.where(lane_row == 4 * g + k, jnp.sum(part, axis=1, keepdims=True), line)
    table[...] = jnp.broadcast_to(line, table.shape)


def finish(groups, size, table, z_near, z_own, w_near, w_own, strips, factors, out):
    width, thick = out.shape[1:]
    at = Spot(groups, size, width, thick)
    core = lax.rem(at.spot, 2)
    line = jnp.sum(table[...], axis=0, keepdims=True)
    lane_row = lanes_of((1, thick))
    total = [jnp.zeros(at.shape, jnp.float32), jnp.zeros(at.shape, jnp.float32)]
    for g in range(groups):
        m0, m1, m2, m3 = (
            jnp.sum(jnp.where(lane_row == 4 * g + k, line, 0.0), axis=1, keepdims=True) for k in range(4)
        )
        step_one = m0 / m1
        rz_next = step_one * step_one * m2 - m0
        factor = rz_next / m0
        curve = (m1 - 2.0 * step_one * m2 + step_one * step_one * m3) - factor * factor * m1
        step_two = rz_next / curve
        of_z = step_one + step_two * (1.0 + factor)
        of_w = -step_one * step_two
        z = [z_near[g], z_own[g, 0], z_own[g, 1], z_own[g, 2]]
        w = [w_near[g, 0], w_near[g, 1], w_own[g, 0], w_own[g, 1]]
        u = [of_z * v + of_w * t for v, t in zip(z, w)]
        ends = {1: [0.0, 0.0], 2: [0.0, 0.0]}
        for k, (is_right, present) in enumerate(at.sides()):
            strip = of_z * strips[g, 0, k] + of_w * strips[g, 1, k]
            here = at.held(is_right) & (present > 0.5)
            for place in range(4):
                part = of_strip(strip, place + 3)
                u[place] = jnp.where(here, part, u[place])
                if place in ends:
                    if at.n_strips == 1:
                        ends[place] = [part * at.has_left, part * at.has_right]
                    else:
                        ends[place][k] = part * present
        between = [u[k] - u[k + 1] for k in range(3)]
        for k in (1, 2):
            plane = u[k]
            left = turn(jnp.where(at.at_right, ends[k][0], plane), 1, 1)
            right = turn(jnp.where(at.at_left, ends[k][1], plane), -1, 1)
            up = jnp.where(at.first, 0.0, turn(plane, 1, 0))
            down = jnp.where(at.last, 0.0, turn(plane, -1, 0))
            steps = [between[k - 1], between[k]] + [plane - other for other in (left, right, up, down)]
            squares = [v * v for v in steps]
            total[k - 1] = total[k - 1] + factors[g, k - 1] * sum(squares[1:], squares[0])
    for k in range(2):
        out[lax.rem(k + core, 2)] = total[k]


def call(body, outs, *args, scalars=(), scratch=(), flops=0):
    smem = pl.BlockSpec(memory_space=pltpu.SMEM)
    return pl.pallas_call(
        body,
        out_shape=[jax.ShapeDtypeStruct(shape, jnp.float32) for shape in outs],
        in_specs=[pl.BlockSpec(memory_space=pltpu.VMEM)] * len(args) + [smem] * len(scalars),
        out_specs=[pl.BlockSpec(memory_space=pltpu.VMEM)] * len(outs),
        scratch_shapes=[pltpu.VMEM(shape, jnp.float32) for shape in scratch],
        cost_estimate=pl.CostEstimate(flops=flops, transcendentals=0, bytes_accessed=0) if flops else None,
        compiler_params=pltpu.CompilerParams(vmem_limit_bytes=32 * 1024 * 1024),
    )(*args, *scalars)


def local(design, solid_mask, void_mask, load_mask, support_mask, thresholds, group_weight):
    depth, width, thick = design.shape
    size, groups = lax.axis_size("space"), lax.axis_size("proj")
    quarter = width // 4
    pair, near_pairs = pair_swap(size), near_swap(size)
    fixed = jnp.where(solid_mask == 1, 1.0, jnp.where(void_mask == 1, 0.0, design))
    (packed_own,) = call(
        functools.partial(prepare, groups), [(6 * width + quarter, thick)], fixed, load_mask, support_mask
    )
    partner = lax.ppermute(packed_own, "space", pair)
    own, own_masks, scalars = call(
        join, [(4 * width, thick), (4 * width + quarter, thick), (8, thick)], packed_own, partner,
        scalars=(thresholds, group_weight),
    )
    others = [lax.ppermute(scalars, "proj", [((g + k) % groups, g) for g in range(groups)]) for k in range(1, groups)]
    near = lax.ppermute(own, "space", near_pairs)
    near_masks = lax.ppermute(own_masks, "space", near_pairs)
    others = [call(keep, [other.shape], other, flops=1_650_000_000)[0] for other in others]
    steps = (1,) if groups == 2 else (1, -1)
    packed = call(
        functools.partial(pack, groups),
        [(width // 2, thick)] * len(steps) + [(width // 8, thick)] * len(steps),
        own, near,
    )
    straight = [(i, i) for i in range(size)]
    both = ("proj", "space")
    beside = [lax.ppermute(v, both, both_axes(straight, size, groups, k)) for k, v in zip(steps, packed)]
    crossed = [lax.ppermute(v, both, both_axes(pair, size, groups, k)) for k, v in zip(steps, packed[len(steps) :])]
    (beyond,) = call(pick, [(2 * width, thick)], near, packed[0])
    inner = lax.ppermute(beyond, "space", pair)
    n_strips = 1 if groups == 2 else 2
    plane = (width, thick)
    six = (groups, 6, *plane)
    stiff, links, factors, wide, inside = call(
        functools.partial(density_kernel, groups, size),
        [six, six, (groups, 2, *plane), (n_strips, *plane), plane],
        own, near, inner, scalars, *others,
        flops=1,
        scratch=[(PLACES, width + 16, thick), (6, width + 16, thick)],
    )
    one, two, four = (groups, *plane), (groups, 2, *plane), (groups, 4, *plane)
    strips_shape = (2, n_strips, *plane)
    sums = (-(-4 * groups // 8) * 8, thick)
    z_own, w_own, q_own, over_own, totals, mask_strips = call(
        functools.partial(own_kernel, groups, size),
        [four, two, one, one, sums, strips_shape],
        stiff, links, own_masks, partner,
        flops=1,
        scratch=[(3, width + 16, thick), (3, width + 16, thick), (1, width + 16, thick)],
    )
    totals, z_near, w_near, mask_strips = call(
        functools.partial(near_kernel, groups, size),
        [sums, one, two, strips_shape],
        stiff, links, near_masks, z_own, w_own, q_own, over_own, totals, mask_strips,
        flops=1,
        scratch=[(2, width + 16, thick), (1, width + 16, thick), (1, width + 16, thick)],
    )
    beside, crossed = ([call(keep, [v.shape], v, totals)[0] for v in vs] for vs in (beside, crossed))
    table, strips, factors = call(
        functools.partial(edge_kernel, groups, size),
        [(size * groups, thick), (groups, 2, n_strips, *plane), (groups, 2, *plane)],
        inside, wide, mask_strips, totals, factors, scalars, *beside, *crossed, *others,
    )
    table = lax.all_to_all(table, ("proj", "space"), 0, 0, tiled=True)
    (out,) = call(functools.partial(finish, groups, size), [(depth, *plane)], table, z_near, z_own, w_near, w_own, strips, factors)
    return out


def solution(mesh):
    placed = (
        P("space", None, "proj"),
        P("space", None, "proj"),
        P("space", None, "proj"),
        P("space", None, None),
        P("space", None, None),
        P("proj"),
        P("proj"),
    )
    return jax.shard_map(
        local, mesh=mesh, in_specs=placed, out_specs=P("space", None, "proj"), check_vma=False
    )
```

```python
import functools
import math

import jax
import jax.numpy as jnp
from jax import lax
from jax.experimental import pallas as pl
from jax.experimental.pallas import tpu as pltpu
from jax.sharding import PartitionSpec as P

RMIN = 2.0
BETA = 8.0
EMIN = 0.05
PENALTY = 4.0

PLACES = 10
GROUP = 8
HALF = GROUP // 2
WIDE = 2 * GROUP
INNER = PLACES - 2


def pair_swap(size):
    return [(i, i ^ 1) for i in range(size)]


def near_swap(size):
    ups = [(i, i + 1) for i in range(1, size - 1, 2)]
    return ups + [(j, i) for i, j in ups]


def both_axes(pairs, size, groups, step):
    return [
        (g * size + i, (g + step) % groups * size + j)
        for g in range(groups)
        for i, j in pairs
        if groups == 2 or 0 <= g + step < groups
    ]


def lanes_of(shape):
    return lax.broadcasted_iota(jnp.int32, shape, len(shape) - 1)


def turn(array, shift, axis):
    return pltpu.roll(array, shift % array.shape[axis], axis)


def squeeze(strips):
    rows, lanes = strips.shape[0] // 4, strips.shape[1]
    parts = [turn(strips[k * rows : (k + 1) * rows], k * lanes // 4, 1) for k in range(4)]
    block = lanes_of((rows, lanes)) // (lanes // 4)
    return functools.reduce(lambda out, k: jnp.where(block == k, parts[k], out), range(1, 4), parts[0])


def spread(squeezed, start=0):
    lanes = squeezed.shape[1]
    return jnp.concatenate([turn(squeezed, start - k * lanes // 4, 1) for k in range(4)], axis=0)


def prepare(groups, fixed, load, support, out):
    core = lax.rem(lax.axis_index("space"), 2)
    layer = lax.axis_index("proj")
    width, thick = load.shape[1], load.shape[2] // groups
    lane = lanes_of((width, thick))
    lower = lax.rem(lane, GROUP) < HALF
    has_left = layer > 0
    has_right = layer < groups - 1
    centre = pl.ds(pl.multiple_of(layer * thick, thick), thick)
    left = pl.ds(pl.multiple_of(jnp.maximum(layer - 1, 0) * thick, thick), thick)
    right = pl.ds(pl.multiple_of(jnp.minimum(layer + 1, groups - 1) * thick, thick), thick)
    strips = jnp.zeros((width, thick), jnp.float32)
    for place in range(2):
        plane = lax.rem(place + core, 2)
        out[place * width : (place + 1) * width] = fixed[plane]
        for which, mask in enumerate((load, support)):
            held = 2 * which + place
            out[(2 + held) * width : (3 + held) * width] = mask[plane, :, centre].astype(jnp.float32)
            before = jnp.where(has_left, mask[plane, :, left].astype(jnp.float32), 0.0)
            after = jnp.where(has_right, mask[plane, :, right].astype(jnp.float32), 0.0)
            shift = held * GROUP + HALF
            outside = jnp.where(lower, turn(before, shift, 1), turn(after, shift, 1))
            strips = jnp.where(lane // GROUP == held, outside, strips)
    out[6 * width :] = squeeze(strips)


def join(own, partner, thresholds, weights, near_out, mask_out, scalars):
    rows = near_out.shape[0] // 2
    near_out[0:rows] = own[0:rows]
    near_out[rows:] = partner[0:rows]
    mask_out[...] = own[rows:]
    row = lax.broadcasted_iota(jnp.int32, scalars.shape, 0)
    scalars[...] = jnp.where(row == 0, thresholds[0].astype(jnp.float32) / 1000.0, jnp.where(row == 1, weights[0], 0.0))


def keep(array, *refs):
    refs[-1][...] = array[...]


def pick(near, *refs):
    out = refs[-1]
    out[...] = near[0 : out.shape[0]]


def plane_of(ref, k, width):
    return ref[k * width : (k + 1) * width]


def frame_of(own, near):
    order = ((near, 2), (near, 3), (near, 1), (near, 0), (own, 0), (own, 1), (own, 3), (own, 2))
    return [plane_of(ref, k, near.shape[0] // 4) for ref, k in order]


def folded(planes, lower):
    half, lanes = planes[0].shape[0] // 2, planes[0].shape[1]
    lane = lanes_of((half, lanes))
    low, group = lax.rem(lane, GROUP) < HALF, lane // GROUP
    out = jnp.zeros((half, lanes), jnp.float32)
    for place, plane in enumerate(planes):
        start = place * GROUP + HALF
        top, bottom = turn(plane[:half], start, 1), plane[half:]
        of_lower = jnp.where(low, top, turn(bottom, start + HALF, 1))
        of_upper = jnp.where(low, turn(bottom, start - HALF, 1), top)
        out = jnp.where(group == place, jnp.where(lower, of_lower, of_upper), out)
    return out


def unfold(folded, lower):
    return jnp.concatenate([folded, jnp.where(lower, turn(folded, -HALF, 1), turn(folded, HALF, 1))], axis=0)


def pack(groups, own, near, *outs):
    planes = frame_of(own, near)
    sides = (lax.axis_index("proj") == 0,) if groups == 2 else (True, False)
    for k, lower in enumerate(sides):
        outs[k][...] = folded(planes, lower)
        outs[len(sides) + k][...] = squeeze(folded([planes[3], planes[2]], lower))


def around_y(plane, first, last):
    return jnp.where(first, 0.0, turn(plane, 1, 0)) + jnp.where(last, 0.0, turn(plane, -1, 0))


class Spot:
    def __init__(self, groups, size, width, thick):
        self.groups, self.width, self.thick = groups, width, thick
        self.spot, self.layer = lax.axis_index("space"), lax.axis_index("proj")
        core = lax.rem(self.spot, 2)
        self.shape = (width, thick)
        self.lane = lanes_of(self.shape)
        row = lax.broadcasted_iota(jnp.int32, self.shape, 0)
        self.first, self.last = row == 0, row == width - 1
        self.at_left, self.at_right = self.lane == 0, self.lane == thick - 1
        self.where = self.lane // GROUP
        self.slot = lax.rem(self.lane, GROUP)
        self.lower = self.slot < HALF
        self.near_real = jnp.where(jnp.where(core == 0, self.spot > 0, self.spot < size - 1), 1.0, 0.0)
        self.inner_real = jnp.where(jnp.where(core == 0, self.spot < size - 2, self.spot > 1), 1.0, 0.0)
        self.real = [self.near_real] * 4 + [1.0] * 4 + [self.inner_real] * 2
        self.has_left = jnp.where(self.layer > 0, 1.0, 0.0)
        self.has_right = jnp.where(self.layer < groups - 1, 1.0, 0.0)
        self.n_strips = 1 if groups == 2 else 2
        self.is_right = self.layer == 0

    def real_at(self, places):
        return jnp.where(places < 4, self.near_real, jnp.where(places < 8, 1.0, self.inner_real))

    def strips(self, inside, outside):
        right = jnp.where(self.lower, inside, outside[-1])
        left = jnp.where(self.lower, outside[0], inside)
        return [jnp.where(self.is_right, right, left)] if self.n_strips == 1 else [left, right]

    def strip_z(self):
        left, right = (self.layer * self.thick + self.slot + shift for shift in (-HALF, self.thick - HALF))
        return [jnp.where(self.is_right, right, left)] if self.n_strips == 1 else [left, right]

    def sides(self):
        if self.n_strips == 1:
            return [(self.is_right, 1.0)]
        return [(False, self.has_left), (True, self.has_right)]

    def wide(self, is_right):
        lane = lax.rem(self.lane + by_side(is_right, 0, WIDE // 2), self.thick)
        return lane // WIDE, lax.rem(lane, WIDE)

    def counted(self):
        counted = jnp.ones(self.shape, jnp.float32)
        for is_right, present in self.sides():
            counted = jnp.where(self.held(is_right), 1.0 - present, counted)
        return counted

    def held(self, is_right):
        right, left = self.lane >= self.thick - HALF, self.lane < HALF
        if isinstance(is_right, bool):
            return right if is_right else left
        return jnp.where(is_right, self.lane, self.thick - 1 - self.lane) >= self.thick - HALF


def by_side(is_right, left, right):
    if isinstance(is_right, bool):
        return right if is_right else left
    return jnp.where(is_right, right, left)


def of_strip(strip, place):
    return turn(strip, -((place - 1) * WIDE + HALF), 1)


def count_terms(count_y, count_z):
    two, three = RMIN - math.sqrt(2.0), RMIN - math.sqrt(3.0)
    head = 2.0 + (count_y + count_z) + two * (count_y * count_z)
    side = 1.0 + two * (count_y + count_z) + three * (count_y * count_z)
    return head, side


def weights_of(at, packed, others, g):
    eta, weight = packed[0:1], packed[1:2]
    for k, other in enumerate(others):
        mine = lax.rem(at.layer + k + 1, at.groups) == g
        eta = jnp.where(mine, other[0:1], eta)
        weight = jnp.where(mine, other[1:2], weight)
    return eta, weight


def projection(eta):
    low = jnp.tanh(BETA * eta)
    over_bottom = 1.0 / (low + jnp.tanh(BETA * (1.0 - eta)))

    def stiffness(density, present):
        inner_part = jnp.tanh(BETA * (density - eta))
        value = (low + inner_part) * over_bottom
        return inner_part, value, (EMIN + (1.0 - EMIN) * (value * value * value)) * present

    def factor(inner_part, value, weight):
        slope = (BETA * over_bottom) * (1.0 - inner_part * inner_part)
        return (-0.5 * 3.0 * (1.0 - EMIN)) * weight * (value * value) * slope

    return stiffness, factor


def border(ref, width):
    ref[:, 0:8] = jnp.zeros((ref.shape[0], 8, ref.shape[2]), jnp.float32)
    ref[:, 8 + width :] = jnp.zeros((ref.shape[0], 8, ref.shape[2]), jnp.float32)


def to_left(at, plane):
    return jnp.where(at.at_left, 0.0, turn(plane, 1, 1))


def to_right(at, plane):
    return jnp.where(at.at_right, 0.0, turn(plane, -1, 1))


def own_columns(plane, place):
    return turn(plane, (place - 1) * WIDE + HALF, 1)


def density_kernel(groups, size, *refs):
    own, near, inner, scalars = refs[:4]
    others = refs[4 : len(refs) - 7]
    stiff_out, links_out, factor_out, wide_out, inside_out, f_rows, s_rows = refs[len(refs) - 7 :]
    width, thick = near.shape[0] // 4, near.shape[1]
    at = Spot(groups, size, width, thick)
    two, three = RMIN - math.sqrt(2.0), RMIN - math.sqrt(3.0)
    planes = frame_of(own, near) + [plane_of(inner, k, width) for k in (0, 1)]
    strip = jnp.zeros(at.shape, jnp.float32)
    for place in range(PLACES):
        strip = jnp.where(at.where == place, turn(planes[place], place * GROUP + HALF, 1), strip)
    inside_out[...] = strip
    for ref in (f_rows, s_rows):
        border(ref, width)
    for place in range(PLACES):
        f_rows[place, 8 : 8 + width] = planes[place]

    count_y = jnp.where(at.first, 0.0, 1.0) + jnp.where(at.last, 0.0, 1.0)
    places_z = at.layer * thick + at.lane
    count_z = jnp.where(places_z >= 1, 1.0, 0.0) + jnp.where(places_z < groups * thick - 1, 1.0, 0.0)
    head, side = count_terms(count_y, count_z)
    over_two, over_one = 1.0 / (head + 2.0 * side), 1.0 / (head + side)
    straight, once, twice = [], [], []
    for place in range(PLACES):
        plane = planes[place]
        by_y = f_rows[place, 7 : 7 + width] + f_rows[place, 9 : 9 + width]
        straight.append(2.0 * plane + by_y)
        once.append(plane + two * by_y)
        twice.append(two * plane + three * by_y)
    filtered = {}
    for place in range(1, PLACES - 1):
        beside = once[place] + (twice[place - 1] + twice[place + 1])
        total = straight[place] + (once[place - 1] + once[place + 1]) + (to_left(at, beside) + to_right(at, beside))
        count_x = at.real[place - 1] + at.real[place + 1]
        filtered[place] = total * jnp.where(count_x > 1.5, over_two, over_one)

    for k, (is_right, _) in enumerate(at.sides()):
        block, _ = at.wide(is_right)
        strip = jnp.zeros(at.shape, jnp.float32)
        for place in range(1, PLACES - 1):
            strip = jnp.where(block == place - 1, own_columns(filtered[place], place), strip)
        wide_out[k] = strip

    for g in range(groups):
        eta, weight = weights_of(at, scalars, others, g)
        stiffness, factor = projection(eta)
        stiff = {}
        for place in range(1, PLACES - 1):
            inner_part, value, stiff[place] = stiffness(filtered[place], at.real[place])
            if place in (4, 5):
                factor_out[g, place - 4] = factor(inner_part, value, weight)
            if 2 <= place < 8:
                s_rows[place - 2, 8 : 8 + width] = stiff[place]
                stiff_out[g, place - 2] = stiff[place]
        for place in range(2, 8):
            s = stiff[place]
            by_y = s_rows[place - 2, 7 : 7 + width] + s_rows[place - 2, 9 : 9 + width]
            by_z = to_left(at, s) + to_right(at, s)
            links_out[g, place - 2] = 3.0 * s + 0.5 * ((stiff[place - 1] + stiff[place + 1]) + by_z + by_y)


def image_of(at, stiff, rows_of_stiff, field, rows, place, before, after):
    v, s = field[place], stiff[place]
    width = at.width

    def beside(ref_and_start, first):
        ref, start = ref_and_start
        return ref[place - start, first : first + width]

    k_right = s + to_right(at, s)
    flow_z = k_right * (v - to_right(at, v))
    total = (after - before) + (flow_z - jnp.where(at.at_left, -(s * v), turn(flow_z, 1, 1)))
    s_up, s_down = beside(rows_of_stiff, 7), beside(rows_of_stiff, 9)
    v_up, v_down = beside(rows, 7), beside(rows, 9)
    return total + ((s + s_up) * (v - v_up) + (s + s_down) * (v - v_down))


def flow_x(stiff, field, place):
    return (stiff[place] + stiff[place + 1]) * (field[place] - field[place + 1])


def start_of(at, links, load, support, place):
    over = at.real[place] / jnp.maximum(links + PENALTY * support, 0.1)
    return over, load * over


def mask_strips_of(at, is_right, strip, which, parts):
    block, slot = at.wide(is_right)
    beyond = by_side(is_right, slot, WIDE - 1 - slot) < HALF
    for place, plane, source, held in parts:
        start = (place - 1) * WIDE - (held + 2 * which) * GROUP
        value = jnp.where(beyond, turn(source, start, 1), own_columns(plane, place))
        strip = jnp.where(block == place - 1, value, strip)
    return strip


def own_kernel(groups, size, *refs):
    stiff_in, links_in, own_masks, partner = refs[:4]
    z_out, w_out, q_out, over_out, totals_out, masks_out, s_rows, z_rows, w_rows = refs[4:]
    width, thick = stiff_in.shape[2:]
    partner_masks = partner.at[2 * width :]
    at = Spot(groups, size, width, thick)
    for ref in (s_rows, z_rows, w_rows):
        border(ref, width)
    order = ((own_masks, 0), (own_masks, 1), (partner_masks, 1), (partner_masks, 0))
    load, support = (
        {place + 4: plane_of(ref, 2 * which + k, width) for place, (ref, k) in enumerate(order)} for which in (0, 1)
    )
    mine, theirs = spread(own_masks[4 * width :]), spread(partner_masks[4 * width :])
    for k, (is_right, _) in enumerate(at.sides()):
        for which, mask in enumerate((load, support)):
            sources = ((mine, 0), (mine, 1), (theirs, 1), (theirs, 0))
            parts = [(place + 4, mask[place + 4], *source) for place, source in enumerate(sources)]
            masks_out[which, k] = mask_strips_of(at, is_right, jnp.zeros(at.shape, jnp.float32), which, parts)

    counted = at.counted()
    for g in range(groups):
        stiff = {place: stiff_in[g, place - 2] for place in range(4, 8)}
        over, z = {}, {}
        for place in range(4, 8):
            over[place], z[place] = start_of(at, links_in[g, place - 2], load[place], support[place], place)
            z_out[g, place - 4] = z[place]
        over_out[g] = over[4]
        for place in (4, 5, 6):
            s_rows[place - 4, 8 : 8 + width] = stiff[place]
            z_rows[place - 4, 8 : 8 + width] = z[place]
        flows = {3: 0.0} | {place: flow_x(stiff, z, place) for place in (4, 5, 6)}
        q, w = {}, {}
        for place in (4, 5, 6):
            q[place] = 0.5 * image_of(at, stiff, (s_rows, 4), z, (z_rows, 4), place, flows[place - 1], flows[place])
        for place in (5, 6):
            w[place] = q[place] * over[place]
            w_out[g, place - 5] = w[place]
        q_out[g] = q[4]
        w_rows[0, 8 : 8 + width] = w[5]
        aw = 0.5 * image_of(at, stiff, (s_rows, 4), w, (w_rows, 5), 5, 0.0, flow_x(stiff, w, 5))
        terms = (z[4] + z[5], z[5] * q[5], q[5] * w[5], w[5] * aw)
        for k, term in enumerate(terms):
            totals_out[4 * g + k : 4 * g + k + 1] = jnp.sum(term * counted, axis=0, keepdims=True)


def near_kernel(groups, size, *refs):
    stiff_in, links_in, near_masks, z_in, w_in, q_in, over_in, totals_in, masks_in = refs[:9]
    totals_out, z_out, w_out, masks_out, s_rows, z_rows, w_rows = refs[9:]
    width, thick = stiff_in.shape[2:]
    at = Spot(groups, size, width, thick)
    for ref in (s_rows, z_rows, w_rows):
        border(ref, width)
    load, support = (
        {place: plane_of(near_masks, 2 * which + 3 - place, width) for place in (2, 3)} for which in (0, 1)
    )
    nears = spread(near_masks[4 * width :])
    for k, (is_right, _) in enumerate(at.sides()):
        for which, mask in enumerate((load, support)):
            parts = [(place, mask[place], nears, 3 - place) for place in (2, 3)]
            masks_out[which, k] = mask_strips_of(at, is_right, masks_in[which, k], which, parts)

    counted = at.counted()
    for g in range(groups):
        stiff = {place: stiff_in[g, place - 2] for place in range(2, 6)}
        z = {4: z_in[g, 0]}
        over = {4: over_in[g]}
        for place in (2, 3):
            over[place], z[place] = start_of(at, links_in[g, place - 2], load[place], support[place], place)
        z_out[g] = z[3]
        for place in (3, 4):
            s_rows[place - 3, 8 : 8 + width] = stiff[place]
        z_rows[0, 8 : 8 + width] = z[3]
        flows = {place: flow_x(stiff, z, place) for place in (2, 3)}
        q = 0.5 * image_of(at, stiff, (s_rows, 3), z, (z_rows, 3), 3, flows[2], flows[3])
        q = {3: q, 4: q_in[g] - 0.5 * flows[3]}
        w = {place: q[place] * over[place] for place in (3, 4)} | {5: w_in[g, 0]}
        for place in (3, 4):
            w_out[g, place - 3] = w[place]
        w_rows[0, 8 : 8 + width] = w[4]
        flows = {place: flow_x(stiff, w, place) for place in (3, 4)}
        aw = 0.5 * image_of(at, stiff, (s_rows, 3), w, (w_rows, 4), 4, flows[3], flows[4])
        terms = (None, z[4] * q[4], q[4] * w[4], w[4] * aw - w[5] * (0.5 * flows[4]))
        for k, term in enumerate(terms):
            row = totals_in[4 * g + k : 4 * g + k + 1]
            if term is not None:
                row = row + jnp.sum(term * counted, axis=0, keepdims=True)
            totals_out[4 * g + k : 4 * g + k + 1] = row


def edge_kernel(groups, size, *refs):
    n_side = 1 if groups == 2 else 2
    inside, wide, masks, totals, factors, scalars = refs[:6]
    beside, crossed = refs[6 : 6 + n_side], refs[6 + n_side : 6 + 2 * n_side]
    others = refs[6 + 2 * n_side : len(refs) - 3]
    table, strip_out, factor_out = refs[len(refs) - 3 :]
    width, thick = inside.shape
    at = Spot(groups, size, width, thick)
    first, last = at.first, at.last
    two, three = RMIN - math.sqrt(2.0), RMIN - math.sqrt(3.0)

    outside = []
    for k in range(n_side):
        lower = at.layer == 1 if groups == 2 else k == 0
        group = lanes_of(beside[k].shape) // GROUP
        strip = jnp.where(group < 8, beside[k][...], spread(crossed[k][...], 8 * GROUP))
        outside.append(unfold(jnp.where(group < PLACES, strip, 0.0), lower))
    outside = [outside[0] * at.has_left, outside[-1] * at.has_right]
    fixed = at.strips(inside[...], outside)

    count_y = jnp.where(first, 0.0, 1.0) + jnp.where(last, 0.0, 1.0)
    count_x = at.real_at(at.where - 1) + at.real_at(at.where + 1)
    span_z = thick * groups
    filtered, presents, counts = [], [], []
    for k, (strip, z_at, (is_right, present)) in enumerate(zip(fixed, at.strip_z(), at.sides())):
        by_y = around_y(strip, first, last)
        once = strip + two * by_y
        twice = two * strip + three * by_y
        total = 2.0 * strip + by_y
        for step in (GROUP, -GROUP, 1, -1):
            total = total + turn(once, step, 1)
        for step in (GROUP + 1, GROUP - 1, 1 - GROUP, -1 - GROUP):
            total = total + turn(twice, step, 1)
        count_z = jnp.where(z_at >= 1, 1.0, 0.0) + jnp.where(z_at < span_z - 1, 1.0, 0.0)
        head, side = count_terms(count_y, count_z)
        total = total * (1.0 / (head + count_x * side))
        value = wide[k]
        block, slot = at.wide(is_right)
        better = by_side(is_right, slot, WIDE - 1 - slot) <= HALF
        for place in range(1, PLACES - 1):
            moved = turn(total, (place - 1) * WIDE - place * GROUP, 1)
            value = jnp.where(better & (block == place - 1), moved, value)
        filtered.append(value)
        z_wide = at.layer * thick + slot + by_side(is_right, -HALF, thick - WIDE + HALF)
        presents.append(jnp.where((z_wide >= 0) & (z_wide < span_z), at.real_at(block + 1), 0.0))
        own = by_side(is_right, slot, WIDE - 1 - slot)
        own = (own >= HALF) & (own < 2 * HALF) & (block >= 3) & (block < 5)
        counts.append(jnp.where(own, present, 0.0))

    def around(v):
        up, down = jnp.where(first, 0.0, turn(v, 1, 0)), jnp.where(last, 0.0, turn(v, -1, 0))
        return [turn(v, shift, 1) for shift in (WIDE, -WIDE, 1, -1)] + [up, down]

    lane_row = lanes_of((1, thick))
    line = jnp.zeros((1, thick), jnp.float32)
    for g in range(groups):
        eta, weight = weights_of(at, scalars, others, g)
        stiffness, factor = projection(eta)
        sums = [totals[4 * g + k : 4 * g + k + 1] for k in range(4)]
        patched = [factors[g, 0], factors[g, 1]]
        for k, (is_right, present) in enumerate(at.sides()):
            inner_part, value, s = stiffness(filtered[k], presents[k])
            of_place = factor(inner_part, value, weight)
            for place in (0, 1):
                here = at.held(is_right) & (present > 0.5)
                patched[place] = jnp.where(here, of_strip(of_place, place + 4), patched[place])
            beside_s = around(s)
            links = 6.0 * s + sum(beside_s[1:], beside_s[0])
            inverse = presents[k] / jnp.maximum(0.5 * links + PENALTY * masks[1, k], 0.1)
            pairs = [s + other for other in beside_s]

            def image(v):
                terms = [pair * (v - other) for pair, other in zip(pairs, around(v))]
                return 0.5 * ((terms[0] + terms[1]) + (terms[2] + terms[3]) + (terms[4] + terms[5]))

            z = masks[0, k] * inverse
            q = image(z)
            w = q * inverse
            strip_out[g, 0, k] = z
            strip_out[g, 1, k] = w
            terms = (z, z * q, q * w, w * image(w))
            sums = [a + jnp.sum(b * counts[k], axis=0, keepdims=True) for a, b in zip(sums, terms)]
        for place in (0, 1):
            factor_out[g, place] = patched[place]
        for k, part in enumerate(sums):
            line = jnp.where(lane_row == 4 * g + k, jnp.sum(part, axis=1, keepdims=True), line)
    table[...] = jnp.broadcast_to(line, table.shape)


def finish(groups, size, table, z_near, z_own, w_near, w_own, strips, factors, out):
    width, thick = out.shape[1:]
    at = Spot(groups, size, width, thick)
    core = lax.rem(at.spot, 2)
    line = jnp.sum(table[...], axis=0, keepdims=True)
    lane_row = lanes_of((1, thick))
    total = [jnp.zeros(at.shape, jnp.float32), jnp.zeros(at.shape, jnp.float32)]
    for g in range(groups):
        m0, m1, m2, m3 = (
            jnp.sum(jnp.where(lane_row == 4 * g + k, line, 0.0), axis=1, keepdims=True) for k in range(4)
        )
        step_one = m0 / m1
        rz_next = step_one * step_one * m2 - m0
        factor = rz_next / m0
        curve = (m1 - 2.0 * step_one * m2 + step_one * step_one * m3) - factor * factor * m1
        step_two = rz_next / curve
        of_z = step_one + step_two * (1.0 + factor)
        of_w = -step_one * step_two
        z = [z_near[g], z_own[g, 0], z_own[g, 1], z_own[g, 2]]
        w = [w_near[g, 0], w_near[g, 1], w_own[g, 0], w_own[g, 1]]
        u = [of_z * v + of_w * t for v, t in zip(z, w)]
        ends = {1: [0.0, 0.0], 2: [0.0, 0.0]}
        for k, (is_right, present) in enumerate(at.sides()):
            strip = of_z * strips[g, 0, k] + of_w * strips[g, 1, k]
            here = at.held(is_right) & (present > 0.5)
            for place in range(4):
                part = of_strip(strip, place + 3)
                u[place] = jnp.where(here, part, u[place])
                if place in ends:
                    if at.n_strips == 1:
                        ends[place] = [part * at.has_left, part * at.has_right]
                    else:
                        ends[place][k] = part * present
        between = [u[k] - u[k + 1] for k in range(3)]
        for k in (1, 2):
            plane = u[k]
            left = turn(jnp.where(at.at_right, ends[k][0], plane), 1, 1)
            right = turn(jnp.where(at.at_left, ends[k][1], plane), -1, 1)
            up = jnp.where(at.first, 0.0, turn(plane, 1, 0))
            down = jnp.where(at.last, 0.0, turn(plane, -1, 0))
            steps = [between[k - 1], between[k]] + [plane - other for other in (left, right, up, down)]
            squares = [v * v for v in steps]
            total[k - 1] = total[k - 1] + factors[g, k - 1] * sum(squares[1:], squares[0])
    for k in range(2):
        out[lax.rem(k + core, 2)] = total[k]


def call(body, outs, *args, scalars=(), scratch=(), flops=0):
    smem = pl.BlockSpec(memory_space=pltpu.SMEM)
    return pl.pallas_call(
        body,
        out_shape=[jax.ShapeDtypeStruct(shape, jnp.float32) for shape in outs],
        in_specs=[pl.BlockSpec(memory_space=pltpu.VMEM)] * len(args) + [smem] * len(scalars),
        out_specs=[pl.BlockSpec(memory_space=pltpu.VMEM)] * len(outs),
        scratch_shapes=[pltpu.VMEM(shape, jnp.float32) for shape in scratch],
        cost_estimate=pl.CostEstimate(flops=flops, transcendentals=0, bytes_accessed=0) if flops else None,
        compiler_params=pltpu.CompilerParams(vmem_limit_bytes=32 * 1024 * 1024),
    )(*args, *scalars)


def local(design, solid_mask, void_mask, load_mask, support_mask, thresholds, group_weight):
    depth, width, thick = design.shape
    size, groups = lax.axis_size("space"), lax.axis_size("proj")
    quarter = width // 4
    pair, near_pairs = pair_swap(size), near_swap(size)
    fixed = jnp.where(solid_mask == 1, 1.0, jnp.where(void_mask == 1, 0.0, design))
    (packed_own,) = call(
        functools.partial(prepare, groups), [(6 * width + quarter, thick)], fixed, load_mask, support_mask
    )
    partner = lax.ppermute(packed_own, "space", pair)
    own, own_masks, scalars = call(
        join, [(4 * width, thick), (4 * width + quarter, thick), (8, thick)], packed_own, partner,
        scalars=(thresholds, group_weight),
    )
    others = [lax.ppermute(scalars, "proj", [((g + k) % groups, g) for g in range(groups)]) for k in range(1, groups)]
    near = lax.ppermute(own, "space", near_pairs)
    near_masks = lax.ppermute(own_masks, "space", near_pairs)
    others = [call(keep, [other.shape], other, flops=1_650_000_000)[0] for other in others]
    steps = (1,) if groups == 2 else (1, -1)
    packed = call(
        functools.partial(pack, groups),
        [(width // 2, thick)] * len(steps) + [(width // 8, thick)] * len(steps),
        own, near,
    )
    straight = [(i, i) for i in range(size)]
    both = ("proj", "space")
    beside = [lax.ppermute(v, both, both_axes(straight, size, groups, k)) for k, v in zip(steps, packed)]
    crossed = [lax.ppermute(v, both, both_axes(pair, size, groups, k)) for k, v in zip(steps, packed[len(steps) :])]
    (beyond,) = call(pick, [(2 * width, thick)], near, packed[0])
    inner = lax.ppermute(beyond, "space", pair)
    n_strips = 1 if groups == 2 else 2
    plane = (width, thick)
    six = (groups, 6, *plane)
    stiff, links, factors, wide, inside = call(
        functools.partial(density_kernel, groups, size),
        [six, six, (groups, 2, *plane), (n_strips, *plane), plane],
        own, near, inner, scalars, *others,
        flops=1,
        scratch=[(PLACES, width + 16, thick), (6, width + 16, thick)],
    )
    one, two, four = (groups, *plane), (groups, 2, *plane), (groups, 4, *plane)
    strips_shape = (2, n_strips, *plane)
    sums = (-(-4 * groups // 8) * 8, thick)
    z_own, w_own, q_own, over_own, totals, mask_strips = call(
        functools.partial(own_kernel, groups, size),
        [four, two, one, one, sums, strips_shape],
        stiff, links, own_masks, partner,
        flops=1,
        scratch=[(3, width + 16, thick), (3, width + 16, thick), (1, width + 16, thick)],
    )
    totals, z_near, w_near, mask_strips = call(
        functools.partial(near_kernel, groups, size),
        [sums, one, two, strips_shape],
        stiff, links, near_masks, z_own, w_own, q_own, over_own, totals, mask_strips,
        flops=1,
        scratch=[(2, width + 16, thick), (1, width + 16, thick), (1, width + 16, thick)],
    )
    table, strips, factors = call(
        functools.partial(edge_kernel, groups, size),
        [(size * groups, thick), (groups, 2, n_strips, *plane), (groups, 2, *plane)],
        inside, wide, mask_strips, totals, factors, scalars, *beside, *crossed, *others,
    )
    table = lax.all_to_all(table, ("proj", "space"), 0, 0, tiled=True)
    (out,) = call(functools.partial(finish, groups, size), [(depth, *plane)], table, z_near, z_own, w_near, w_own, strips, factors)
    return out


def solution(mesh):
    placed = (
        P("space", None, "proj"),
        P("space", None, "proj"),
        P("space", None, "proj"),
        P("space", None, None),
        P("space", None, None),
        P("proj"),
        P("proj"),
    )
    return jax.shard_map(
        local, mesh=mesh, in_specs=placed, out_specs=P("space", None, "proj"), check_vma=False
    )
```

```python
import functools
import math

import jax
import jax.numpy as jnp
from jax import lax
from jax.experimental import pallas as pl
from jax.experimental.pallas import tpu as pltpu
from jax.sharding import PartitionSpec as P

RMIN = 2.0
BETA = 8.0
EMIN = 0.05
PENALTY = 4.0

PLACES = 10
GROUP = 8
HALF = GROUP // 2
WIDE = 2 * GROUP
INNER = PLACES - 2


def pair_swap(size):
    return [(i, i ^ 1) for i in range(size)]


def near_swap(size):
    ups = [(i, i + 1) for i in range(1, size - 1, 2)]
    return ups + [(j, i) for i, j in ups]


def both_axes(pairs, size, groups, step):
    return [
        (g * size + i, (g + step) % groups * size + j)
        for g in range(groups)
        for i, j in pairs
        if groups == 2 or 0 <= g + step < groups
    ]


def lanes_of(shape):
    return lax.broadcasted_iota(jnp.int32, shape, len(shape) - 1)


def turn(array, shift, axis):
    return pltpu.roll(array, shift % array.shape[axis], axis)


def squeeze(strips):
    rows, lanes = strips.shape[0] // 4, strips.shape[1]
    parts = [turn(strips[k * rows : (k + 1) * rows], k * lanes // 4, 1) for k in range(4)]
    block = lanes_of((rows, lanes)) // (lanes // 4)
    return functools.reduce(lambda out, k: jnp.where(block == k, parts[k], out), range(1, 4), parts[0])


def spread(squeezed, start=0):
    lanes = squeezed.shape[1]
    return jnp.concatenate([turn(squeezed, start - k * lanes // 4, 1) for k in range(4)], axis=0)


def prepare(groups, fixed, load, support, out):
    core = lax.rem(lax.axis_index("space"), 2)
    layer = lax.axis_index("proj")
    width, thick = load.shape[1], load.shape[2] // groups
    quarter = width // 4
    lane = lanes_of((quarter, thick))
    lower = lax.rem(lane, GROUP) < HALF
    has_left = layer > 0
    has_right = layer < groups - 1
    centre = pl.ds(pl.multiple_of(layer * thick, thick), thick)
    left = pl.ds(pl.multiple_of(jnp.maximum(layer - 1, 0) * thick, thick), thick)
    right = pl.ds(pl.multiple_of(jnp.minimum(layer + 1, groups - 1) * thick, thick), thick)
    strips = jnp.zeros((quarter, thick), jnp.float32)
    for place in range(2):
        plane = lax.rem(place + core, 2)
        out[place * width : (place + 1) * width] = fixed[plane]
        for which, mask in enumerate((load, support)):
            held = 2 * which + place
            out[(2 + held) * width : (3 + held) * width] = mask[plane, :, centre].astype(jnp.float32)
            before = jnp.where(has_left, mask[plane, :, left].astype(jnp.float32), 0.0)
            after = jnp.where(has_right, mask[plane, :, right].astype(jnp.float32), 0.0)
            for block in range(4):
                rows = slice(block * quarter, (block + 1) * quarter)
                shift = held * GROUP + HALF + block * (thick // 4)
                outside = jnp.where(lower, turn(before[rows], shift, 1), turn(after[rows], shift, 1))
                strips = jnp.where(lane // GROUP == held + block * (thick // (4 * GROUP)), outside, strips)
    out[6 * width :] = strips


def join(own, partner, thresholds, weights, near_out, mask_out, scalars):
    rows = near_out.shape[0] // 2
    near_out[0:rows] = own[0:rows]
    near_out[rows:] = partner[0:rows]
    mask_out[...] = own[rows:]
    row = lax.broadcasted_iota(jnp.int32, scalars.shape, 0)
    scalars[...] = jnp.where(row == 0, thresholds[0].astype(jnp.float32) / 1000.0, jnp.where(row == 1, weights[0], 0.0))


def keep(array, *refs):
    refs[-1][...] = array[...]


def pick(near, *refs):
    out = refs[-1]
    out[...] = near[0 : out.shape[0]]


def plane_of(ref, k, width):
    return ref[k * width : (k + 1) * width]


def frame_of(own, near):
    order = ((near, 2), (near, 3), (near, 1), (near, 0), (own, 0), (own, 1), (own, 3), (own, 2))
    return [plane_of(ref, k, near.shape[0] // 4) for ref, k in order]


def folded(planes, lower):
    half, lanes = planes[0].shape[0] // 2, planes[0].shape[1]
    lane = lanes_of((half, lanes))
    low, group = lax.rem(lane, GROUP) < HALF, lane // GROUP
    out = jnp.zeros((half, lanes), jnp.float32)
    for place, plane in enumerate(planes):
        start = place * GROUP + HALF
        top, bottom = turn(plane[:half], start, 1), plane[half:]
        of_lower = jnp.where(low, top, turn(bottom, start + HALF, 1))
        of_upper = jnp.where(low, turn(bottom, start - HALF, 1), top)
        out = jnp.where(group == place, jnp.where(lower, of_lower, of_upper), out)
    return out


def unfold(folded, lower):
    return jnp.concatenate([folded, jnp.where(lower, turn(folded, -HALF, 1), turn(folded, HALF, 1))], axis=0)


def pack(groups, own, near, *outs):
    planes = frame_of(own, near)
    sides = (lax.axis_index("proj") == 0,) if groups == 2 else (True, False)
    for k, lower in enumerate(sides):
        outs[k][...] = folded(planes, lower)
        outs[len(sides) + k][...] = squeeze(folded([planes[3], planes[2]], lower))


def around_y(plane, first, last):
    return jnp.where(first, 0.0, turn(plane, 1, 0)) + jnp.where(last, 0.0, turn(plane, -1, 0))


class Spot:
    def __init__(self, groups, size, width, thick):
        self.groups, self.width, self.thick = groups, width, thick
        self.spot, self.layer = lax.axis_index("space"), lax.axis_index("proj")
        core = lax.rem(self.spot, 2)
        self.shape = (width, thick)
        self.lane = lanes_of(self.shape)
        row = lax.broadcasted_iota(jnp.int32, self.shape, 0)
        self.first, self.last = row == 0, row == width - 1
        self.at_left, self.at_right = self.lane == 0, self.lane == thick - 1
        self.where = self.lane // GROUP
        self.slot = lax.rem(self.lane, GROUP)
        self.lower = self.slot < HALF
        self.near_real = jnp.where(jnp.where(core == 0, self.spot > 0, self.spot < size - 1), 1.0, 0.0)
        self.inner_real = jnp.where(jnp.where(core == 0, self.spot < size - 2, self.spot > 1), 1.0, 0.0)
        self.real = [self.near_real] * 4 + [1.0] * 4 + [self.inner_real] * 2
        self.has_left = jnp.where(self.layer > 0, 1.0, 0.0)
        self.has_right = jnp.where(self.layer < groups - 1, 1.0, 0.0)
        self.n_strips = 1 if groups == 2 else 2
        self.is_right = self.layer == 0

    def real_at(self, places):
        return jnp.where(places < 4, self.near_real, jnp.where(places < 8, 1.0, self.inner_real))

    def strips(self, inside, outside):
        right = jnp.where(self.lower, inside, outside[-1])
        left = jnp.where(self.lower, outside[0], inside)
        return [jnp.where(self.is_right, right, left)] if self.n_strips == 1 else [left, right]

    def strip_z(self):
        left, right = (self.layer * self.thick + self.slot + shift for shift in (-HALF, self.thick - HALF))
        return [jnp.where(self.is_right, right, left)] if self.n_strips == 1 else [left, right]

    def sides(self):
        if self.n_strips == 1:
            return [(self.is_right, 1.0)]
        return [(False, self.has_left), (True, self.has_right)]

    def wide(self, is_right):
        lane = lax.rem(self.lane + by_side(is_right, 0, WIDE // 2), self.thick)
        return lane // WIDE, lax.rem(lane, WIDE)

    def counted(self):
        counted = jnp.ones(self.shape, jnp.float32)
        for is_right, present in self.sides():
            counted = jnp.where(self.held(is_right), 1.0 - present, counted)
        return counted

    def held(self, is_right):
        right, left = self.lane >= self.thick - HALF, self.lane < HALF
        if isinstance(is_right, bool):
            return right if is_right else left
        return jnp.where(is_right, self.lane, self.thick - 1 - self.lane) >= self.thick - HALF


def by_side(is_right, left, right):
    if isinstance(is_right, bool):
        return right if is_right else left
    return jnp.where(is_right, right, left)


def of_strip(strip, place):
    return turn(strip, -((place - 1) * WIDE + HALF), 1)


def count_terms(count_y, count_z):
    two, three = RMIN - math.sqrt(2.0), RMIN - math.sqrt(3.0)
    head = 2.0 + (count_y + count_z) + two * (count_y * count_z)
    side = 1.0 + two * (count_y + count_z) + three * (count_y * count_z)
    return head, side


def weights_of(at, packed, others, g):
    eta, weight = packed[0:1], packed[1:2]
    for k, other in enumerate(others):
        mine = lax.rem(at.layer + k + 1, at.groups) == g
        eta = jnp.where(mine, other[0:1], eta)
        weight = jnp.where(mine, other[1:2], weight)
    return eta, weight


def projection(eta):
    low = jnp.tanh(BETA * eta)
    over_bottom = 1.0 / (low + jnp.tanh(BETA * (1.0 - eta)))

    def stiffness(density, present):
        inner_part = jnp.tanh(BETA * (density - eta))
        value = (low + inner_part) * over_bottom
        return inner_part, value, (EMIN + (1.0 - EMIN) * (value * value * value)) * present

    def factor(inner_part, value, weight):
        slope = (BETA * over_bottom) * (1.0 - inner_part * inner_part)
        return (-0.5 * 3.0 * (1.0 - EMIN)) * weight * (value * value) * slope

    return stiffness, factor


def border(ref, width):
    ref[:, 0:8] = jnp.zeros((ref.shape[0], 8, ref.shape[2]), jnp.float32)
    ref[:, 8 + width :] = jnp.zeros((ref.shape[0], 8, ref.shape[2]), jnp.float32)


def to_left(at, plane):
    return jnp.where(at.at_left, 0.0, turn(plane, 1, 1))


def to_right(at, plane):
    return jnp.where(at.at_right, 0.0, turn(plane, -1, 1))


def own_columns(plane, place):
    return turn(plane, (place - 1) * WIDE + HALF, 1)


def density_kernel(groups, size, *refs):
    own, near, inner, scalars = refs[:4]
    others = refs[4 : len(refs) - 7]
    stiff_out, links_out, factor_out, wide_out, inside_out, f_rows, s_rows = refs[len(refs) - 7 :]
    width, thick = near.shape[0] // 4, near.shape[1]
    at = Spot(groups, size, width, thick)
    two, three = RMIN - math.sqrt(2.0), RMIN - math.sqrt(3.0)
    planes = frame_of(own, near) + [plane_of(inner, k, width) for k in (0, 1)]
    strip = jnp.zeros(at.shape, jnp.float32)
    for place in range(PLACES):
        strip = jnp.where(at.where == place, turn(planes[place], place * GROUP + HALF, 1), strip)
    inside_out[...] = strip
    for ref in (f_rows, s_rows):
        border(ref, width)
    for place in range(PLACES):
        f_rows[place, 8 : 8 + width] = planes[place]

    count_y = jnp.where(at.first, 0.0, 1.0) + jnp.where(at.last, 0.0, 1.0)
    places_z = at.layer * thick + at.lane
    count_z = jnp.where(places_z >= 1, 1.0, 0.0) + jnp.where(places_z < groups * thick - 1, 1.0, 0.0)
    head, side = count_terms(count_y, count_z)
    over_two, over_one = 1.0 / (head + 2.0 * side), 1.0 / (head + side)
    straight, once, twice = [], [], []
    for place in range(PLACES):
        plane = planes[place]
        by_y = f_rows[place, 7 : 7 + width] + f_rows[place, 9 : 9 + width]
        straight.append(2.0 * plane + by_y)
        once.append(plane + two * by_y)
        twice.append(two * plane + three * by_y)
    filtered = {}
    for place in range(1, PLACES - 1):
        beside = once[place] + (twice[place - 1] + twice[place + 1])
        total = straight[place] + (once[place - 1] + once[place + 1]) + (to_left(at, beside) + to_right(at, beside))
        count_x = at.real[place - 1] + at.real[place + 1]
        filtered[place] = total * jnp.where(count_x > 1.5, over_two, over_one)

    for k, (is_right, _) in enumerate(at.sides()):
        block, _ = at.wide(is_right)
        strip = jnp.zeros(at.shape, jnp.float32)
        for place in range(1, PLACES - 1):
            strip = jnp.where(block == place - 1, own_columns(filtered[place], place), strip)
        wide_out[k] = strip

    for g in range(groups):
        eta, weight = weights_of(at, scalars, others, g)
        stiffness, factor = projection(eta)
        stiff = {}
        for place in range(1, PLACES - 1):
            inner_part, value, stiff[place] = stiffness(filtered[place], at.real[place])
            if place in (4, 5):
                factor_out[g, place - 4] = factor(inner_part, value, weight)
            if 2 <= place < 8:
                s_rows[place - 2, 8 : 8 + width] = stiff[place]
                stiff_out[g, place - 2] = stiff[place]
        for place in range(2, 8):
            s = stiff[place]
            by_y = s_rows[place - 2, 7 : 7 + width] + s_rows[place - 2, 9 : 9 + width]
            by_z = to_left(at, s) + to_right(at, s)
            links_out[g, place - 2] = 3.0 * s + 0.5 * ((stiff[place - 1] + stiff[place + 1]) + by_z + by_y)


def image_of(at, stiff, rows_of_stiff, field, rows, place, before, after):
    v, s = field[place], stiff[place]
    width = at.width

    def beside(ref_and_start, first):
        ref, start = ref_and_start
        return ref[place - start, first : first + width]

    k_right = s + to_right(at, s)
    flow_z = k_right * (v - to_right(at, v))
    total = (after - before) + (flow_z - jnp.where(at.at_left, -(s * v), turn(flow_z, 1, 1)))
    s_up, s_down = beside(rows_of_stiff, 7), beside(rows_of_stiff, 9)
    v_up, v_down = beside(rows, 7), beside(rows, 9)
    return total + ((s + s_up) * (v - v_up) + (s + s_down) * (v - v_down))


def flow_x(stiff, field, place):
    return (stiff[place] + stiff[place + 1]) * (field[place] - field[place + 1])


def start_of(at, links, load, support, place):
    over = at.real[place] / jnp.maximum(links + PENALTY * support, 0.1)
    return over, load * over


def mask_strips_of(at, is_right, strip, which, parts):
    block, slot = at.wide(is_right)
    beyond = by_side(is_right, slot, WIDE - 1 - slot) < HALF
    for place, plane, source, held in parts:
        start = (place - 1) * WIDE - (held + 2 * which) * GROUP
        value = jnp.where(beyond, turn(source, start, 1), own_columns(plane, place))
        strip = jnp.where(block == place - 1, value, strip)
    return strip


def own_kernel(groups, size, *refs):
    stiff_in, links_in, own_masks, partner = refs[:4]
    z_out, w_out, q_out, over_out, totals_out, masks_out, s_rows, z_rows, w_rows = refs[4:]
    width, thick = stiff_in.shape[2:]
    partner_masks = partner.at[2 * width :]
    at = Spot(groups, size, width, thick)
    for ref in (s_rows, z_rows, w_rows):
        border(ref, width)
    order = ((own_masks, 0), (own_masks, 1), (partner_masks, 1), (partner_masks, 0))
    load, support = (
        {place + 4: plane_of(ref, 2 * which + k, width) for place, (ref, k) in enumerate(order)} for which in (0, 1)
    )
    mine, theirs = spread(own_masks[4 * width :]), spread(partner_masks[4 * width :])
    for k, (is_right, _) in enumerate(at.sides()):
        for which, mask in enumerate((load, support)):
            sources = ((mine, 0), (mine, 1), (theirs, 1), (theirs, 0))
            parts = [(place + 4, mask[place + 4], *source) for place, source in enumerate(sources)]
            masks_out[which, k] = mask_strips_of(at, is_right, jnp.zeros(at.shape, jnp.float32), which, parts)

    counted = at.counted()
    for g in range(groups):
        stiff = {place: stiff_in[g, place - 2] for place in range(4, 8)}
        over, z = {}, {}
        for place in range(4, 8):
            over[place], z[place] = start_of(at, links_in[g, place - 2], load[place], support[place], place)
            z_out[g, place - 4] = z[place]
        over_out[g] = over[4]
        for place in (4, 5, 6):
            s_rows[place - 4, 8 : 8 + width] = stiff[place]
            z_rows[place - 4, 8 : 8 + width] = z[place]
        flows = {3: 0.0} | {place: flow_x(stiff, z, place) for place in (4, 5, 6)}
        q, w = {}, {}
        for place in (4, 5, 6):
            q[place] = 0.5 * image_of(at, stiff, (s_rows, 4), z, (z_rows, 4), place, flows[place - 1], flows[place])
        for place in (5, 6):
            w[place] = q[place] * over[place]
            w_out[g, place - 5] = w[place]
        q_out[g] = q[4]
        w_rows[0, 8 : 8 + width] = w[5]
        aw = 0.5 * image_of(at, stiff, (s_rows, 4), w, (w_rows, 5), 5, 0.0, flow_x(stiff, w, 5))
        terms = (z[4] + z[5], z[5] * q[5], q[5] * w[5], w[5] * aw)
        for k, term in enumerate(terms):
            totals_out[4 * g + k : 4 * g + k + 1] = jnp.sum(term * counted, axis=0, keepdims=True)


def near_kernel(groups, size, *refs):
    stiff_in, links_in, near_masks, z_in, w_in, q_in, over_in, totals_in, masks_in = refs[:9]
    totals_out, z_out, w_out, masks_out, s_rows, z_rows, w_rows = refs[9:]
    width, thick = stiff_in.shape[2:]
    at = Spot(groups, size, width, thick)
    for ref in (s_rows, z_rows, w_rows):
        border(ref, width)
    load, support = (
        {place: plane_of(near_masks, 2 * which + 3 - place, width) for place in (2, 3)} for which in (0, 1)
    )
    nears = spread(near_masks[4 * width :])
    for k, (is_right, _) in enumerate(at.sides()):
        for which, mask in enumerate((load, support)):
            parts = [(place, mask[place], nears, 3 - place) for place in (2, 3)]
            masks_out[which, k] = mask_strips_of(at, is_right, masks_in[which, k], which, parts)

    counted = at.counted()
    for g in range(groups):
        stiff = {place: stiff_in[g, place - 2] for place in range(2, 6)}
        z = {4: z_in[g, 0]}
        over = {4: over_in[g]}
        for place in (2, 3):
            over[place], z[place] = start_of(at, links_in[g, place - 2], load[place], support[place], place)
        z_out[g] = z[3]
        for place in (3, 4):
            s_rows[place - 3, 8 : 8 + width] = stiff[place]
        z_rows[0, 8 : 8 + width] = z[3]
        flows = {place: flow_x(stiff, z, place) for place in (2, 3)}
        q = 0.5 * image_of(at, stiff, (s_rows, 3), z, (z_rows, 3), 3, flows[2], flows[3])
        q = {3: q, 4: q_in[g] - 0.5 * flows[3]}
        w = {place: q[place] * over[place] for place in (3, 4)} | {5: w_in[g, 0]}
        for place in (3, 4):
            w_out[g, place - 3] = w[place]
        w_rows[0, 8 : 8 + width] = w[4]
        flows = {place: flow_x(stiff, w, place) for place in (3, 4)}
        aw = 0.5 * image_of(at, stiff, (s_rows, 3), w, (w_rows, 4), 4, flows[3], flows[4])
        terms = (None, z[4] * q[4], q[4] * w[4], w[4] * aw - w[5] * (0.5 * flows[4]))
        for k, term in enumerate(terms):
            row = totals_in[4 * g + k : 4 * g + k + 1]
            if term is not None:
                row = row + jnp.sum(term * counted, axis=0, keepdims=True)
            totals_out[4 * g + k : 4 * g + k + 1] = row


def edge_kernel(groups, size, *refs):
    n_side = 1 if groups == 2 else 2
    inside, wide, masks, totals, factors, scalars = refs[:6]
    beside, crossed = refs[6 : 6 + n_side], refs[6 + n_side : 6 + 2 * n_side]
    others = refs[6 + 2 * n_side : len(refs) - 3]
    table, strip_out, factor_out = refs[len(refs) - 3 :]
    width, thick = inside.shape
    at = Spot(groups, size, width, thick)
    first, last = at.first, at.last
    two, three = RMIN - math.sqrt(2.0), RMIN - math.sqrt(3.0)

    outside = []
    for k in range(n_side):
        lower = at.layer == 1 if groups == 2 else k == 0
        group = lanes_of(beside[k].shape) // GROUP
        strip = jnp.where(group < 8, beside[k][...], spread(crossed[k][...], 8 * GROUP))
        outside.append(unfold(jnp.where(group < PLACES, strip, 0.0), lower))
    outside = [outside[0] * at.has_left, outside[-1] * at.has_right]
    fixed = at.strips(inside[...], outside)

    count_y = jnp.where(first, 0.0, 1.0) + jnp.where(last, 0.0, 1.0)
    count_x = at.real_at(at.where - 1) + at.real_at(at.where + 1)
    span_z = thick * groups
    filtered, presents, counts = [], [], []
    for k, (strip, z_at, (is_right, present)) in enumerate(zip(fixed, at.strip_z(), at.sides())):
        by_y = around_y(strip, first, last)
        once = strip + two * by_y
        twice = two * strip + three * by_y
        total = 2.0 * strip + by_y
        for step in (GROUP, -GROUP, 1, -1):
            total = total + turn(once, step, 1)
        for step in (GROUP + 1, GROUP - 1, 1 - GROUP, -1 - GROUP):
            total = total + turn(twice, step, 1)
        count_z = jnp.where(z_at >= 1, 1.0, 0.0) + jnp.where(z_at < span_z - 1, 1.0, 0.0)
        head, side = count_terms(count_y, count_z)
        total = total * (1.0 / (head + count_x * side))
        value = wide[k]
        block, slot = at.wide(is_right)
        better = by_side(is_right, slot, WIDE - 1 - slot) <= HALF
        for place in range(1, PLACES - 1):
            moved = turn(total, (place - 1) * WIDE - place * GROUP, 1)
            value = jnp.where(better & (block == place - 1), moved, value)
        filtered.append(value)
        z_wide = at.layer * thick + slot + by_side(is_right, -HALF, thick - WIDE + HALF)
        presents.append(jnp.where((z_wide >= 0) & (z_wide < span_z), at.real_at(block + 1), 0.0))
        own = by_side(is_right, slot, WIDE - 1 - slot)
        own = (own >= HALF) & (own < 2 * HALF) & (block >= 3) & (block < 5)
        counts.append(jnp.where(own, present, 0.0))

    def around(v):
        up, down = jnp.where(first, 0.0, turn(v, 1, 0)), jnp.where(last, 0.0, turn(v, -1, 0))
        return [turn(v, shift, 1) for shift in (WIDE, -WIDE, 1, -1)] + [up, down]

    lane_row = lanes_of((1, thick))
    line = jnp.zeros((1, thick), jnp.float32)
    for g in range(groups):
        eta, weight = weights_of(at, scalars, others, g)
        stiffness, factor = projection(eta)
        sums = [totals[4 * g + k : 4 * g + k + 1] for k in range(4)]
        patched = [factors[g, 0], factors[g, 1]]
        for k, (is_right, present) in enumerate(at.sides()):
            inner_part, value, s = stiffness(filtered[k], presents[k])
            of_place = factor(inner_part, value, weight)
            for place in (0, 1):
                here = at.held(is_right) & (present > 0.5)
                patched[place] = jnp.where(here, of_strip(of_place, place + 4), patched[place])
            beside_s = around(s)
            links = 6.0 * s + sum(beside_s[1:], beside_s[0])
            inverse = presents[k] / jnp.maximum(0.5 * links + PENALTY * masks[1, k], 0.1)
            pairs = [s + other for other in beside_s]

            def image(v):
                terms = [pair * (v - other) for pair, other in zip(pairs, around(v))]
                return 0.5 * ((terms[0] + terms[1]) + (terms[2] + terms[3]) + (terms[4] + terms[5]))

            z = masks[0, k] * inverse
            q = image(z)
            w = q * inverse
            strip_out[g, 0, k] = z
            strip_out[g, 1, k] = w
            terms = (z, z * q, q * w, w * image(w))
            sums = [a + jnp.sum(b * counts[k], axis=0, keepdims=True) for a, b in zip(sums, terms)]
        for place in (0, 1):
            factor_out[g, place] = patched[place]
        for k, part in enumerate(sums):
            line = jnp.where(lane_row == 4 * g + k, jnp.sum(part, axis=1, keepdims=True), line)
    table[...] = jnp.broadcast_to(line, table.shape)


def finish(groups, size, table, z_near, z_own, w_near, w_own, strips, factors, out):
    width, thick = out.shape[1:]
    at = Spot(groups, size, width, thick)
    core = lax.rem(at.spot, 2)
    line = jnp.sum(table[...], axis=0, keepdims=True)
    lane_row = lanes_of((1, thick))
    total = [jnp.zeros(at.shape, jnp.float32), jnp.zeros(at.shape, jnp.float32)]
    for g in range(groups):
        m0, m1, m2, m3 = (
            jnp.sum(jnp.where(lane_row == 4 * g + k, line, 0.0), axis=1, keepdims=True) for k in range(4)
        )
        step_one = m0 / m1
        rz_next = step_one * step_one * m2 - m0
        factor = rz_next / m0
        curve = (m1 - 2.0 * step_one * m2 + step_one * step_one * m3) - factor * factor * m1
        step_two = rz_next / curve
        of_z = step_one + step_two * (1.0 + factor)
        of_w = -step_one * step_two
        z = [z_near[g], z_own[g, 0], z_own[g, 1], z_own[g, 2]]
        w = [w_near[g, 0], w_near[g, 1], w_own[g, 0], w_own[g, 1]]
        u = [of_z * v + of_w * t for v, t in zip(z, w)]
        ends = {1: [0.0, 0.0], 2: [0.0, 0.0]}
        for k, (is_right, present) in enumerate(at.sides()):
            strip = of_z * strips[g, 0, k] + of_w * strips[g, 1, k]
            here = at.held(is_right) & (present > 0.5)
            for place in range(4):
                part = of_strip(strip, place + 3)
                u[place] = jnp.where(here, part, u[place])
                if place in ends:
                    if at.n_strips == 1:
                        ends[place] = [part * at.has_left, part * at.has_right]
                    else:
                        ends[place][k] = part * present
        between = [u[k] - u[k + 1] for k in range(3)]
        for k in (1, 2):
            plane = u[k]
            left = turn(jnp.where(at.at_right, ends[k][0], plane), 1, 1)
            right = turn(jnp.where(at.at_left, ends[k][1], plane), -1, 1)
            up = jnp.where(at.first, 0.0, turn(plane, 1, 0))
            down = jnp.where(at.last, 0.0, turn(plane, -1, 0))
            steps = [between[k - 1], between[k]] + [plane - other for other in (left, right, up, down)]
            squares = [v * v for v in steps]
            total[k - 1] = total[k - 1] + factors[g, k - 1] * sum(squares[1:], squares[0])
    for k in range(2):
        out[lax.rem(k + core, 2)] = total[k]


def call(body, outs, *args, scalars=(), scratch=(), flops=0):
    smem = pl.BlockSpec(memory_space=pltpu.SMEM)
    return pl.pallas_call(
        body,
        out_shape=[jax.ShapeDtypeStruct(shape, jnp.float32) for shape in outs],
        in_specs=[pl.BlockSpec(memory_space=pltpu.VMEM)] * len(args) + [smem] * len(scalars),
        out_specs=[pl.BlockSpec(memory_space=pltpu.VMEM)] * len(outs),
        scratch_shapes=[pltpu.VMEM(shape, jnp.float32) for shape in scratch],
        cost_estimate=pl.CostEstimate(flops=flops, transcendentals=0, bytes_accessed=0) if flops else None,
        compiler_params=pltpu.CompilerParams(vmem_limit_bytes=32 * 1024 * 1024),
    )(*args, *scalars)


def local(design, solid_mask, void_mask, load_mask, support_mask, thresholds, group_weight):
    depth, width, thick = design.shape
    size, groups = lax.axis_size("space"), lax.axis_size("proj")
    quarter = width // 4
    pair, near_pairs = pair_swap(size), near_swap(size)
    fixed = jnp.where(solid_mask == 1, 1.0, jnp.where(void_mask == 1, 0.0, design))
    (packed_own,) = call(
        functools.partial(prepare, groups), [(6 * width + quarter, thick)], fixed, load_mask, support_mask
    )
    partner = lax.ppermute(packed_own, "space", pair)
    own, own_masks, scalars = call(
        join, [(4 * width, thick), (4 * width + quarter, thick), (8, thick)], packed_own, partner,
        scalars=(thresholds, group_weight),
    )
    others = [lax.ppermute(scalars, "proj", [((g + k) % groups, g) for g in range(groups)]) for k in range(1, groups)]
    near = lax.ppermute(own, "space", near_pairs)
    near_masks = lax.ppermute(own_masks, "space", near_pairs)
    others = [call(keep, [other.shape], other, flops=1_650_000_000)[0] for other in others]
    steps = (1,) if groups == 2 else (1, -1)
    packed = call(
        functools.partial(pack, groups),
        [(width // 2, thick)] * len(steps) + [(width // 8, thick)] * len(steps),
        own, near,
    )
    straight = [(i, i) for i in range(size)]
    both = ("proj", "space")
    beside = [lax.ppermute(v, both, both_axes(straight, size, groups, k)) for k, v in zip(steps, packed)]
    crossed = [lax.ppermute(v, both, both_axes(pair, size, groups, k)) for k, v in zip(steps, packed[len(steps) :])]
    (beyond,) = call(pick, [(2 * width, thick)], near, packed[0])
    inner = lax.ppermute(beyond, "space", pair)
    n_strips = 1 if groups == 2 else 2
    plane = (width, thick)
    six = (groups, 6, *plane)
    stiff, links, factors, wide, inside = call(
        functools.partial(density_kernel, groups, size),
        [six, six, (groups, 2, *plane), (n_strips, *plane), plane],
        own, near, inner, scalars, *others,
        flops=1,
        scratch=[(PLACES, width + 16, thick), (6, width + 16, thick)],
    )
    one, two, four = (groups, *plane), (groups, 2, *plane), (groups, 4, *plane)
    strips_shape = (2, n_strips, *plane)
    sums = (-(-4 * groups // 8) * 8, thick)
    z_own, w_own, q_own, over_own, totals, mask_strips = call(
        functools.partial(own_kernel, groups, size),
        [four, two, one, one, sums, strips_shape],
        stiff, links, own_masks, partner,
        flops=1,
        scratch=[(3, width + 16, thick), (3, width + 16, thick), (1, width + 16, thick)],
    )
    totals, z_near, w_near, mask_strips = call(
        functools.partial(near_kernel, groups, size),
        [sums, one, two, strips_shape],
        stiff, links, near_masks, z_own, w_own, q_own, over_own, totals, mask_strips,
        flops=1,
        scratch=[(2, width + 16, thick), (1, width + 16, thick), (1, width + 16, thick)],
    )
    table, strips, factors = call(
        functools.partial(edge_kernel, groups, size),
        [(size * groups, thick), (groups, 2, n_strips, *plane), (groups, 2, *plane)],
        inside, wide, mask_strips, totals, factors, scalars, *beside, *crossed, *others,
    )
    table = lax.all_to_all(table, ("proj", "space"), 0, 0, tiled=True)
    (out,) = call(functools.partial(finish, groups, size), [(depth, *plane)], table, z_near, z_own, w_near, w_own, strips, factors)
    return out


def solution(mesh):
    placed = (
        P("space", None, "proj"),
        P("space", None, "proj"),
        P("space", None, "proj"),
        P("space", None, None),
        P("space", None, None),
        P("proj"),
        P("proj"),
    )
    return jax.shard_map(
        local, mesh=mesh, in_specs=placed, out_specs=P("space", None, "proj"), check_vma=False
    )
```

```python
import functools
import math

import jax
import jax.numpy as jnp
from jax import lax
from jax.experimental import pallas as pl
from jax.experimental.pallas import tpu as pltpu
from jax.sharding import PartitionSpec as P

RMIN = 2.0
BETA = 8.0
EMIN = 0.05
PENALTY = 4.0

PLACES = 10
GROUP = 8
HALF = GROUP // 2
WIDE = 2 * GROUP
INNER = PLACES - 2


def pair_swap(size):
    return [(i, i ^ 1) for i in range(size)]


def near_swap(size):
    ups = [(i, i + 1) for i in range(1, size - 1, 2)]
    return ups + [(j, i) for i, j in ups]


def both_axes(pairs, size, groups, step):
    return [
        (g * size + i, (g + step) % groups * size + j)
        for g in range(groups)
        for i, j in pairs
        if groups == 2 or 0 <= g + step < groups
    ]


def lanes_of(shape):
    return lax.broadcasted_iota(jnp.int32, shape, len(shape) - 1)


def turn(array, shift, axis):
    return pltpu.roll(array, shift % array.shape[axis], axis)


def squeeze(strips):
    rows, lanes = strips.shape[0] // 4, strips.shape[1]
    parts = [turn(strips[k * rows : (k + 1) * rows], k * lanes // 4, 1) for k in range(4)]
    block = lanes_of((rows, lanes)) // (lanes // 4)
    return functools.reduce(lambda out, k: jnp.where(block == k, parts[k], out), range(1, 4), parts[0])


def spread(squeezed, start=0):
    lanes = squeezed.shape[1]
    return jnp.concatenate([turn(squeezed, start - k * lanes // 4, 1) for k in range(4)], axis=0)


def prepare(groups, fixed, load, support, out):
    core = lax.rem(lax.axis_index("space"), 2)
    layer = lax.axis_index("proj")
    width, thick = load.shape[1], load.shape[2] // groups
    quarter = width // 4
    lane = lanes_of((quarter, thick))
    lower = lax.rem(lane, GROUP) < HALF
    has_left = layer > 0
    has_right = layer < groups - 1
    centre = pl.ds(pl.multiple_of(layer * thick, thick), thick)
    left = pl.ds(pl.multiple_of(jnp.maximum(layer - 1, 0) * thick, thick), thick)
    right = pl.ds(pl.multiple_of(jnp.minimum(layer + 1, groups - 1) * thick, thick), thick)
    strips = jnp.zeros((quarter, thick), jnp.float32)
    for place in range(2):
        plane = lax.rem(place + core, 2)
        out[place * width : (place + 1) * width] = fixed[plane]
        for which, mask in enumerate((load, support)):
            held = 2 * which + place
            out[(2 + held) * width : (3 + held) * width] = mask[plane, :, centre].astype(jnp.float32)
            before = jnp.where(has_left, mask[plane, :, left].astype(jnp.float32), 0.0)
            after = jnp.where(has_right, mask[plane, :, right].astype(jnp.float32), 0.0)
            for block in range(4):
                rows = slice(block * quarter, (block + 1) * quarter)
                shift = held * GROUP + HALF + block * (thick // 4)
                outside = jnp.where(lower, turn(before[rows], shift, 1), turn(after[rows], shift, 1))
                strips = jnp.where(lane // GROUP == held + block * (thick // (4 * GROUP)), outside, strips)
    out[6 * width :] = strips


def join(own, partner, thresholds, weights, near_out, mask_out, scalars):
    rows = near_out.shape[0] // 2
    near_out[0:rows] = own[0:rows]
    near_out[rows:] = partner[0:rows]
    mask_out[...] = own[rows:]
    row = lax.broadcasted_iota(jnp.int32, scalars.shape, 0)
    scalars[...] = jnp.where(row == 0, thresholds[0].astype(jnp.float32) / 1000.0, jnp.where(row == 1, weights[0], 0.0))


def keep(array, *refs):
    refs[-1][...] = array[...]


def pick(near, *refs):
    out = refs[-1]
    out[...] = near[0 : out.shape[0]]


def plane_of(ref, k, width):
    return ref[k * width : (k + 1) * width]


def frame_of(own, near):
    order = ((near, 2), (near, 3), (near, 1), (near, 0), (own, 0), (own, 1), (own, 3), (own, 2))
    return [plane_of(ref, k, near.shape[0] // 4) for ref, k in order]


def folded(planes, lower, offset=0):
    half, lanes = planes[0].shape[0] // 2, planes[0].shape[1]
    lane = lanes_of((half, lanes))
    low, group = lax.rem(lane, GROUP) < HALF, lane // GROUP
    out = jnp.zeros((half, lanes), jnp.float32)
    for place, plane in enumerate(planes):
        start = place * GROUP + HALF + offset
        top, bottom = turn(plane[:half], start, 1), plane[half:]
        of_lower = jnp.where(low, top, turn(bottom, start + HALF, 1))
        of_upper = jnp.where(low, turn(bottom, start - HALF, 1), top)
        out = jnp.where(group == place + offset // GROUP, jnp.where(lower, of_lower, of_upper), out)
    return out


def unfold(folded, lower):
    return jnp.concatenate([folded, jnp.where(lower, turn(folded, -HALF, 1), turn(folded, HALF, 1))], axis=0)


def pack(groups, own, near, *outs):
    planes = frame_of(own, near)
    sides = (lax.axis_index("proj") == 0,) if groups == 2 else (True, False)
    for k, lower in enumerate(sides):
        outs[k][...] = folded(planes, lower)
        rows, lanes = outs[len(sides) + k].shape
        parts = []
        for block in range(4):
            starts = (block * rows, (block + 4) * rows)
            pieces = [jnp.concatenate([p[i : i + rows] for i in starts], axis=0) for p in (planes[3], planes[2])]
            parts.append(folded(pieces, lower, block * (lanes // 4)))
        outs[len(sides) + k][...] = (parts[0] + parts[1]) + (parts[2] + parts[3])


def around_y(plane, first, last):
    return jnp.where(first, 0.0, turn(plane, 1, 0)) + jnp.where(last, 0.0, turn(plane, -1, 0))


class Spot:
    def __init__(self, groups, size, width, thick):
        self.groups, self.width, self.thick = groups, width, thick
        self.spot, self.layer = lax.axis_index("space"), lax.axis_index("proj")
        core = lax.rem(self.spot, 2)
        self.shape = (width, thick)
        self.lane = lanes_of(self.shape)
        row = lax.broadcasted_iota(jnp.int32, self.shape, 0)
        self.first, self.last = row == 0, row == width - 1
        self.at_left, self.at_right = self.lane == 0, self.lane == thick - 1
        self.where = self.lane // GROUP
        self.slot = lax.rem(self.lane, GROUP)
        self.lower = self.slot < HALF
        self.near_real = jnp.where(jnp.where(core == 0, self.spot > 0, self.spot < size - 1), 1.0, 0.0)
        self.inner_real = jnp.where(jnp.where(core == 0, self.spot < size - 2, self.spot > 1), 1.0, 0.0)
        self.real = [self.near_real] * 4 + [1.0] * 4 + [self.inner_real] * 2
        self.has_left = jnp.where(self.layer > 0, 1.0, 0.0)
        self.has_right = jnp.where(self.layer < groups - 1, 1.0, 0.0)
        self.n_strips = 1 if groups == 2 else 2
        self.is_right = self.layer == 0

    def real_at(self, places):
        return jnp.where(places < 4, self.near_real, jnp.where(places < 8, 1.0, self.inner_real))

    def strips(self, inside, outside):
        right = jnp.where(self.lower, inside, outside[-1])
        left = jnp.where(self.lower, outside[0], inside)
        return [jnp.where(self.is_right, right, left)] if self.n_strips == 1 else [left, right]

    def strip_z(self):
        left, right = (self.layer * self.thick + self.slot + shift for shift in (-HALF, self.thick - HALF))
        return [jnp.where(self.is_right, right, left)] if self.n_strips == 1 else [left, right]

    def sides(self):
        if self.n_strips == 1:
            return [(self.is_right, 1.0)]
        return [(False, self.has_left), (True, self.has_right)]

    def wide(self, is_right):
        lane = lax.rem(self.lane + by_side(is_right, 0, WIDE // 2), self.thick)
        return lane // WIDE, lax.rem(lane, WIDE)

    def counted(self):
        counted = jnp.ones(self.shape, jnp.float32)
        for is_right, present in self.sides():
            counted = jnp.where(self.held(is_right), 1.0 - present, counted)
        return counted

    def held(self, is_right):
        right, left = self.lane >= self.thick - HALF, self.lane < HALF
        if isinstance(is_right, bool):
            return right if is_right else left
        return jnp.where(is_right, self.lane, self.thick - 1 - self.lane) >= self.thick - HALF


def by_side(is_right, left, right):
    if isinstance(is_right, bool):
        return right if is_right else left
    return jnp.where(is_right, right, left)


def of_strip(strip, place):
    return turn(strip, -((place - 1) * WIDE + HALF), 1)


def count_terms(count_y, count_z):
    two, three = RMIN - math.sqrt(2.0), RMIN - math.sqrt(3.0)
    head = 2.0 + (count_y + count_z) + two * (count_y * count_z)
    side = 1.0 + two * (count_y + count_z) + three * (count_y * count_z)
    return head, side


def weights_of(at, packed, others, g):
    eta, weight = packed[0:1], packed[1:2]
    for k, other in enumerate(others):
        mine = lax.rem(at.layer + k + 1, at.groups) == g
        eta = jnp.where(mine, other[0:1], eta)
        weight = jnp.where(mine, other[1:2], weight)
    return eta, weight


def projection(eta):
    low = jnp.tanh(BETA * eta)
    over_bottom = 1.0 / (low + jnp.tanh(BETA * (1.0 - eta)))

    def stiffness(density, present):
        inner_part = jnp.tanh(BETA * (density - eta))
        value = (low + inner_part) * over_bottom
        return inner_part, value, (EMIN + (1.0 - EMIN) * (value * value * value)) * present

    def factor(inner_part, value, weight):
        slope = (BETA * over_bottom) * (1.0 - inner_part * inner_part)
        return (-0.5 * 3.0 * (1.0 - EMIN)) * weight * (value * value) * slope

    return stiffness, factor


def border(ref, width):
    ref[:, 0:8] = jnp.zeros((ref.shape[0], 8, ref.shape[2]), jnp.float32)
    ref[:, 8 + width :] = jnp.zeros((ref.shape[0], 8, ref.shape[2]), jnp.float32)


def to_left(at, plane):
    return jnp.where(at.at_left, 0.0, turn(plane, 1, 1))


def to_right(at, plane):
    return jnp.where(at.at_right, 0.0, turn(plane, -1, 1))


def own_columns(plane, place):
    return turn(plane, (place - 1) * WIDE + HALF, 1)


def density_kernel(groups, size, *refs):
    own, near, inner, scalars = refs[:4]
    others = refs[4 : len(refs) - 7]
    stiff_out, links_out, factor_out, wide_out, inside_out, f_rows, s_rows = refs[len(refs) - 7 :]
    width, thick = near.shape[0] // 4, near.shape[1]
    at = Spot(groups, size, width, thick)
    two, three = RMIN - math.sqrt(2.0), RMIN - math.sqrt(3.0)
    planes = frame_of(own, near) + [plane_of(inner, k, width) for k in (0, 1)]
    strip = jnp.zeros(at.shape, jnp.float32)
    for place in range(PLACES):
        strip = jnp.where(at.where == place, turn(planes[place], place * GROUP + HALF, 1), strip)
    inside_out[...] = strip
    for ref in (f_rows, s_rows):
        border(ref, width)
    for place in range(PLACES):
        f_rows[place, 8 : 8 + width] = planes[place]

    count_y = jnp.where(at.first, 0.0, 1.0) + jnp.where(at.last, 0.0, 1.0)
    places_z = at.layer * thick + at.lane
    count_z = jnp.where(places_z >= 1, 1.0, 0.0) + jnp.where(places_z < groups * thick - 1, 1.0, 0.0)
    head, side = count_terms(count_y, count_z)
    over_two, over_one = 1.0 / (head + 2.0 * side), 1.0 / (head + side)
    straight, once, twice = [], [], []
    for place in range(PLACES):
        plane = planes[place]
        by_y = f_rows[place, 7 : 7 + width] + f_rows[place, 9 : 9 + width]
        straight.append(2.0 * plane + by_y)
        once.append(plane + two * by_y)
        twice.append(two * plane + three * by_y)
    filtered = {}
    for place in range(1, PLACES - 1):
        beside = once[place] + (twice[place - 1] + twice[place + 1])
        total = straight[place] + (once[place - 1] + once[place + 1]) + (to_left(at, beside) + to_right(at, beside))
        count_x = at.real[place - 1] + at.real[place + 1]
        filtered[place] = total * jnp.where(count_x > 1.5, over_two, over_one)

    for k, (is_right, _) in enumerate(at.sides()):
        block, _ = at.wide(is_right)
        strip = jnp.zeros(at.shape, jnp.float32)
        for place in range(1, PLACES - 1):
            strip = jnp.where(block == place - 1, own_columns(filtered[place], place), strip)
        wide_out[k] = strip

    for g in range(groups):
        eta, weight = weights_of(at, scalars, others, g)
        stiffness, factor = projection(eta)
        stiff = {}
        for place in range(1, PLACES - 1):
            inner_part, value, stiff[place] = stiffness(filtered[place], at.real[place])
            if place in (4, 5):
                factor_out[g, place - 4] = factor(inner_part, value, weight)
            if 2 <= place < 8:
                s_rows[place - 2, 8 : 8 + width] = stiff[place]
                stiff_out[g, place - 2] = stiff[place]
        for place in range(2, 8):
            s = stiff[place]
            by_y = s_rows[place - 2, 7 : 7 + width] + s_rows[place - 2, 9 : 9 + width]
            by_z = to_left(at, s) + to_right(at, s)
            links_out[g, place - 2] = 3.0 * s + 0.5 * ((stiff[place - 1] + stiff[place + 1]) + by_z + by_y)


def image_of(at, stiff, rows_of_stiff, field, rows, place, before, after):
    v, s = field[place], stiff[place]
    width = at.width

    def beside(ref_and_start, first):
        ref, start = ref_and_start
        return ref[place - start, first : first + width]

    k_right = s + to_right(at, s)
    flow_z = k_right * (v - to_right(at, v))
    total = (after - before) + (flow_z - jnp.where(at.at_left, -(s * v), turn(flow_z, 1, 1)))
    s_up, s_down = beside(rows_of_stiff, 7), beside(rows_of_stiff, 9)
    v_up, v_down = beside(rows, 7), beside(rows, 9)
    return total + ((s + s_up) * (v - v_up) + (s + s_down) * (v - v_down))


def flow_x(stiff, field, place):
    return (stiff[place] + stiff[place + 1]) * (field[place] - field[place + 1])


def start_of(at, links, load, support, place):
    over = at.real[place] / jnp.maximum(links + PENALTY * support, 0.1)
    return over, load * over


def mask_strips_of(at, is_right, strip, which, parts):
    block, slot = at.wide(is_right)
    beyond = by_side(is_right, slot, WIDE - 1 - slot) < HALF
    for place, plane, source, held in parts:
        start = (place - 1) * WIDE - (held + 2 * which) * GROUP
        value = jnp.where(beyond, turn(source, start, 1), own_columns(plane, place))
        strip = jnp.where(block == place - 1, value, strip)
    return strip


def own_kernel(groups, size, *refs):
    stiff_in, links_in, own_masks, partner = refs[:4]
    z_out, w_out, q_out, over_out, totals_out, masks_out, s_rows, z_rows, w_rows = refs[4:]
    width, thick = stiff_in.shape[2:]
    partner_masks = partner.at[2 * width :]
    at = Spot(groups, size, width, thick)
    for ref in (s_rows, z_rows, w_rows):
        border(ref, width)
    order = ((own_masks, 0), (own_masks, 1), (partner_masks, 1), (partner_masks, 0))
    load, support = (
        {place + 4: plane_of(ref, 2 * which + k, width) for place, (ref, k) in enumerate(order)} for which in (0, 1)
    )
    mine, theirs = spread(own_masks[4 * width :]), spread(partner_masks[4 * width :])
    for k, (is_right, _) in enumerate(at.sides()):
        for which, mask in enumerate((load, support)):
            sources = ((mine, 0), (mine, 1), (theirs, 1), (theirs, 0))
            parts = [(place + 4, mask[place + 4], *source) for place, source in enumerate(sources)]
            masks_out[which, k] = mask_strips_of(at, is_right, jnp.zeros(at.shape, jnp.float32), which, parts)

    counted = at.counted()
    for g in range(groups):
        stiff = {place: stiff_in[g, place - 2] for place in range(4, 8)}
        over, z = {}, {}
        for place in range(4, 8):
            over[place], z[place] = start_of(at, links_in[g, place - 2], load[place], support[place], place)
            z_out[g, place - 4] = z[place]
        over_out[g] = over[4]
        for place in (4, 5, 6):
            s_rows[place - 4, 8 : 8 + width] = stiff[place]
            z_rows[place - 4, 8 : 8 + width] = z[place]
        flows = {3: 0.0} | {place: flow_x(stiff, z, place) for place in (4, 5, 6)}
        q, w = {}, {}
        for place in (4, 5, 6):
            q[place] = 0.5 * image_of(at, stiff, (s_rows, 4), z, (z_rows, 4), place, flows[place - 1], flows[place])
        for place in (5, 6):
            w[place] = q[place] * over[place]
            w_out[g, place - 5] = w[place]
        q_out[g] = q[4]
        w_rows[0, 8 : 8 + width] = w[5]
        aw = 0.5 * image_of(at, stiff, (s_rows, 4), w, (w_rows, 5), 5, 0.0, flow_x(stiff, w, 5))
        terms = (z[4] + z[5], z[5] * q[5], q[5] * w[5], w[5] * aw)
        for k, term in enumerate(terms):
            totals_out[4 * g + k : 4 * g + k + 1] = jnp.sum(term * counted, axis=0, keepdims=True)


def near_kernel(groups, size, *refs):
    stiff_in, links_in, near_masks, z_in, w_in, q_in, over_in, totals_in, masks_in = refs[:9]
    totals_out, z_out, w_out, masks_out, s_rows, z_rows, w_rows = refs[9:]
    width, thick = stiff_in.shape[2:]
    at = Spot(groups, size, width, thick)
    for ref in (s_rows, z_rows, w_rows):
        border(ref, width)
    load, support = (
        {place: plane_of(near_masks, 2 * which + 3 - place, width) for place in (2, 3)} for which in (0, 1)
    )
    nears = spread(near_masks[4 * width :])
    for k, (is_right, _) in enumerate(at.sides()):
        for which, mask in enumerate((load, support)):
            parts = [(place, mask[place], nears, 3 - place) for place in (2, 3)]
            masks_out[which, k] = mask_strips_of(at, is_right, masks_in[which, k], which, parts)

    counted = at.counted()
    for g in range(groups):
        stiff = {place: stiff_in[g, place - 2] for place in range(2, 6)}
        z = {4: z_in[g, 0]}
        over = {4: over_in[g]}
        for place in (2, 3):
            over[place], z[place] = start_of(at, links_in[g, place - 2], load[place], support[place], place)
        z_out[g] = z[3]
        for place in (3, 4):
            s_rows[place - 3, 8 : 8 + width] = stiff[place]
        z_rows[0, 8 : 8 + width] = z[3]
        flows = {place: flow_x(stiff, z, place) for place in (2, 3)}
        q = 0.5 * image_of(at, stiff, (s_rows, 3), z, (z_rows, 3), 3, flows[2], flows[3])
        q = {3: q, 4: q_in[g] - 0.5 * flows[3]}
        w = {place: q[place] * over[place] for place in (3, 4)} | {5: w_in[g, 0]}
        for place in (3, 4):
            w_out[g, place - 3] = w[place]
        w_rows[0, 8 : 8 + width] = w[4]
        flows = {place: flow_x(stiff, w, place) for place in (3, 4)}
        aw = 0.5 * image_of(at, stiff, (s_rows, 3), w, (w_rows, 4), 4, flows[3], flows[4])
        terms = (None, z[4] * q[4], q[4] * w[4], w[4] * aw - w[5] * (0.5 * flows[4]))
        for k, term in enumerate(terms):
            row = totals_in[4 * g + k : 4 * g + k + 1]
            if term is not None:
                row = row + jnp.sum(term * counted, axis=0, keepdims=True)
            totals_out[4 * g + k : 4 * g + k + 1] = row


def edge_kernel(groups, size, *refs):
    n_side = 1 if groups == 2 else 2
    inside, wide, masks, totals, factors, scalars = refs[:6]
    beside, crossed = refs[6 : 6 + n_side], refs[6 + n_side : 6 + 2 * n_side]
    others = refs[6 + 2 * n_side : len(refs) - 3]
    table, strip_out, factor_out = refs[len(refs) - 3 :]
    width, thick = inside.shape
    at = Spot(groups, size, width, thick)
    first, last = at.first, at.last
    two, three = RMIN - math.sqrt(2.0), RMIN - math.sqrt(3.0)

    outside = []
    for k in range(n_side):
        lower = at.layer == 1 if groups == 2 else k == 0
        group = lanes_of(beside[k].shape) // GROUP
        strip = jnp.where(group < 8, beside[k][...], spread(crossed[k][...], 8 * GROUP))
        outside.append(unfold(jnp.where(group < PLACES, strip, 0.0), lower))
    outside = [outside[0] * at.has_left, outside[-1] * at.has_right]
    fixed = at.strips(inside[...], outside)

    count_y = jnp.where(first, 0.0, 1.0) + jnp.where(last, 0.0, 1.0)
    count_x = at.real_at(at.where - 1) + at.real_at(at.where + 1)
    span_z = thick * groups
    filtered, presents, counts = [], [], []
    for k, (strip, z_at, (is_right, present)) in enumerate(zip(fixed, at.strip_z(), at.sides())):
        by_y = around_y(strip, first, last)
        once = strip + two * by_y
        twice = two * strip + three * by_y
        total = 2.0 * strip + by_y
        for step in (GROUP, -GROUP, 1, -1):
            total = total + turn(once, step, 1)
        for step in (GROUP + 1, GROUP - 1, 1 - GROUP, -1 - GROUP):
            total = total + turn(twice, step, 1)
        count_z = jnp.where(z_at >= 1, 1.0, 0.0) + jnp.where(z_at < span_z - 1, 1.0, 0.0)
        head, side = count_terms(count_y, count_z)
        total = total * (1.0 / (head + count_x * side))
        value = wide[k]
        block, slot = at.wide(is_right)
        better = by_side(is_right, slot, WIDE - 1 - slot) <= HALF
        for place in range(1, PLACES - 1):
            moved = turn(total, (place - 1) * WIDE - place * GROUP, 1)
            value = jnp.where(better & (block == place - 1), moved, value)
        filtered.append(value)
        z_wide = at.layer * thick + slot + by_side(is_right, -HALF, thick - WIDE + HALF)
        presents.append(jnp.where((z_wide >= 0) & (z_wide < span_z), at.real_at(block + 1), 0.0))
        own = by_side(is_right, slot, WIDE - 1 - slot)
        own = (own >= HALF) & (own < 2 * HALF) & (block >= 3) & (block < 5)
        counts.append(jnp.where(own, present, 0.0))

    def around(v):
        up, down = jnp.where(first, 0.0, turn(v, 1, 0)), jnp.where(last, 0.0, turn(v, -1, 0))
        return [turn(v, shift, 1) for shift in (WIDE, -WIDE, 1, -1)] + [up, down]

    lane_row = lanes_of((1, thick))
    line = jnp.zeros((1, thick), jnp.float32)
    for g in range(groups):
        eta, weight = weights_of(at, scalars, others, g)
        stiffness, factor = projection(eta)
        sums = [totals[4 * g + k : 4 * g + k + 1] for k in range(4)]
        patched = [factors[g, 0], factors[g, 1]]
        for k, (is_right, present) in enumerate(at.sides()):
            inner_part, value, s = stiffness(filtered[k], presents[k])
            of_place = factor(inner_part, value, weight)
            for place in (0, 1):
                here = at.held(is_right) & (present > 0.5)
                patched[place] = jnp.where(here, of_strip(of_place, place + 4), patched[place])
            beside_s = around(s)
            links = 6.0 * s + sum(beside_s[1:], beside_s[0])
            inverse = presents[k] / jnp.maximum(0.5 * links + PENALTY * masks[1, k], 0.1)
            pairs = [s + other for other in beside_s]

            def image(v):
                terms = [pair * (v - other) for pair, other in zip(pairs, around(v))]
                return 0.5 * ((terms[0] + terms[1]) + (terms[2] + terms[3]) + (terms[4] + terms[5]))

            z = masks[0, k] * inverse
            q = image(z)
            w = q * inverse
            strip_out[g, 0, k] = z
            strip_out[g, 1, k] = w
            terms = (z, z * q, q * w, w * image(w))
            sums = [a + jnp.sum(b * counts[k], axis=0, keepdims=True) for a, b in zip(sums, terms)]
        for place in (0, 1):
            factor_out[g, place] = patched[place]
        for k, part in enumerate(sums):
            line = jnp.where(lane_row == 4 * g + k, jnp.sum(part, axis=1, keepdims=True), line)
    table[...] = jnp.broadcast_to(line, table.shape)


def finish(groups, size, table, z_near, z_own, w_near, w_own, strips, factors, out):
    width, thick = out.shape[1:]
    at = Spot(groups, size, width, thick)
    core = lax.rem(at.spot, 2)
    line = jnp.sum(table[...], axis=0, keepdims=True)
    lane_row = lanes_of((1, thick))
    total = [jnp.zeros(at.shape, jnp.float32), jnp.zeros(at.shape, jnp.float32)]
    for g in range(groups):
        m0, m1, m2, m3 = (
            jnp.sum(jnp.where(lane_row == 4 * g + k, line, 0.0), axis=1, keepdims=True) for k in range(4)
        )
        step_one = m0 / m1
        rz_next = step_one * step_one * m2 - m0
        factor = rz_next / m0
        curve = (m1 - 2.0 * step_one * m2 + step_one * step_one * m3) - factor * factor * m1
        step_two = rz_next / curve
        of_z = step_one + step_two * (1.0 + factor)
        of_w = -step_one * step_two
        z = [z_near[g], z_own[g, 0], z_own[g, 1], z_own[g, 2]]
        w = [w_near[g, 0], w_near[g, 1], w_own[g, 0], w_own[g, 1]]
        u = [of_z * v + of_w * t for v, t in zip(z, w)]
        ends = {1: [0.0, 0.0], 2: [0.0, 0.0]}
        for k, (is_right, present) in enumerate(at.sides()):
            strip = of_z * strips[g, 0, k] + of_w * strips[g, 1, k]
            here = at.held(is_right) & (present > 0.5)
            for place in range(4):
                part = of_strip(strip, place + 3)
                u[place] = jnp.where(here, part, u[place])
                if place in ends:
                    if at.n_strips == 1:
                        ends[place] = [part * at.has_left, part * at.has_right]
                    else:
                        ends[place][k] = part * present
        between = [u[k] - u[k + 1] for k in range(3)]
        for k in (1, 2):
            plane = u[k]
            left = turn(jnp.where(at.at_right, ends[k][0], plane), 1, 1)
            right = turn(jnp.where(at.at_left, ends[k][1], plane), -1, 1)
            up = jnp.where(at.first, 0.0, turn(plane, 1, 0))
            down = jnp.where(at.last, 0.0, turn(plane, -1, 0))
            steps = [between[k - 1], between[k]] + [plane - other for other in (left, right, up, down)]
            squares = [v * v for v in steps]
            total[k - 1] = total[k - 1] + factors[g, k - 1] * sum(squares[1:], squares[0])
    for k in range(2):
        out[lax.rem(k + core, 2)] = total[k]


def call(body, outs, *args, scalars=(), scratch=(), flops=0):
    smem = pl.BlockSpec(memory_space=pltpu.SMEM)
    return pl.pallas_call(
        body,
        out_shape=[jax.ShapeDtypeStruct(shape, jnp.float32) for shape in outs],
        in_specs=[pl.BlockSpec(memory_space=pltpu.VMEM)] * len(args) + [smem] * len(scalars),
        out_specs=[pl.BlockSpec(memory_space=pltpu.VMEM)] * len(outs),
        scratch_shapes=[pltpu.VMEM(shape, jnp.float32) for shape in scratch],
        cost_estimate=pl.CostEstimate(flops=flops, transcendentals=0, bytes_accessed=0) if flops else None,
        compiler_params=pltpu.CompilerParams(vmem_limit_bytes=32 * 1024 * 1024),
    )(*args, *scalars)


def local(design, solid_mask, void_mask, load_mask, support_mask, thresholds, group_weight):
    depth, width, thick = design.shape
    size, groups = lax.axis_size("space"), lax.axis_size("proj")
    quarter = width // 4
    pair, near_pairs = pair_swap(size), near_swap(size)
    fixed = jnp.where(solid_mask == 1, 1.0, jnp.where(void_mask == 1, 0.0, design))
    (packed_own,) = call(
        functools.partial(prepare, groups), [(6 * width + quarter, thick)], fixed, load_mask, support_mask
    )
    partner = lax.ppermute(packed_own, "space", pair)
    own, own_masks, scalars = call(
        join, [(4 * width, thick), (4 * width + quarter, thick), (8, thick)], packed_own, partner,
        scalars=(thresholds, group_weight),
    )
    others = [lax.ppermute(scalars, "proj", [((g + k) % groups, g) for g in range(groups)]) for k in range(1, groups)]
    near = lax.ppermute(own, "space", near_pairs)
    near_masks = lax.ppermute(own_masks, "space", near_pairs)
    others = [call(keep, [other.shape], other, flops=1_650_000_000)[0] for other in others]
    steps = (1,) if groups == 2 else (1, -1)
    packed = call(
        functools.partial(pack, groups),
        [(width // 2, thick)] * len(steps) + [(width // 8, thick)] * len(steps),
        own, near,
    )
    straight = [(i, i) for i in range(size)]
    both = ("proj", "space")
    beside = [lax.ppermute(v, both, both_axes(straight, size, groups, k)) for k, v in zip(steps, packed)]
    crossed = [lax.ppermute(v, both, both_axes(pair, size, groups, k)) for k, v in zip(steps, packed[len(steps) :])]
    (beyond,) = call(pick, [(2 * width, thick)], near, packed[0])
    inner = lax.ppermute(beyond, "space", pair)
    n_strips = 1 if groups == 2 else 2
    plane = (width, thick)
    six = (groups, 6, *plane)
    stiff, links, factors, wide, inside = call(
        functools.partial(density_kernel, groups, size),
        [six, six, (groups, 2, *plane), (n_strips, *plane), plane],
        own, near, inner, scalars, *others,
        flops=1,
        scratch=[(PLACES, width + 16, thick), (6, width + 16, thick)],
    )
    one, two, four = (groups, *plane), (groups, 2, *plane), (groups, 4, *plane)
    strips_shape = (2, n_strips, *plane)
    sums = (-(-4 * groups // 8) * 8, thick)
    z_own, w_own, q_own, over_own, totals, mask_strips = call(
        functools.partial(own_kernel, groups, size),
        [four, two, one, one, sums, strips_shape],
        stiff, links, own_masks, partner,
        flops=1,
        scratch=[(3, width + 16, thick), (3, width + 16, thick), (1, width + 16, thick)],
    )
    totals, z_near, w_near, mask_strips = call(
        functools.partial(near_kernel, groups, size),
        [sums, one, two, strips_shape],
        stiff, links, near_masks, z_own, w_own, q_own, over_own, totals, mask_strips,
        flops=1,
        scratch=[(2, width + 16, thick), (1, width + 16, thick), (1, width + 16, thick)],
    )
    table, strips, factors = call(
        functools.partial(edge_kernel, groups, size),
        [(size * groups, thick), (groups, 2, n_strips, *plane), (groups, 2, *plane)],
        inside, wide, mask_strips, totals, factors, scalars, *beside, *crossed, *others,
    )
    table = lax.all_to_all(table, ("proj", "space"), 0, 0, tiled=True)
    (out,) = call(functools.partial(finish, groups, size), [(depth, *plane)], table, z_near, z_own, w_near, w_own, strips, factors)
    return out


def solution(mesh):
    placed = (
        P("space", None, "proj"),
        P("space", None, "proj"),
        P("space", None, "proj"),
        P("space", None, None),
        P("space", None, None),
        P("proj"),
        P("proj"),
    )
    return jax.shard_map(
        local, mesh=mesh, in_specs=placed, out_specs=P("space", None, "proj"), check_vma=False
    )
```
